128 devices in a mesh: cube: 32 (over z, y, core), band: 4 (over x).
Axes of the slice: x: 4, y: 4, z: 4, core: 2. Of those that a mesh axis runs over, the one named last changes fastest.
Arguments:
- vis: bfloat16 [32, 864, 512], P('cube', 'band'), may hold values from -6 to 6
- keep_slots: int32 [32, 864], P('cube', 'band'), may hold values from 0 to 1727, as said below
- counts: int32 [32, 4], P('cube', 'band'), may hold values from 108 to 216, as said below
- band_mask: int32 [32, 4], P('cube'), may hold values from 0 to 1, as said below
- mask_token: float32 [512], replicated, may hold values from -6 to 6
- pos: bfloat16 [1728, 512], P('band'), may hold values from -3 to 3
- ln1_gain: float32 [512], replicated, may hold values from 0.5 to 1.5
- ln1_bias: float32 [512], replicated, may hold values from -1.8 to 1.8
- w_qkv: bfloat16 [512, 1536], replicated, may hold values from -0.25 to 0.25
- b_query: float32 [512], replicated, may hold values from -3 to 3
- b_value: float32 [512], replicated, may hold values from -3 to 3
- w_out: bfloat16 [512, 512], replicated, may hold values from -2 to 2
- b_out: float32 [512], replicated, may hold values from -1.8 to 1.8
- ln2_gain: float32 [512], replicated, may hold values from 0.5 to 1.5
- ln2_bias: float32 [512], replicated, may hold values from -1.8 to 1.8
- w_up: bfloat16 [512, 2048], replicated, may hold values from -0.25 to 0.25
- b_up: float32 [2048], replicated, may hold values from -1.8 to 1.8
- w_down: bfloat16 [2048, 512], replicated, may hold values from -0.125 to 0.125
- b_down: float32 [512], replicated, may hold values from -1.8 to 1.8
- d_out: bfloat16 [32, 1728, 512], P('cube', 'band'), may hold values from -6 to 6
Outputs:
- out: bfloat16 [32, 1728, 512], P('cube', 'band')
- grad_vis: bfloat16 [32, 864, 512], P('cube', 'band')
- grad_mask_token: float32 [512], replicated
- grad_pos: float32 [1728, 512], P('band')
- grad_ln1_gain: float32 [512], replicated
- grad_ln1_bias: float32 [512], replicated
- grad_w_qkv: float32 [512, 1536], replicated
- grad_b_query: float32 [512], replicated
- grad_b_value: float32 [512], replicated
- grad_w_out: float32 [512, 512], replicated
- grad_b_out: float32 [512], replicated
- grad_ln2_gain: float32 [512], replicated
- grad_ln2_bias: float32 [512], replicated
- grad_w_up: float32 [512, 2048], replicated
- grad_b_up: float32 [2048], replicated
- grad_w_down: float32 [2048, 512], replicated
- grad_b_down: float32 [512], replicated
The draws below stay inside these ranges and needn't reach their ends.
Inputs may be any that keep to these rules, and one draw needn't show every extreme that they name: `keep_slots`: within a cube the entries are distinct slots; of the rows of one piece, at most 72 name slots of one band group, and some piece with all its rows counted has 72 for some group. `counts`: the value 216 is taken in every draw. `band_mask`: each cube has all groups, or all but one.
All inputs are finite; a program needn't handle non-finite values.
Results may differ from the reference program's by a relative error of at most 0.018.
Values may be sent and summed in bfloat16 or wider, within the bound.
No kernel may reach another device: no remote copies, remote signals or barrier semaphores. Data moves between devices by JAX's collectives and lax.ppermute only.
A program may use at most 128 MiB of HBM per device.

```python
import jax
import jax.numpy as jnp
from jax import lax

D = 512
HEADS = 16
HEAD_DIM = 32
FF = 2048
GROUPS = 4
SPAT = 432
PIECE = 216
CAP = 72
SLOTS = 1728
CUBES = 32


def choose_special(key):
    picks = jax.random.randint(key, (2,), 0, 1 << 20)
    return (picks[0] % CUBES, picks[1] % GROUPS)


def lax_iota(rows, columns, dimension):
    return jax.lax.broadcasted_iota(jnp.int32, (rows, columns), dimension)


def draw_keep_slots(key, part):
    key = jax.random.fold_in(key, 11)
    cube_keys = jax.random.split(key, CUBES)
    spare = (PIECE - 2 * CAP) // 2
    row_ids = jnp.arange(PIECE, dtype=jnp.int32)
    base = jnp.where(row_ids < CAP, 0, jnp.where(row_ids < 2 * CAP, 1, jnp.where(row_ids < 2 * CAP + spare, 2, 3))).astype(jnp.int32)
    group_range = jnp.arange(GROUPS, dtype=jnp.int32)

    def one_cube(cube_key):
        turn_key, shuffle_key, slot_key = jax.random.split(cube_key, 3)
        turns = jax.random.randint(turn_key, (GROUPS, 1), 0, GROUPS)
        labels = (base[None, :] + turns) % GROUPS
        labels = jax.vmap(lambda k, l: jax.random.permutation(k, l))(jax.random.split(shuffle_key, GROUPS), labels)
        flat = labels.reshape(GROUPS * PIECE).astype(jnp.int32)
        hot = (flat[:, None] == group_range[None, :]).astype(jnp.int32)
        ranking = jnp.sum((jnp.cumsum(hot, axis=0) - 1) * hot, axis=1).astype(jnp.int32)
        orders = jax.vmap(lambda k: jax.random.permutation(k, SPAT))(jax.random.split(slot_key, GROUPS)).astype(jnp.int32)
        return (flat * SPAT + orders[flat, ranking]).astype(jnp.int32)
    return jax.vmap(one_cube)(cube_keys)


def draw_counts(key, part):
    cube_star, piece_star = choose_special(key)
    key = jax.random.fold_in(key, 12)
    drawn = jax.random.randint(key, (CUBES, GROUPS), PIECE // 2, PIECE + 1)
    cube_ids = lax_iota(CUBES, GROUPS, 0)
    group_ids = lax_iota(CUBES, GROUPS, 1)
    return jnp.where((cube_ids == cube_star) & (group_ids == piece_star), PIECE, drawn).astype(jnp.int32)


def draw_band_mask(key, part):
    key = jax.random.fold_in(key, 13)
    first_key, second_key = jax.random.split(key)
    sensor_short = jax.random.randint(first_key, (CUBES, 1), 0, 2)
    blank = jax.random.randint(second_key, (CUBES, 1), 0, GROUPS)
    group_ids = lax_iota(CUBES, GROUPS, 1)
    return jnp.where((sensor_short == 1) & (group_ids == blank), 0, 1).astype(jnp.int32)


def block_levels(stream_key, extent, shards, least, largest):
    level = 1.0
    for position, shards_of in shards:
        draws = jax.random.uniform(jax.random.fold_in(jax.random.fold_in(stream_key, 6), position), (shards_of,), jnp.float32, least / len(shards), largest / len(shards))
        level = level * jnp.repeat(jnp.exp(draws), extent[position] // shards_of).reshape((-1,) + (1,) * (len(extent) - 1 - position))
    return level


def centred(key, dims, spread, bound, cuts=(), kind=jnp.bfloat16):
    loudness = block_levels(key, dims, cuts, -0.22, 0.18) if cuts else 1.0
    values = jax.random.normal(key, dims, jnp.float32) * spread * loudness
    return jnp.minimum(jnp.maximum(values, -bound), bound).astype(kind)


def setup_inputs(seed: int = 0) -> dict:
    key_of = jax.random.split(jax.random.key(seed), 21)
    vis = centred(key_of[0], (CUBES, GROUPS * PIECE, D), 1.0, 6.0, ((0, 32), (1, 4)))
    keep_slots = draw_keep_slots(jax.random.fold_in(key_of[20], 71), 0)
    counts = draw_counts(jax.random.fold_in(key_of[20], 71), 0)
    band_mask = draw_band_mask(jax.random.fold_in(key_of[20], 71), 0)
    mask_token = centred(key_of[4], (D,), 1.0, 6.0, (), jnp.float32)
    pos = centred(key_of[5], (SLOTS, D), 0.5, 3.0, ((0, 4),))
    ln1_gain = jnp.clip(1.0 + 0.1 * jax.random.normal(key_of[6], (D,), jnp.float32), 0.5, 1.5)
    ln1_bias = centred(key_of[7], (D,), 0.3, 1.8, (), jnp.float32)
    w_qkv = centred(key_of[8], (D, 3 * D), D ** -0.5, 0.25)
    b_query = centred(key_of[9], (D,), 0.5, 3.0, (), jnp.float32)
    b_value = centred(key_of[10], (D,), 0.5, 3.0, (), jnp.float32)
    w_out = centred(key_of[11], (D, D), (D // 64) ** -0.5, 2.0)
    b_out = centred(key_of[12], (D,), 0.3, 1.8, (), jnp.float32)
    ln2_gain = jnp.clip(1.0 + 0.1 * jax.random.normal(key_of[13], (D,), jnp.float32), 0.5, 1.5)
    ln2_bias = centred(key_of[14], (D,), 0.3, 1.8, (), jnp.float32)
    w_up = centred(key_of[15], (D, FF), D ** -0.5, 0.25)
    b_up = centred(key_of[16], (FF,), 0.3, 1.8, (), jnp.float32)
    w_down = centred(key_of[17], (FF, D), FF ** -0.5, 0.125)
    b_down = centred(key_of[18], (D,), 0.3, 1.8, (), jnp.float32)
    d_out = centred(key_of[19], (CUBES, SLOTS, D), 1.0, 6.0, ((0, 32), (1, 4)))
    return dict(vis=vis, keep_slots=keep_slots, counts=counts, band_mask=band_mask, mask_token=mask_token, pos=pos, ln1_gain=ln1_gain, ln1_bias=ln1_bias, w_qkv=w_qkv, b_query=b_query, b_value=b_value, w_out=w_out, b_out=b_out, ln2_gain=ln2_gain, ln2_bias=ln2_bias, w_up=w_up, b_up=b_up, w_down=w_down, b_down=b_down, d_out=d_out)


@jax.custom_vjp
def low(v):
    return lax.optimization_barrier(v.astype(jnp.bfloat16)).astype(jnp.float32)

@jax.custom_vjp
def low_back(v):
    return v

def low_keep(v):
    return (low(v), None)

def low_pass(kept, grad):
    return (grad,)

def back_keep(v):
    return (v, None)

def back_low(kept, grad):
    return (low(grad),)
low.defvjp(low_keep, low_pass)
low_back.defvjp(back_keep, back_low)
highest = lax.Precision.HIGHEST
epsilon = 1e-05
neg_large = -1e+30

def normalize(values, gain, offset):
    average = lax.optimization_barrier(jnp.mean(values, axis=-1, keepdims=True))
    centered = values - average
    variance = lax.optimization_barrier(jnp.mean(centered * centered, axis=-1, keepdims=True))
    return centered * lax.rsqrt(variance + epsilon) * gain + offset

def attend_group(items):
    queries, keys, values, live = items
    scale = HEAD_DIM ** (-0.5)
    scores = low_back(jnp.einsum('hqd,hkd->hqk', queries, keys, precision=highest) * scale)
    scores = jnp.where(live[None, None, :], scores, neg_large)
    peak = lax.optimization_barrier(jnp.max(scores, axis=-1, keepdims=True))
    weights = jnp.exp(scores - peak)
    attention = weights / lax.optimization_barrier(jnp.sum(weights, axis=-1, keepdims=True))
    return jnp.einsum('hqk,hkd->hqd', low(attention), values, precision=highest)

def to_heads(tensor):
    return tensor.reshape(SLOTS, HEADS // 4, 4, HEAD_DIM).transpose(1, 2, 0, 3)

def cube_layer(params, vis_cube, ids_cube, mask_cube):
    mask_token, pos, ln1_gain, ln1_bias, w_qkv, b_query, b_value, w_out, b_out, ln2_gain, ln2_bias, w_up, b_up, w_down, b_down = params
    slot_range = jnp.arange(SLOTS, dtype=jnp.int32)
    one_hot = (ids_cube[None, :] == slot_range[:, None]).astype(jnp.float32)
    placed = jnp.dot(one_hot, low_back(vis_cube), precision=highest)
    visible = lax.optimization_barrier(jnp.sum(one_hot, axis=1, keepdims=True))
    start = placed + (1.0 - visible) * mask_token + pos
    normed_first = low(normalize(start, ln1_gain, ln1_bias))
    projected = jnp.dot(normed_first, w_qkv, precision=highest)
    queries = low(low_back(projected[:, :D] + b_query))
    keys = low(low_back(projected[:, D:2 * D]))
    values = low(low_back(projected[:, 2 * D:] + b_value))
    live = jnp.repeat(mask_cube > 0, SPAT)
    live_items = jnp.broadcast_to(live, (HEADS // 4, SLOTS))
    head_out = lax.map(jax.checkpoint(attend_group), (to_heads(queries), to_heads(keys), to_heads(values), live_items))
    mixed = head_out.transpose(2, 0, 1, 3).reshape(SLOTS, D)
    mixed = low(low_back(mixed))
    branch = low_back(jnp.dot(mixed, w_out, precision=highest) + b_out)
    middle = start + branch
    normed_second = low(normalize(middle, ln2_gain, ln2_bias))
    up_value = low_back(jnp.dot(normed_second, w_up, precision=highest) + b_up)
    activated = low(jax.nn.gelu(up_value, approximate=True))
    return middle + (jnp.dot(activated, w_down, precision=highest) + b_down)

def reference(vis, keep_slots, counts, band_mask, mask_token, pos, ln1_gain, ln1_bias, w_qkv, b_query, b_value, w_out, b_out, ln2_gain, ln2_bias, w_up, b_up, w_down, b_down, d_out):
    positions = lax.broadcasted_iota(jnp.int32, keep_slots.shape, 1) % PIECE
    limits = jnp.repeat(counts, PIECE, axis=1)
    slot_ids = jnp.where(positions < limits, keep_slots, -1).astype(jnp.int32)
    params = tuple((tensor.astype(jnp.float32) for tensor in (mask_token, pos, ln1_gain, ln1_bias, w_qkv, b_query, b_value, w_out, b_out, ln2_gain, ln2_bias, w_up, b_up, w_down, b_down)))

    def forward(params, vis_float):

        def step_cube(carry, items):
            vis_cube, ids_cube, mask_cube = items
            return (carry, cube_layer(params, vis_cube, ids_cube, mask_cube))
        _, result = lax.scan(jax.checkpoint(step_cube), jnp.zeros((), jnp.float32), (vis_float, slot_ids, band_mask))
        return result
    result, pullback = jax.vjp(forward, params, vis.astype(jnp.float32))
    grad_params, grad_vis = pullback(d_out.astype(jnp.float32))
    return (result.astype(jnp.bfloat16), grad_vis.astype(jnp.bfloat16), grad_params[0], grad_params[1], grad_params[2], grad_params[3], grad_params[4], grad_params[5], grad_params[6], grad_params[7], grad_params[8], grad_params[9], grad_params[10], grad_params[11], grad_params[12], grad_params[13], grad_params[14])
```

```python
import functools

import jax
import jax.numpy as jnp
from jax import lax
from jax.experimental import pallas as pl
from jax.experimental.pallas import tpu as pltpu
from jax.sharding import Mesh, PartitionSpec as P

bf = jnp.bfloat16
f32 = jnp.float32

HEADS = 16
DEPTH = 32
QUAD = 4
GROUPS = 4
LOG2E = 1.4426950408889634
SCALE = DEPTH**-0.5
EPS = 1e-05
BIG = 1e30
PAD = 8

NT = (((1,), (1,)), ((), ()))
NN = (((1,), (0,)), ((), ()))
TN = (((0,), (0,)), ((), ()))
VMEM_LIMIT = 56 * 1024 * 1024


def dg(a, b, dims):
    return lax.dot_general(a, b, dims, preferred_element_type=f32)


def params():
    return pltpu.CompilerParams(vmem_limit_bytes=VMEM_LIMIT)


def cost(flops, nbytes, trans=0):
    return pl.CostEstimate(flops=int(flops), bytes_accessed=int(nbytes), transcendentals=int(trans))


def sds(shape, dtype):
    return jax.ShapeDtypeStruct(shape, dtype)


def prep_kernel(base_ref, v0, v1, v2, v3, ids_ref, pos_ref, mt_ref, gain_ref, bias_ref, w_ref, badd_ref, *outs, own):
    base = base_ref[pl.program_id(0)]
    rows = pos_ref.shape[-2]
    piece = v0.shape[0]
    slot = lax.broadcasted_iota(jnp.int32, (rows, piece), 0) + base
    placed = jnp.zeros((rows, pos_ref.shape[-1]), f32)
    seen = jnp.zeros((rows, 1), f32)
    for i, v in enumerate((v0, v1, v2, v3)):
        hot = (slot == ids_ref[i]).astype(f32)
        seen += jnp.sum(hot, axis=1, keepdims=True)
        placed += dg(hot.astype(bf), v[...], NN)
    pos = pos_ref[...].reshape(placed.shape).astype(f32)
    start = placed + (1.0 - seen) * mt_ref[...] + pos
    centered = start - jnp.mean(start, axis=-1, keepdims=True)
    variance = jnp.mean(centered * centered, axis=-1, keepdims=True)
    normed = (centered * lax.rsqrt(variance + EPS) * gain_ref[...] + bias_ref[...]).astype(bf)
    width = normed.shape[1]
    proj = dg(normed, w_ref[...], NN) + badd_ref[...]
    if own:
        start_ref, normed_ref, q_ref, k_ref, v_ref = outs
        start_ref[...] = start
        q_ref[...] = (proj[:, :width] * (SCALE * LOG2E)).astype(bf)
        proj = proj[:, width:]
    else:
        normed_ref, k_ref, v_ref = outs
    normed_ref[...] = normed.reshape(normed_ref.shape)
    k_ref[...] = proj[:, :width].astype(bf).reshape(k_ref.shape)
    v_ref[...] = proj[:, width:].astype(bf).reshape(v_ref.shape)


def prep(base, pieces, ids, pos, mt, gain, bias, w, badd, own):
    width = pos.shape[-1]
    rows = pos.shape[-2]
    count = 1 if own else pos.shape[0]
    full = lambda a: pl.BlockSpec(a.shape, lambda g, b: (0,) * a.ndim)
    if own:
        block = pl.BlockSpec((rows, width), lambda g, b: (0, 0))
        shape = (rows, width)
        out_shape = [sds(shape, f32)] + [sds(shape, bf)] * 4
    else:
        block = pl.BlockSpec((1, rows, width), lambda g, b: (g, 0, 0))
        shape = (count, rows, width)
        out_shape = [sds(shape, bf)] * 3
    flops = 2 * count * rows * width * (w.shape[1] + 4 * pieces[0].shape[0])
    return pl.pallas_call(
        functools.partial(prep_kernel, own=own),
        grid_spec=pltpu.PrefetchScalarGridSpec(
            num_scalar_prefetch=1,
            grid=(count,),
            in_specs=[full(p) for p in pieces] + [full(ids), block, full(mt), full(gain), full(bias), full(w), full(badd)],
            out_specs=[block] * len(out_shape),
        ),
        out_shape=out_shape,
        compiler_params=params(),
        cost_estimate=cost(flops, 4 * count * rows * width * 4),
        name="prep_own" if own else "prep_rest",
    )(base, *pieces, ids, pos, mt, gain, bias, w, badd)


def stack_heads(x):
    lane = lax.broadcasted_iota(jnp.int32, x.shape, 1) // DEPTH
    return jnp.concatenate([jnp.where(lane == h, x, jnp.zeros_like(x)) for h in range(QUAD)], axis=0)


def unstack_heads(xt):
    rows = xt.shape[1] // QUAD
    parts = [xt[DEPTH * h : DEPTH * (h + 1), rows * h : rows * (h + 1)] for h in range(QUAD)]
    return jnp.concatenate(parts, axis=0).T


def fwd_step(state, live, k, v, qs):
    m, l, o = state
    s = dg(k, qs, NT)
    top = jnp.where(live, jnp.max(s, axis=0, keepdims=True), -BIG)
    peak = jnp.maximum(m, top)
    p = jnp.exp2(s - jnp.where(live, peak, BIG))
    keep = jnp.exp2(m - peak)
    l = l * keep + jnp.sum(p, axis=0, keepdims=True)
    o = o * keep + dg(v, p.astype(bf), TN)
    return (peak, l, o)


def fwd_own_kernel(live_ref, q_ref, k_ref, v_ref, m_ref, l_ref, o_ref):
    qs = stack_heads(q_ref[...])
    n = qs.shape[0]
    live = live_ref[0] > 0
    s = dg(k_ref[...], qs, NT)
    m = jnp.where(live, jnp.max(s, axis=0, keepdims=True), -BIG)
    p = jnp.exp2(s - jnp.where(live, m, BIG))
    m_ref[0] = m
    l_ref[0] = jnp.sum(p, axis=0, keepdims=True)
    o_ref[0] = dg(v_ref[...], p.astype(bf), TN)


def fwd_rest_kernel(live_ref, q_ref, k_ref, v_ref, m_ref, l_ref, o_ref, mixed_ref, lse_ref):
    qs = stack_heads(q_ref[...])
    state = (m_ref[0], l_ref[0], o_ref[0])
    for g in range(k_ref.shape[0]):
        state = fwd_step(state, live_ref[g + 1] > 0, k_ref[g], v_ref[g], qs)
    m, l, o = state
    mixed_ref[...] = unstack_heads(o / l).astype(bf)
    lse_ref[0] = m + jnp.log2(l)


def attention_forward(live, q, k_own, v_own, k_rest, v_rest):
    rows, width = q.shape
    quads = width // 128
    n = rows * QUAD
    blk = pl.BlockSpec((rows, 128), lambda g, b: (0, g))
    vec = pl.BlockSpec((1, 1, n), lambda g, b: (g, 0, 0))
    acc = pl.BlockSpec((1, 128, n), lambda g, b: (g, 0, 0))
    rest = pl.BlockSpec((k_rest.shape[0], rows, 128), lambda g, b: (0, 0, g))
    work = 2 * rows * n * 256 * 2 * quads
    state = pl.pallas_call(
        fwd_own_kernel,
        grid_spec=pltpu.PrefetchScalarGridSpec(
            num_scalar_prefetch=1, grid=(quads,), in_specs=[blk] * 3, out_specs=[vec, vec, acc]
        ),
        out_shape=[sds((quads, 1, n), f32), sds((quads, 1, n), f32), sds((quads, 128, n), f32)],
        compiler_params=params(),
        cost_estimate=cost(work, 4 << 20, rows * n * quads),
        name="attention_own",
    )(live, q, k_own, v_own)
    return pl.pallas_call(
        fwd_rest_kernel,
        grid_spec=pltpu.PrefetchScalarGridSpec(
            num_scalar_prefetch=1,
            grid=(quads,),
            in_specs=[blk, rest, rest, vec, vec, acc],
            out_specs=[blk, vec],
        ),
        out_shape=[sds((rows, width), bf), sds((quads, 1, n), f32)],
        compiler_params=params(),
        cost_estimate=cost(3 * work, 8 << 20, 3 * rows * n * quads),
        name="attention_rest",
    )(live, q, k_rest, v_rest, *state)


def bwd_kernel(live_ref, q_ref, do_ref, k_ref, v_ref, lse_ref, delta_ref, *refs, index, last):
    *dq_in, dk_ref, dv_ref, dq_ref = refs
    qs = stack_heads(q_ref[...])
    dos = stack_heads(do_ref[...])
    k = k_ref[...].reshape(q_ref.shape)
    v = v_ref[...].reshape(q_ref.shape)
    dead = jnp.where(live_ref[index] > 0, 0.0, BIG)
    p = jnp.exp2(dg(k, qs, NT) - (lse_ref[0] + dead))
    ds = (p * (dg(v, dos, NT) - delta_ref[0])).astype(bf)
    dv_ref[...] = dg(p.astype(bf), dos, NN).astype(bf)
    dk_ref[...] = (dg(ds, qs, NN) * (1.0 / LOG2E)).astype(bf)
    dq = unstack_heads(dg(k, ds, TN))
    if dq_in:
        dq += dq_in[0][...]
    if last:
        dq_ref[...] = (dq * SCALE).astype(bf)
    else:
        dq_ref[...] = dq


def attention_backward(live, index, q, do, k, v, lse, delta, dq):
    rows, width = q.shape
    quads = width // 128
    n = rows * QUAD
    blk = pl.BlockSpec((rows, 128), lambda g, b: (0, g))
    vec = pl.BlockSpec((1, 1, n), lambda g, b: (g, 0, 0))
    if k.ndim == 3:
        kv = pl.BlockSpec((1, rows, 128), lambda g, b: (index - 1, 0, g))
    else:
        kv = blk
    last = index == 0
    extra = [] if dq is None else [dq]
    return pl.pallas_call(
        functools.partial(bwd_kernel, index=index, last=last),
        grid_spec=pltpu.PrefetchScalarGridSpec(
            num_scalar_prefetch=1,
            grid=(quads,),
            in_specs=[blk, blk, kv, kv, vec, vec] + [blk] * len(extra),
            out_specs=[blk] * 3,
        ),
        out_shape=[sds((rows, width), bf)] * 2 + [sds((rows, width), bf if last else f32)],
        compiler_params=params(),
        cost_estimate=cost(2 * rows * n * 256 * 5 * quads, 5 << 20, rows * n * quads),
        name="attention_grad_%d" % index,
    )(live, q, do, k, v, lse, delta, *extra)


def normalize(values, gain, offset):
    average = jnp.mean(values, axis=-1, keepdims=True)
    centered = values - average
    variance = jnp.mean(centered * centered, axis=-1, keepdims=True)
    return centered * lax.rsqrt(variance + EPS) * gain + offset


def smooth_gate(values):
    return jax.nn.gelu(values, approximate=True)


def column_sum(tensor):
    return jnp.sum(tensor.astype(f32), axis=0)


def shift(array, axis, step):
    size = lax.axis_size(axis)
    return lax.ppermute(array, axis, [(i, (i + step) % size) for i in range(size)])


def peers(array, axis):
    return [shift(array, axis, step) for step in (1, 3, 2)]


def swap(array):
    return shift(array, "core", 1)


def total(parts):
    return functools.reduce(jnp.add, [p.astype(f32) for p in parts])


RING = ("z", "y", "x")


def ring_scatter(array):
    chunks = 64
    rows = array.shape[0] // chunks
    got = lax.all_to_all(array.reshape(chunks, rows, array.shape[1]), RING, 0, 0, tiled=True)
    return jnp.sum(got.astype(f32), axis=0).astype(bf)


def ring_gather(chunk):
    spread = jnp.broadcast_to(chunk[None], (64,) + chunk.shape)
    got = lax.all_to_all(spread, RING, 0, 0, tiled=True)
    return got.reshape(64 * chunk.shape[0], chunk.shape[1])


def body(
    vis,
    keep_slots,
    counts,
    band_mask,
    mask_token,
    pos,
    ln1_gain,
    ln1_bias,
    w_qkv,
    b_query,
    b_value,
    w_out,
    b_out,
    ln2_gain,
    ln2_bias,
    w_up,
    b_up,
    w_down,
    b_down,
    d_out,
):
    x = lax.axis_index("x")
    core = lax.axis_index("core")
    first_core = core == 0
    piece = keep_slots.shape[1]
    rows, width = pos.shape
    half = rows // 2
    hidden = w_up.shape[1]
    d_out = d_out[0]

    index = lax.broadcasted_iota(jnp.int32, (1, piece), 1)
    code = jnp.where(index < counts, keep_slots, -1) + 1
    marks = jnp.concatenate([code // 64, code % 64], axis=0).astype(bf)
    marks = jnp.pad(marks, ((0, PAD - 2), (0, width - piece)))
    message = jnp.concatenate([vis[0], marks], axis=0)
    pieces = [message] + peers(message, "x")

    pos_half = lax.dynamic_slice(pos, (half * core, 0), (half, width))
    mine = jnp.stack(peers(pos_half, "x"))
    other = swap(mine)
    pos_rest = jnp.where(
        first_core, jnp.concatenate([mine, other], axis=1), jnp.concatenate([other, mine], axis=1)
    )

    def decode(msg):
        ids = msg[piece].astype(jnp.int32) * 64 + msg[piece + 1].astype(jnp.int32) - 1
        return ids[: piece + PAD]

    lanes = lax.broadcasted_iota(jnp.int32, (1, piece + PAD), 1)
    ids = jnp.stack([jnp.where(lanes < piece, decode(m)[None], -1) for m in pieces])

    order = (x + jnp.array([0, 3, 1, 2], jnp.int32)) % GROUPS
    base = order * rows
    live = jnp.take(band_mask[0], order)

    row = lambda a: a.reshape(1, -1)
    badd = jnp.concatenate([b_query, jnp.zeros_like(b_query), b_value])
    start, normed_own, q, k_own, v_own = prep(
        base[:1], pieces, ids, pos, row(mask_token), row(ln1_gain), row(ln1_bias), w_qkv, row(badd), True
    )
    normed_rest, k_rest, v_rest = prep(
        base[1:],
        pieces,
        ids,
        pos_rest,
        row(mask_token),
        row(ln1_gain),
        row(ln1_bias),
        w_qkv[:, width:],
        row(badd[width:]),
        False,
    )
    mixed, lse = attention_forward(live, q, k_own, v_own, k_rest, v_rest)

    branch = dg(mixed, w_out, NN) + b_out
    middle = start + branch
    normed_second = normalize(middle, ln2_gain, ln2_bias).astype(bf)
    up_value = dg(normed_second, w_up, NN) + b_up
    activated = smooth_gate(up_value).astype(bf)
    out = (middle + (dg(activated, w_down, NN) + b_down)).astype(bf)
    grad_result = d_out.astype(f32)
    grad_activated = dg(d_out, w_down, NT)
    _, gate_pull = jax.vjp(smooth_gate, up_value)
    grad_up = gate_pull(grad_activated)[0].astype(bf)
    grad_w_down = dg(activated, d_out, TN).astype(bf)
    blocks = hidden // width
    grad_w_up = jnp.concatenate(
        [dg(normed_second, grad_up[:, width * i : width * (i + 1)], TN).astype(bf) for i in range(blocks)], axis=0
    )
    grad_second = dg(grad_up, w_up, NT)
    _, second_pull = jax.vjp(normalize, middle, ln2_gain, ln2_bias)
    grad_middle_part, grad_ln2_gain, grad_ln2_bias = second_pull(grad_second)
    grad_middle = grad_result + grad_middle_part
    grad_branch = grad_middle.astype(bf)
    grad_mixed = dg(grad_branch, w_out, NT).astype(bf)
    grad_w_out = dg(mixed, grad_branch, TN).astype(bf)

    ff_kept = jnp.where(first_core, grad_w_down, grad_w_up)
    ff_sent = jnp.where(first_core, grad_w_up, grad_w_down)
    ff_half = (ff_kept.astype(f32) + swap(ff_sent).astype(f32)).astype(bf)
    ff_chunk = ring_scatter(ff_half)

    head_of = lax.broadcasted_iota(jnp.int32, (HEADS, width), 1) // DEPTH
    pick = (head_of == lax.broadcasted_iota(jnp.int32, (HEADS, width), 0)).astype(f32)
    delta = lax.dot_general(
        pick, mixed.astype(f32) * grad_mixed.astype(f32), NT, precision=lax.Precision.HIGHEST
    ).reshape(HEADS // QUAD, 1, QUAD * rows)
    w_k, w_v = w_qkv[:, width : 2 * width], w_qkv[:, 2 * width :]
    dq = None
    first_parts = []
    grad_w_k = jnp.zeros((width, width), f32)
    grad_w_v = jnp.zeros((width, width), f32)
    grad_b_value = jnp.zeros((width,), f32)
    for group, step in ((3, 2), (1, 3), (2, 1)):
        dk, dv, dq = attention_backward(live, group, q, grad_mixed, k_rest, v_rest, lse, delta, dq)
        part = (dg(dk, w_k, NT) + dg(dv, w_v, NT)).astype(bf)
        first_parts.append(shift(part, "x", step))
        grad_w_k += dg(normed_rest[group - 1], dk, TN)
        grad_w_v += dg(normed_rest[group - 1], dv, TN)
        grad_b_value += column_sum(dv)
    dk, dv, dq = attention_backward(live, 0, q, grad_mixed, k_own, v_own, lse, delta, dq)
    grad_w_k += dg(normed_own, dk, TN)
    grad_w_v += dg(normed_own, dv, TN)
    grad_b_value += column_sum(dv)
    grad_w_q = dg(normed_own, dq, TN)
    grad_b_query = column_sum(dq)

    low = jnp.concatenate([grad_w_k, grad_w_v], axis=0).astype(bf)
    high = jnp.concatenate([grad_w_q.astype(bf), grad_w_out], axis=0)
    at_kept = jnp.where(first_core, low, high)
    at_sent = jnp.where(first_core, high, low)
    at_half = (at_kept.astype(f32) + swap(at_sent).astype(f32)).astype(bf)
    at_chunk = ring_scatter(at_half)

    grad_first = dg(dq, w_qkv[:, :width], NT) + dg(dk, w_k, NT) + dg(dv, w_v, NT) + total(first_parts)
    _, first_pull = jax.vjp(normalize, start, ln1_gain, ln1_bias)
    grad_start_part, grad_ln1_gain, grad_ln1_bias = first_pull(grad_first)
    grad_start = grad_middle + grad_start_part

    slots = lax.broadcasted_iota(jnp.int32, (1, rows), 1) + base[0]
    grad_low = grad_start.astype(bf)
    shares = []
    for i in range(GROUPS):
        hot = (ids[i, 0, :piece][:, None] == slots).astype(bf)
        shares.append(dg(hot, grad_low, NN).astype(bf))
    returned = [shares[0], shift(shares[1], "x", 3), shift(shares[2], "x", 1), shift(shares[3], "x", 2)]
    grad_vis = total(returned).astype(bf)

    own_slots = lax.broadcasted_iota(jnp.int32, (rows, 1), 0) + base[0]
    seen = jnp.any(own_slots[:, :, None] == ids.reshape(1, 1, -1), axis=2)
    grad_mask_token = jnp.sum(jnp.where(seen, 0.0, grad_start), axis=0)

    vectors = jnp.stack(
        [
            grad_mask_token,
            grad_ln1_gain,
            grad_ln1_bias,
            grad_b_query,
            grad_b_value,
            column_sum(grad_branch),
            grad_ln2_gain,
            grad_ln2_bias,
            column_sum(grad_result),
        ]
    )
    vectors = jnp.concatenate([vectors, column_sum(grad_up).reshape(blocks, width)], axis=0)
    count = vectors.shape[0]
    vectors = jnp.pad(vectors, ((0, 16 - count), (0, 0))).astype(bf)
    vectors = total([vectors] + peers(vectors, "x")).astype(bf)
    upper, lower = grad_start[:half], grad_start[half:]
    pos_kept = jnp.where(first_core, upper, lower)
    pos_sent = jnp.where(first_core, lower, upper).astype(bf)
    pos_half_sum = (pos_kept + swap(pos_sent).astype(f32)).astype(bf)
    vectors = (vectors.astype(f32) + swap(vectors).astype(f32)).astype(bf)
    bundle = jnp.concatenate([pos_half_sum, vectors], axis=0)
    bundle = total([bundle] + peers(bundle, "y")).astype(bf)
    bundle = total([bundle] + peers(bundle, "z"))
    vectors = bundle[half:]
    pos_mine = bundle[:half].astype(bf)
    pos_other = swap(pos_mine)
    grad_pos = jnp.where(
        first_core, jnp.concatenate([pos_mine, pos_other]), jnp.concatenate([pos_other, pos_mine])
    ).astype(f32)

    ff_mine = ring_gather(ff_chunk)
    ff_other = swap(ff_mine)
    grad_w_down = jnp.where(first_core, ff_mine, ff_other).astype(f32)
    up_rows = jnp.where(first_core, ff_other, ff_mine).astype(f32)
    grad_w_up = up_rows.reshape(blocks, width, width).transpose(1, 0, 2).reshape(width, hidden)

    at_mine = ring_gather(at_chunk)
    at_other = swap(at_mine)
    low = jnp.where(first_core, at_mine, at_other).astype(f32)
    high = jnp.where(first_core, at_other, at_mine).astype(f32)
    grad_w_qkv = jnp.concatenate([high[:width], low[:width], low[width:]], axis=1)
    grad_w_out = high[width:]

    return (
        out[None],
        grad_vis[None],
        vectors[0],
        grad_pos,
        vectors[1],
        vectors[2],
        grad_w_qkv,
        vectors[3],
        vectors[4],
        grad_w_out,
        vectors[5],
        vectors[6],
        vectors[7],
        grad_w_up,
        vectors[9 : 9 + blocks].reshape(hidden),
        grad_w_down,
        vectors[8],
    )


CUBE = ("z", "y", "core")


def solution(mesh):
    fine = Mesh(mesh.devices.reshape(4, 4, 2, 4), ("z", "y", "core", "x"))
    return jax.shard_map(
        body,
        mesh=fine,
        in_specs=(
            P(CUBE, "x", None),
            P(CUBE, "x"),
            P(CUBE, "x"),
            P(CUBE, None),
            P(),
            P("x", None),
        )
        + (P(),) * 13
        + (P(CUBE, "x", None),),
        out_specs=(P(CUBE, "x", None), P(CUBE, "x", None), P(), P("x", None)) + (P(),) * 13,
        check_vma=False,
    )
```

```python
import functools

import jax
import jax.numpy as jnp
from jax import lax
from jax.experimental import pallas as pl
from jax.experimental.pallas import tpu as pltpu
from jax.sharding import Mesh, PartitionSpec as P

bf = jnp.bfloat16
f32 = jnp.float32

HEADS = 16
DEPTH = 32
QUAD = 4
GROUPS = 4
LOG2E = 1.4426950408889634
SCALE = DEPTH**-0.5
EPS = 1e-05
BIG = 1e30
PAD = 8
GELU_SCALE = 0.7978845608028654
GELU_CUBE = 0.044715
SPREAD = 16

NT = (((1,), (1,)), ((), ()))
NN = (((1,), (0,)), ((), ()))
TN = (((0,), (0,)), ((), ()))
VMEM_LIMIT = 56 * 1024 * 1024


def dg(a, b, dims):
    return lax.dot_general(a, b, dims, preferred_element_type=f32)


def sds(shape, dtype):
    return jax.ShapeDtypeStruct(shape, dtype)


def call(kernel, name, scalar, operands, out_shape, scratch=(), aliases=None, limit=32):
    inside = pl.BlockSpec(memory_space=pltpu.VMEM)
    return pl.pallas_call(
        kernel,
        in_specs=[pl.BlockSpec(memory_space=pltpu.SMEM)] + [inside] * len(operands),
        out_specs=[inside] * len(out_shape),
        out_shape=out_shape,
        scratch_shapes=list(scratch),
        compiler_params=pltpu.CompilerParams(vmem_limit_bytes=limit * 1024 * 1024),
        cost_estimate=pl.CostEstimate(flops=1000, bytes_accessed=1000, transcendentals=0),
        input_output_aliases=aliases or {},
        name=name,
    )(scalar, *operands)


def grid_call(kernel, name, scalar, steps, in_specs, out_specs, out_shape, operands):
    return pl.pallas_call(
        kernel,
        grid_spec=pltpu.PrefetchScalarGridSpec(
            num_scalar_prefetch=1, grid=(steps,), in_specs=in_specs, out_specs=out_specs
        ),
        out_shape=out_shape,
        compiler_params=pltpu.CompilerParams(vmem_limit_bytes=32 * 1024 * 1024),
        cost_estimate=pl.CostEstimate(flops=1000, bytes_accessed=1000, transcendentals=0),
        name=name,
    )(scalar, *operands)


def column_sum(tensor):
    return jnp.sum(tensor.astype(f32), axis=0, keepdims=True)


def norm_parts(values):
    centered = values - jnp.mean(values, axis=-1, keepdims=True)
    variance = jnp.mean(centered * centered, axis=-1, keepdims=True)
    inverse = lax.rsqrt(variance + EPS)
    return centered * inverse, inverse


def norm_pull(grad, n, inverse, gain):
    g = grad * gain
    return inverse * (
        g - jnp.mean(g, axis=-1, keepdims=True) - n * jnp.mean(g * n, axis=-1, keepdims=True)
    )


def prep_kernel(scalar_ref, *refs, own):
    vis_refs, id_refs, refs = refs[:GROUPS], refs[GROUPS : 2 * GROUPS], refs[2 * GROUPS :]
    pos_ref, rows_ref, w_ref, *outs = refs
    rows, width = pos_ref.shape[-2:]
    piece = vis_refs[0].shape[0]
    for g in range(1 if own else pos_ref.shape[0]):
        slot = lax.broadcasted_iota(jnp.int32, (rows, piece), 0) + scalar_ref[GROUPS if own else GROUPS + 1 + g]
        placed = jnp.zeros((rows, width), f32)
        seen = jnp.zeros((rows, 1), f32)
        for v, ids in zip(vis_refs, id_refs):
            hot = (slot == ids[...]).astype(f32)
            seen += jnp.sum(hot, axis=1, keepdims=True)
            placed += dg(hot.astype(bf), v[...], NN)
        pos = (pos_ref[...] if own else pos_ref[g]).astype(f32)
        start = placed + (1.0 - seen) * rows_ref[0:1] + pos
        n, _ = norm_parts(start)
        normed = (n * rows_ref[1:2] + rows_ref[2:3]).astype(bf)
        if own:
            start_ref, turned_ref, q_ref, k_ref, v_ref = outs
            start_ref[...] = start
            turned_ref[...] = normed.T
            q_ref[...] = ((dg(normed, w_ref[:, :width], NN) + rows_ref[3:4]) * (SCALE * LOG2E)).astype(bf)
            k_ref[...] = dg(normed, w_ref[:, width : 2 * width], NN).astype(bf)
            v_ref[...] = (dg(normed, w_ref[:, 2 * width :], NN) + rows_ref[4:5]).astype(bf)
        else:
            turned_ref, k_ref, v_ref = outs
            turned_ref[g] = normed.T
            k_ref[g] = dg(normed, w_ref[:, width : 2 * width], NN).astype(bf)
            v_ref[g] = (dg(normed, w_ref[:, 2 * width :], NN) + rows_ref[4:5]).astype(bf)


def prep(scalar, pieces, ids, pos, vectors, w_qkv, own):
    rows, width = pos.shape[-2:]
    lead = () if own else pos.shape[:1]
    shape, turned = lead + (rows, width), lead + (width, rows)
    out_shape = [sds(turned, bf)] + [sds(shape, bf)] * (3 if own else 2)
    if own:
        out_shape = [sds(shape, f32)] + out_shape
    return call(
        functools.partial(prep_kernel, own=own),
        "prep_own" if own else "prep_rest",
        scalar,
        [*pieces, *ids, pos, vectors, w_qkv],
        out_shape,
        limit=24,
    )


def stack_heads(x):
    lane = lax.broadcasted_iota(jnp.int32, x.shape, 1) // DEPTH
    return jnp.concatenate([jnp.where(lane == h, x, jnp.zeros_like(x)) for h in range(QUAD)], axis=0)


def unstack_heads(xt):
    rows = xt.shape[1] // QUAD
    parts = [xt[DEPTH * h : DEPTH * (h + 1), rows * h : rows * (h + 1)] for h in range(QUAD)]
    return jnp.concatenate(parts, axis=0).T


def fwd_step(state, live, k, v, qs):
    s = dg(k, qs, NT)
    peak = jnp.where(live, jnp.max(s, axis=0, keepdims=True), -BIG)
    if state is not None:
        peak = jnp.maximum(state[0], peak)
    p = jnp.exp2(s - jnp.where(live, peak, BIG))
    l = jnp.sum(p, axis=0, keepdims=True)
    o = dg(v, p.astype(bf), TN)
    if state is not None:
        keep = jnp.exp2(state[0] - peak)
        l += state[1] * keep
        o += state[2] * keep
    return (peak, l, o)


def fwd_own_kernel(live_ref, q_ref, k_ref, v_ref, m_ref, l_ref, o_ref):
    for j in range(m_ref.shape[0]):
        at = slice(128 * j, 128 * (j + 1))
        state = fwd_step(None, live_ref[0] > 0, k_ref[:, at], v_ref[:, at], stack_heads(q_ref[:, at]))
        m_ref[j], l_ref[j], o_ref[j] = state


def fwd_rest_kernel(live_ref, q_ref, k_ref, v_ref, m_ref, l_ref, o_ref, mixed_ref, lse_ref):
    for j in range(m_ref.shape[0]):
        at = slice(128 * j, 128 * (j + 1))
        qs = stack_heads(q_ref[:, at])
        state = (m_ref[j], l_ref[j], o_ref[j])
        for g in range(k_ref.shape[0]):
            state = fwd_step(state, live_ref[g + 1] > 0, k_ref[g, :, at], v_ref[g, :, at], qs)
        m, l, o = state
        mixed_ref[:, at] = unstack_heads(o / l).astype(bf)
        lse_ref[j] = m + jnp.log2(l)


def attention_own(live, q, k, v):
    rows, width = q.shape
    quads, n = width // 128, rows * QUAD
    return call(
        fwd_own_kernel,
        "attention_own",
        live,
        [q, k, v],
        [sds((quads, 1, n), f32), sds((quads, 1, n), f32), sds((quads, 128, n), f32)],
    )


def attention_rest(live, q, k, v, state):
    rows, width = q.shape
    quads, n = width // 128, rows * QUAD
    return call(
        fwd_rest_kernel,
        "attention_rest",
        live,
        [q, k, v, *state],
        [sds((rows, width), bf), sds((quads, 1, n), f32)],
    )


def bwd_kernel(scalar_ref, q_ref, do_ref, k_ref, v_ref, lse_ref, delta_ref, turned_ref, w_ref, *refs, index, carried):
    width = q_ref.shape[1]
    if carried:
        dq_in, g_in, bv_in, *refs = refs
    if index == 0:
        kept_ref, sent_ref, bq_ref, bv_ref, part_ref, d_s, dq_ref = refs
    else:
        dq_ref, g_ref, bv_ref, part_ref, d_s = refs
    dead = jnp.where(scalar_ref[index] > 0, 0.0, BIG)
    for j in range(width // 128):
        at = slice(128 * j, 128 * (j + 1))
        qs = stack_heads(q_ref[:, at])
        dos = stack_heads(do_ref[:, at])
        k = k_ref[index - 1, :, at] if index else k_ref[:, at]
        v = v_ref[index - 1, :, at] if index else v_ref[:, at]
        p = jnp.exp2(dg(k, qs, NT) - (lse_ref[j] + dead))
        ds = (p * (dg(v, dos, NT) - delta_ref[j])).astype(bf)
        d_s[:, 2 * width + 128 * j : 2 * width + 128 * (j + 1)] = dg(p.astype(bf), dos, NN).astype(bf)
        d_s[:, width + 128 * j : width + 128 * (j + 1)] = (dg(ds, qs, NN) * (1.0 / LOG2E)).astype(bf)
        dq = unstack_heads(dg(k, ds, TN))
        if carried:
            dq += dq_in[:, at]
        if index == 0:
            d_s[:, at] = (dq * SCALE).astype(bf)
        else:
            dq_ref[:, at] = dq
    turned = turned_ref[index - 1] if index else turned_ref[...]
    grads = d_s[...] if index == 0 else d_s[:, width:]
    part = dg(grads, w_ref[...] if index == 0 else w_ref[:, width:], NT)
    part_ref[...] = part.astype(part_ref.dtype)
    bv = column_sum(d_s[:, 2 * width :])
    bv_ref[...] = bv + bv_in[...] if carried else bv
    g = dg(turned, grads[:, -2 * width :], NN)
    if carried:
        g += g_in[...]
    if index != 0:
        g_ref[...] = g
        return
    bq_ref[...] = column_sum(d_s[:, :width])
    gq = dg(turned, d_s[:, :width], NN)
    first = scalar_ref[GROUPS + 4] == 0
    half = width // 2
    for j in range(width // 128):
        at = slice(128 * j, 128 * (j + 1))
        block = jnp.concatenate([gq[:, at], g[:, at], g[:, width + 128 * j : width + 128 * (j + 1)]], axis=1)
        place = (j + GROUPS - scalar_ref[GROUPS + 5]) % GROUPS
        kept_ref[place] = jnp.where(first, block[:half], block[half:]).astype(bf)
        sent_ref[place] = jnp.where(first, block[half:], block[:half]).astype(bf)


def attention_grad(scalar, index, q, do, k, v, lse, delta, turned, w_qkv, carried):
    rows, width = q.shape
    operands = [q, do, k, v, lse, delta, turned, w_qkv]
    aliases = {}
    if carried is not None:
        if index:
            aliases = {len(operands) + 1 + i: i for i in range(3)}
        operands += list(carried)
    scratch = [pltpu.VMEM((rows, 3 * width), bf)]
    if index == 0:
        packed = (width // 128, width // 2, 3 * 128)
        out_shape = [sds(packed, bf)] * 2 + [sds((1, width), f32)] * 2 + [sds((rows, width), f32)]
        scratch.append(pltpu.VMEM((8, 128), f32))
    else:
        out_shape = [
            sds((rows, width), f32),
            sds((width, 2 * width), f32),
            sds((1, width), f32),
            sds((rows, width), bf),
        ]
    return call(
        functools.partial(bwd_kernel, index=index, carried=carried is not None),
        "attention_grad_%d" % index,
        scalar,
        operands,
        out_shape,
        scratch,
        aliases,
    )


def feed_kernel(
    scalar_ref,
    mixed_ref,
    start_ref,
    dout_ref,
    wout_ref,
    rows_ref,
    wup_ref,
    bup_ref,
    wdown_ref,
    out_ref,
    gmid_ref,
    gmix_ref,
    delta_ref,
    kept_ref,
    sent_ref,
    gbup_ref,
    vec_ref,
):
    first = scalar_ref[GROUPS + 4] == 0
    width = mixed_ref.shape[1]
    hidden = wup_ref.shape[1]
    mixed = mixed_ref[...]
    dout = dout_ref[...]
    middle = start_ref[...] + (dg(mixed, wout_ref[...], NN) + rows_ref[0:1])
    n, inverse = norm_parts(middle)
    normed = (n * rows_ref[1:2] + rows_ref[2:3]).astype(bf)
    turned = normed.T
    result = middle + rows_ref[3:4]
    second = jnp.zeros_like(middle)
    lines = hidden // SPREAD
    for h in range(hidden // width):
        at = slice(width * h, width * (h + 1))
        u = dg(normed, wup_ref[:, at], NN) + bup_ref[:, at]
        square = u * u
        t = jnp.tanh(u * (GELU_SCALE + (GELU_SCALE * GELU_CUBE) * square))
        near = 0.5 + 0.5 * t
        act = (u * near).astype(bf)
        result += dg(act, wdown_ref[at, :], NN)
        slope = near + u * (0.5 - 0.5 * (t * t)) * (GELU_SCALE + (3.0 * GELU_SCALE * GELU_CUBE) * square)
        gup = (dg(dout, wdown_ref[at, :], NT) * slope).astype(bf)
        second += dg(gup, wup_ref[:, at], NT)
        gbup_ref[:, at] = column_sum(gup)
        down = dg(act, dout, TN).astype(bf)
        up = dg(turned, gup, NN).astype(bf)
        chunks = (width // lines, lines, width)
        places = slice(h * chunks[0], (h + 1) * chunks[0])
        kept_ref[places, :lines, :] = jnp.where(first, down, up).reshape(chunks)
        sent_ref[places, :lines, :] = jnp.where(first, up, down).reshape(chunks)
    out_ref[...] = result.astype(bf)
    grad = dout.astype(f32)
    gmid = grad + norm_pull(second, n, inverse, rows_ref[1:2])
    gmid_ref[...] = gmid
    branch = gmid.astype(bf)
    gmix = dg(branch, wout_ref[...], NT).astype(bf)
    gmix_ref[...] = gmix
    wout = dg(mixed, branch, TN)
    half = width // 2
    extra = (SPREAD, half // SPREAD, width)
    kept_ref[:, lines:, :] = jnp.where(first, wout[:half], wout[half:]).astype(bf).reshape(extra)
    sent_ref[:, lines:, :] = jnp.where(first, wout[half:], wout[:half]).astype(bf).reshape(extra)
    vec_ref[...] = jnp.concatenate(
        [
            column_sum(branch),
            column_sum(second * n),
            column_sum(second),
            column_sum(grad),
            jnp.zeros((4, width), f32),
        ],
        axis=0,
    )
    product = mixed.astype(f32) * gmix.astype(f32)
    head = lax.broadcasted_iota(jnp.int32, (HEADS, width), 0)
    lane = lax.broadcasted_iota(jnp.int32, (HEADS, width), 1) // DEPTH
    pick = (head == lane).astype(bf)
    high = product.astype(bf)
    low = (product - high.astype(f32)).astype(bf)
    delta = dg(pick, high, NT) + dg(pick, low, NT)
    for j in range(HEADS // QUAD):
        delta_ref[j] = jnp.concatenate([delta[QUAD * j + i : QUAD * j + i + 1] for i in range(QUAD)], axis=1)


def feed_forward(scalar, mixed, start, d_out, w_out, vectors, w_up, b_up, w_down):
    rows, width = mixed.shape
    hidden = w_up.shape[1]
    packed = (SPREAD, hidden // SPREAD + width // 2 // SPREAD, width)
    return call(
        feed_kernel,
        "feed_forward",
        scalar,
        [mixed, start, d_out, w_out, vectors, w_up, b_up, w_down],
        [
            sds((rows, width), bf),
            sds((rows, width), f32),
            sds((rows, width), bf),
            sds((HEADS // QUAD, 1, QUAD * rows), f32),
            sds(packed, bf),
            sds(packed, bf),
            sds((1, hidden), f32),
            sds((8, width), f32),
        ],
    )


def finish_kernel(
    scalar_ref, part_ref, r3, r1, r2, start_ref, gmid_ref, rows_ref, bq_ref, bv_ref, feed_ref, bup_ref, *refs
):
    id_refs, (kept_ref, sent_ref), share_refs = refs[:GROUPS], refs[GROUPS : GROUPS + 2], refs[GROUPS + 2 :]
    rows, width = start_ref.shape
    first_grad = part_ref[...] + r3[...].astype(f32) + r1[...].astype(f32) + r2[...].astype(f32)
    n, inverse = norm_parts(start_ref[...])
    grad = gmid_ref[...] + norm_pull(first_grad, n, inverse, rows_ref[1:2])
    half = rows // 2
    first = scalar_ref[GROUPS + 4] == 0
    top, low = grad[:half], grad[half:]
    grad_low = grad.astype(bf)
    piece = id_refs[0].shape[1]
    slot = lax.broadcasted_iota(jnp.int32, (rows, piece), 0) + scalar_ref[GROUPS]
    seen = jnp.zeros((rows, 1), f32)
    for id_ref, share_ref in zip(id_refs, share_refs):
        hot = (slot == id_ref[...]).astype(f32)
        seen += jnp.sum(hot, axis=1, keepdims=True)
        share_ref[...] = dg(hot.astype(bf), grad_low, TN).astype(bf)
    blank = lambda count: jnp.zeros((count, width), f32)
    lines = [
        blank(PAD),
        column_sum((1.0 - seen) * grad),
        column_sum(first_grad * n),
        column_sum(first_grad),
        bq_ref[...],
        bv_ref[...],
        feed_ref[:4],
    ]
    blocks = bup_ref.shape[1] // width
    lines += [bup_ref[:, width * i : width * (i + 1)] for i in range(blocks)]
    spare = kept_ref.shape[0] - half - sum(a.shape[0] for a in lines)
    lines = jnp.concatenate(lines + [blank(spare)], axis=0)
    kept_ref[:half] = jnp.where(first, top, low)
    kept_ref[half:] = lines
    sent_ref[...] = jnp.concatenate([jnp.where(first, low, top), lines], axis=0).astype(bf)


def finish(scalar, part, received, start, gmid, vectors, bq, bv, feed_vec, grad_b_up, ids):
    rows, width = start.shape
    piece = ids[0].shape[1]
    tail = (SPREAD * SPREAD, width)
    return call(
        finish_kernel,
        "finish",
        scalar,
        [part, *received, start, gmid, vectors, bq, bv, feed_vec, grad_b_up, *ids],
        [sds(tail, f32), sds(tail, bf)] + [sds((piece, width), bf)] * GROUPS,
    )


def unpack_feed_kernel(scalar_ref, mine_ref, other_ref, down_ref, up_ref, out_ref):
    first = scalar_ref[GROUPS + 4] == 0
    extra = out_ref.shape[1] // mine_ref.shape[0]
    lines = mine_ref.shape[1] - extra
    for i in range(mine_ref.shape[0]):
        mine, other = mine_ref[i].astype(f32), other_ref[i].astype(f32)
        low = jnp.where(first, mine, other)
        high = jnp.where(first, other, mine)
        at = slice(lines * i, lines * (i + 1))
        down_ref[at, :] = low[:lines]
        up_ref[at, :] = high[:lines]
        at = slice(extra * i, extra * (i + 1))
        out_ref[0, at, :] = low[lines:]
        out_ref[1, at, :] = high[lines:]


def unpack_feed(scalar, mine, other, width, hidden):
    lines = hidden // SPREAD
    extra = mine.shape[1] - lines
    per = width // lines
    block = pl.BlockSpec((per,) + mine.shape[1:], lambda g, s: (g, 0, 0))
    return grid_call(
        unpack_feed_kernel,
        "unpack_feed",
        scalar,
        SPREAD // per,
        [block, block],
        [
            pl.BlockSpec((width, width), lambda g, s: (g, 0)),
            pl.BlockSpec((width, width), lambda g, s: (0, g)),
            pl.BlockSpec((2, extra * per, width), lambda g, s: (0, g, 0)),
        ],
        [sds((hidden, width), f32), sds((width, hidden), f32), sds((2, extra * SPREAD, width), f32)],
        [mine, other],
    )


def unpack_qkv_kernel(scalar_ref, mine_ref, other_ref, out_ref):
    core = scalar_ref[GROUPS + 4]
    place = scalar_ref[GROUPS + 5]
    half = out_ref.shape[0] // 2
    width = out_ref.shape[1] // 3
    for i, far in enumerate((0, 3, 1, 2)):
        block = (place + far) % GROUPS
        for kept, ref in ((core, mine_ref), (1 - core, other_ref)):
            lines = pl.ds(pl.multiple_of(kept * half, half), half)
            for w in range(3):
                lanes = pl.ds(pl.multiple_of(w * width + block * 128, 128), 128)
                out_ref[lines, lanes] = ref[i, :half, 128 * w : 128 * (w + 1)].astype(f32)


def unpack_qkv(scalar, mine, other, width):
    return call(unpack_qkv_kernel, "unpack_qkv", scalar, [mine, other], [sds((width, 3 * width), f32)])[0]


def shift(array, axis, step):
    size = lax.axis_size(axis)
    return lax.ppermute(array, axis, [(i, (i + step) % size) for i in range(size)])


def peers(array, axis):
    return [shift(array, axis, step) for step in (1, 3, 2)]


def swap(array):
    return shift(array, "core", 1)


def total(parts):
    return functools.reduce(jnp.add, [p.astype(f32) for p in parts])


PLANE = ("z", "y")


def exchange(array):
    return lax.all_to_all(array, PLANE, 0, 0, tiled=True)


def body(
    vis,
    keep_slots,
    counts,
    band_mask,
    mask_token,
    pos,
    ln1_gain,
    ln1_bias,
    w_qkv,
    b_query,
    b_value,
    w_out,
    b_out,
    ln2_gain,
    ln2_bias,
    w_up,
    b_up,
    w_down,
    b_down,
    d_out,
):
    barrier = lax.optimization_barrier
    x = lax.axis_index("x")
    core = lax.axis_index("core")
    first_core = core == 0
    piece = keep_slots.shape[1]
    rows, width = pos.shape
    half = rows // 2
    hidden = w_up.shape[1]

    vis = vis[0]
    pieces = [vis] + peers(vis, "x")
    index = lax.broadcasted_iota(jnp.int32, (1, piece), 1)
    slot_ids = jnp.where(index < counts, keep_slots, -1)
    ids = [slot_ids] + peers(slot_ids, "x")
    pos_half = lax.dynamic_slice(pos, (half * core, 0), (half, width))
    pos_peers = peers(pos_half, "x")

    order = (x + jnp.array([0, 3, 1, 2], jnp.int32)) % GROUPS
    live = jnp.sum(jnp.where(order[:, None] == jnp.arange(GROUPS)[None, :], band_mask, 0), axis=1)
    scalar = jnp.concatenate([live, order * rows, core[None], x[None]]).astype(jnp.int32)

    pack = lambda *vs: jnp.pad(jnp.stack(vs), ((0, 8 - len(vs)), (0, 0)))
    vectors = pack(mask_token, ln1_gain, ln1_bias, b_query, b_value)
    start, turned_own, q, k_own, v_own = prep(scalar, pieces, ids, pos, vectors, w_qkv, True)
    k_own, pos_peers = barrier((k_own, pos_peers))
    mine = jnp.stack(pos_peers)
    other = swap(mine)
    state = attention_own(scalar, q, k_own, v_own)
    state, other = barrier((state, other))
    pos_rest = jnp.where(
        first_core, jnp.concatenate([mine, other], axis=1), jnp.concatenate([other, mine], axis=1)
    )
    turned_rest, k_rest, v_rest = prep(scalar, pieces, ids, pos_rest, vectors, w_qkv, False)
    mixed, lse = attention_rest(scalar, q, k_rest, v_rest, state)

    out, grad_middle, grad_mixed, delta, kept, sent, grad_b_up, feed_vec = feed_forward(
        scalar, mixed, start, d_out[0], w_out, pack(b_out, ln2_gain, ln2_bias, b_down), w_up, b_up[None], w_down
    )

    def grad_group(group, carried):
        k, v, turned = (k_rest, v_rest, turned_rest) if group else (k_own, v_own, turned_own)
        return attention_grad(scalar, group, q, grad_mixed, k, v, lse, delta, turned, w_qkv, carried)

    got = swap(sent)
    *carried, part = grad_group(3, None)
    feed = total((kept, got)).astype(bf)
    carried, part, feed = barrier((carried, part, feed))
    from_3 = shift(part, "x", 2)
    feed_got = exchange(feed)
    *carried, part = grad_group(1, carried)
    carried, part = barrier((carried, part))
    from_1 = shift(part, "x", 3)
    *carried, part = grad_group(2, carried)
    carried, part, from_3 = barrier((carried, part, from_3))
    from_2 = shift(part, "x", 1)
    at_kept, at_sent, grad_b_query, grad_b_value, part = grad_group(0, carried)
    at_kept, at_sent, part, from_1, from_2, feed_got = barrier((at_kept, at_sent, part, from_1, from_2, feed_got))

    at_got = swap(at_sent)
    feed_chunk = jnp.sum(feed_got.astype(f32), axis=0).astype(bf)
    feed_peers = peers(feed_chunk, "x")
    tail_kept, tail_sent, *shares = finish(
        scalar,
        part,
        (from_3, from_1, from_2),
        start,
        grad_middle,
        vectors,
        grad_b_query,
        grad_b_value,
        feed_vec,
        grad_b_up,
        ids,
    )
    at = total((at_kept, at_got)).astype(bf)
    at_peers = [shift(at[step], "x", step) for step in (1, 2, 3)]
    returned = [shares[0], shift(shares[1], "x", 3), shift(shares[2], "x", 1), shift(shares[3], "x", 2)]
    tail_got = swap(tail_sent)
    at_unit = total([at[0]] + at_peers).astype(bf)
    tail = total((tail_kept, tail_got)).astype(bf)
    bundle = jnp.concatenate([at_unit.reshape(SPREAD, SPREAD, -1), tail.reshape(SPREAD, SPREAD, -1)], axis=2)
    bundle, feed_peers = barrier((bundle, feed_peers))
    feed_sum = total([feed_chunk] + feed_peers).astype(bf)
    feed_mine = lax.all_gather(feed_sum, PLANE, axis=0, tiled=True)

    chunk = jnp.sum(exchange(bundle).astype(f32), axis=0).astype(bf)
    chunk, returned = barrier((chunk, returned))
    gathered = exchange(jnp.broadcast_to(chunk[None], (SPREAD,) + chunk.shape))
    lanes = at_unit.shape[1]
    at_mine = gathered[:, :, :lanes].reshape(-1, lanes)
    tail_mine = gathered[:, :, lanes:]
    lines = tail_mine[(half + PAD) // SPREAD]
    extra = jnp.concatenate([lines[:, :lanes], jnp.pad(lines[:, lanes:], ((0, 0), (0, 2 * lanes - width)))], axis=0)
    message = jnp.concatenate([at_mine, extra], axis=0)
    messages = jnp.stack([message] + peers(message, "x"))
    pos_mine = tail_mine.reshape(-1, width)[:half]
    pos_other = swap(pos_mine)
    messages, feed_mine = barrier((messages, feed_mine))
    other = swap(messages)
    feed_mine = feed_mine.reshape(SPREAD, -1, width)
    feed_other = swap(feed_mine)
    grad_pos = jnp.where(
        first_core, jnp.concatenate([pos_mine, pos_other]), jnp.concatenate([pos_other, pos_mine])
    ).astype(f32)
    sums = jnp.sum(messages[:, at_mine.shape[0] :].astype(f32), axis=0)
    sums = jnp.concatenate([sums[:SPREAD], sums[SPREAD:, : width - lanes]], axis=1)
    grad_vis = total(returned).astype(bf)
    grad_w_qkv = unpack_qkv(scalar, messages, other, width)
    grad_w_down, grad_w_up, grad_w_out = unpack_feed(scalar, feed_mine, feed_other, width, hidden)
    blocks = hidden // width

    return (
        out[None],
        grad_vis[None],
        sums[0],
        grad_pos,
        sums[1],
        sums[2],
        grad_w_qkv,
        sums[3],
        sums[4],
        grad_w_out.reshape(width, width),
        sums[5],
        sums[6],
        sums[7],
        grad_w_up,
        sums[9 : 9 + blocks].reshape(hidden),
        grad_w_down,
        sums[8],
    )


CUBE = ("z", "y", "core")


def solution(mesh):
    fine = Mesh(mesh.devices.reshape(4, 4, 2, 4), ("z", "y", "core", "x"))
    return jax.shard_map(
        body,
        mesh=fine,
        in_specs=(
            P(CUBE, "x", None),
            P(CUBE, "x"),
            P(CUBE, "x"),
            P(CUBE, None),
            P(),
            P("x", None),
        )
        + (P(),) * 13
        + (P(CUBE, "x", None),),
        out_specs=(P(CUBE, "x", None), P(CUBE, "x", None), P(), P("x", None)) + (P(),) * 13,
        check_vma=False,
    )
```

```python
import functools

import jax
import jax.numpy as jnp
from jax import lax
from jax.experimental import pallas as pl
from jax.experimental.pallas import tpu as pltpu
from jax.sharding import Mesh, PartitionSpec as P

bf = jnp.bfloat16
f32 = jnp.float32

HEADS = 16
DEPTH = 32
QUAD = 4
GROUPS = 4
LOG2E = 1.4426950408889634
SCALE = DEPTH**-0.5
EPS = 1e-05
BIG = 1e30
GELU_SCALE = 0.7978845608028654
GELU_CUBE = 0.044715
RELATIVE = (0, 3, 1, 2)
MARKS = 16
SPREAD = 16

NT = (((1,), (1,)), ((), ()))
NN = (((1,), (0,)), ((), ()))
TN = (((0,), (0,)), ((), ()))
VMEM_LIMIT = 56 * 1024 * 1024


def dg(a, b, dims):
    return lax.dot_general(a, b, dims, preferred_element_type=f32)


def sds(shape, dtype):
    return jax.ShapeDtypeStruct(shape, dtype)


def call(kernel, name, scalar, operands, out_shape, scratch=(), aliases=None, limit=16):
    inside = pl.BlockSpec(memory_space=pltpu.VMEM)
    return pl.pallas_call(
        kernel,
        in_specs=[pl.BlockSpec(memory_space=pltpu.SMEM)] + [inside] * len(operands),
        out_specs=[inside] * len(out_shape),
        out_shape=out_shape,
        scratch_shapes=list(scratch),
        compiler_params=pltpu.CompilerParams(vmem_limit_bytes=limit * 1024 * 1024),
        cost_estimate=pl.CostEstimate(flops=1000, bytes_accessed=1000, transcendentals=0),
        input_output_aliases=aliases or {},
        name=name,
    )(scalar, *operands)


def grid_call(kernel, name, scalar, steps, in_specs, out_specs, out_shape, operands):
    return pl.pallas_call(
        kernel,
        grid_spec=pltpu.PrefetchScalarGridSpec(
            num_scalar_prefetch=1, grid=(steps,), in_specs=in_specs, out_specs=out_specs
        ),
        out_shape=out_shape,
        compiler_params=pltpu.CompilerParams(vmem_limit_bytes=32 * 1024 * 1024),
        cost_estimate=pl.CostEstimate(flops=1000, bytes_accessed=1000, transcendentals=0),
        name=name,
    )(scalar, *operands)


def column_sum(tensor):
    return jnp.sum(tensor.astype(f32), axis=0, keepdims=True)


def norm_parts(values):
    centered = values - jnp.mean(values, axis=-1, keepdims=True)
    variance = jnp.mean(centered * centered, axis=-1, keepdims=True)
    inverse = lax.rsqrt(variance + EPS)
    return centered * inverse, inverse


def norm_pull(grad, n, inverse, gain):
    g = grad * gain
    return inverse * (
        g - jnp.mean(g, axis=-1, keepdims=True) - n * jnp.mean(g * n, axis=-1, keepdims=True)
    )


def place_rows(base, pieces, ids, pos, rows_ref):
    rows, width = pos.shape
    piece = ids[0].shape[1]
    slot = lax.broadcasted_iota(jnp.int32, (rows, piece), 0) + base
    placed = jnp.zeros((rows, width), f32)
    seen = jnp.zeros((rows, 1), f32)
    for v, i in zip(pieces, ids):
        hot = (slot == i[...]).astype(f32)
        seen += jnp.sum(hot, axis=1, keepdims=True)
        placed += dg(hot.astype(bf), v[MARKS : MARKS + piece, :], NN)
    start = placed + (1.0 - seen) * rows_ref[0:1] + pos
    n, _ = norm_parts(start)
    return start, (n * rows_ref[1:2] + rows_ref[2:3]).astype(bf)


def keys_values(normed, rows_ref, w_ref, turned_ref, k_ref, v_ref):
    width = normed.shape[1]
    k_ref[...] = dg(normed, w_ref[:, width : 2 * width], NN).astype(bf)
    v_ref[...] = (dg(normed, w_ref[:, 2 * width :], NN) + rows_ref[4:5]).astype(bf)
    turned_ref[...] = normed.T


def stack_heads(x):
    lane = lax.broadcasted_iota(jnp.int32, x.shape, 1) // DEPTH
    return jnp.concatenate([jnp.where(lane == h, x, jnp.zeros_like(x)) for h in range(QUAD)], axis=0)


def unstack_heads(xt):
    rows = xt.shape[1] // QUAD
    parts = [xt[DEPTH * h : DEPTH * (h + 1), rows * h : rows * (h + 1)] for h in range(QUAD)]
    return jnp.concatenate(parts, axis=0).T


def fwd_step(state, live, k, v, qs):
    s = dg(k, qs, NT)
    peak = jnp.where(live, jnp.max(s, axis=0, keepdims=True), -BIG)
    if state is not None:
        peak = jnp.maximum(state[0], peak)
    p = jnp.exp2(s - jnp.where(live, peak, BIG))
    l = jnp.sum(p, axis=0, keepdims=True)
    o = dg(v, p.astype(bf), TN)
    if state is not None:
        keep = jnp.exp2(state[0] - peak)
        l += state[1] * keep
        o += state[2] * keep
    return (peak, l, o)


def front_kernel(scalar_ref, *refs):
    pieces, (pos_hbm, rows_ref, w_hbm), refs = refs[:GROUPS], refs[GROUPS : GROUPS + 3], refs[GROUPS + 3 :]
    start_ref, q_ref, turned_ref, k_ref, v_ref, *refs = refs
    ids, (pos_ref, w_ref, sem) = refs[:GROUPS], refs[GROUPS:]
    copies = [
        pltpu.make_async_copy(pos_hbm, pos_ref, sem.at[0]),
        pltpu.make_async_copy(w_hbm, w_ref, sem.at[1]),
    ]
    for copy in copies:
        copy.start()
    piece = ids[0].shape[1]
    for v, i in zip(pieces, ids):
        marks = v[:MARKS, :].astype(f32)[:8, :piece]
        i[...] = (marks[0:1] * 64.0 + marks[1:2]).astype(jnp.int32) - 1
    for copy in copies:
        copy.wait()
    start, normed = place_rows(scalar_ref[GROUPS], pieces, ids, pos_ref[...].astype(f32), rows_ref)
    start_ref[...] = start
    width = start.shape[1]
    q_ref[...] = ((dg(normed, w_ref[:, :width], NN) + rows_ref[3:4]) * (SCALE * LOG2E)).astype(bf)
    keys_values(normed, rows_ref, w_ref, turned_ref, k_ref, v_ref)


def front(scalar, pieces, pos, vectors, w_qkv, piece):
    rows, width = pos.shape
    inside = pl.BlockSpec(memory_space=pltpu.VMEM)
    outside = pl.BlockSpec(memory_space=pltpu.HBM)
    out_shape = [
        sds((rows, width), f32),
        sds((rows, width), bf),
        sds((width, rows), bf),
        sds((rows, width), bf),
        sds((rows, width), bf),
    ] + [sds((1, piece), jnp.int32)] * GROUPS
    return pl.pallas_call(
        front_kernel,
        in_specs=[pl.BlockSpec(memory_space=pltpu.SMEM)] + [inside] * GROUPS + [outside, inside, outside],
        out_specs=[inside] * len(out_shape),
        out_shape=out_shape,
        scratch_shapes=[
            pltpu.VMEM(pos.shape, pos.dtype),
            pltpu.VMEM(w_qkv.shape, w_qkv.dtype),
            pltpu.SemaphoreType.DMA((2,)),
        ],
        compiler_params=pltpu.CompilerParams(vmem_limit_bytes=16 * 1024 * 1024),
        cost_estimate=pl.CostEstimate(flops=1000, bytes_accessed=1000, transcendentals=0),
        name="front",
    )(scalar, *pieces, pos, vectors, w_qkv)


def attention_own_kernel(scalar_ref, q_ref, k_ref, v_ref, m_ref, l_ref, o_ref):
    for j in range(m_ref.shape[0]):
        at = (slice(None), slice(128 * j, 128 * (j + 1)))
        m_ref[j], l_ref[j], o_ref[j] = fwd_step(
            None, scalar_ref[0] > 0, k_ref[at], v_ref[at], stack_heads(q_ref[at])
        )


def attention_own(scalar, q, k, v):
    rows, width = q.shape
    quads, n = width // 128, rows * QUAD
    return call(
        attention_own_kernel,
        "attention_own",
        scalar,
        [q, k, v],
        [sds((quads, 1, n), f32), sds((quads, 1, n), f32), sds((quads, 128, n), f32)],
    )


def middle_kernel(scalar_ref, *refs):
    pieces, ids, refs = refs[:GROUPS], refs[GROUPS : 2 * GROUPS], refs[2 * GROUPS :]
    pos_refs, refs = refs[: 2 * (GROUPS - 1)], refs[2 * (GROUPS - 1) :]
    rows_ref, w_ref, q_ref, m_ref, l_ref, o_ref, *groups, mixed_ref, lse_ref = refs
    first = scalar_ref[GROUPS + GROUPS] == 0
    for g in range(GROUPS - 1):
        mine, other = pos_refs[g][...].astype(f32), pos_refs[GROUPS - 1 + g][...].astype(f32)
        pos = jnp.concatenate([jnp.where(first, mine, other), jnp.where(first, other, mine)], axis=0)
        _, normed = place_rows(scalar_ref[GROUPS + 1 + g], pieces, ids, pos, rows_ref)
        keys_values(normed, rows_ref, w_ref, *groups[3 * g : 3 * g + 3])
    for j in range(m_ref.shape[0]):
        at = (slice(None), slice(128 * j, 128 * (j + 1)))
        qs = stack_heads(q_ref[at])
        state = (m_ref[j], l_ref[j], o_ref[j])
        for g in range(GROUPS - 1):
            state = fwd_step(state, scalar_ref[g + 1] > 0, groups[3 * g + 1][at], groups[3 * g + 2][at], qs)
        m, l, o = state
        mixed_ref[at] = unstack_heads(o / l).astype(bf)
        lse_ref[j] = m + jnp.log2(l)


def middle(scalar, pieces, ids, pos, vectors, w_qkv, q, state):
    rows, width = q.shape
    quads, n = width // 128, rows * QUAD
    group = [sds((width, rows), bf), sds((rows, width), bf), sds((rows, width), bf)]
    return call(
        middle_kernel,
        "middle",
        scalar,
        [*pieces, *ids, *pos, vectors, w_qkv, q, *state],
        [*(group * (GROUPS - 1)), sds((rows, width), bf), sds((quads, 1, n), f32)],
    )


def bwd_kernel(scalar_ref, q_ref, do_ref, k_ref, v_ref, lse_ref, delta_ref, w_ref, *refs, index, carried):
    width = q_ref.shape[1]
    if carried:
        dq_in, *refs = refs
    if index == 0:
        *turned_refs, d_3, d_1, d_2, part_ref, kept_ref, sent_ref, bq_ref, bv_ref, d_s = refs
        base = width
    else:
        dq_ref, d_s, part_ref = refs
        base = 0
    dead = jnp.where(scalar_ref[index] > 0, 0.0, BIG)
    quads = width // 128
    for j in range(quads):
        at = (slice(None), slice(128 * j, 128 * (j + 1)))
        columns = lambda i: (slice(None), slice(base + (i - 1) * width + 128 * j, base + (i - 1) * width + 128 * (j + 1)))
        qs = stack_heads(q_ref[at])
        dos = stack_heads(do_ref[at])
        k, v = k_ref[at], v_ref[at]
        p = jnp.exp2(dg(k, qs, NT) - (lse_ref[j] + dead))
        ds = (p * (dg(v, dos, NT) - delta_ref[j])).astype(bf)
        d_s[columns(2)] = dg(p.astype(bf), dos, NN).astype(bf)
        d_s[columns(1)] = (dg(ds, qs, NN) * (1.0 / LOG2E)).astype(bf)
        dq = unstack_heads(dg(k, ds, TN))
        if carried:
            dq += dq_in[at]
        if index == 0:
            d_s[at] = (dq * SCALE).astype(bf)
        else:
            dq_ref[at] = dq
    grads = d_s[...]
    part_ref[...] = dg(grads, w_ref[...] if index == 0 else w_ref[:, width:], NT).astype(part_ref.dtype)
    if index != 0:
        return
    own, *rest = turned_refs
    g = dg(own[...], grads[:, width:], NN)
    bv = column_sum(grads[:, 2 * width :])
    for turned, d_ref in zip(rest, (d_1, d_2, d_3)):
        d = d_ref[...]
        g += dg(turned[...], d, NN)
        bv += column_sum(d[:, width:])
    bv_ref[...] = bv
    bq_ref[...] = column_sum(grads[:, :width])
    gq = dg(own[...], grads[:, :width], NN)
    first = scalar_ref[GROUPS + 4] == 0
    half = width // 2
    for j in range(quads):
        at = slice(128 * j, 128 * (j + 1))
        block = jnp.concatenate([gq[:, at], g[:, at], g[:, width + 128 * j : width + 128 * (j + 1)]], axis=1)
        kept_ref[j] = jnp.where(first, block[:half], block[half:]).astype(bf)
        sent_ref[j] = jnp.where(first, block[half:], block[:half]).astype(bf)


def attention_grad(scalar, index, q, do, k, v, lse, delta, w_qkv, dq, more=()):
    rows, width = q.shape
    operands = [q, do, k, v, lse, delta, w_qkv]
    aliases = {}
    if dq is not None:
        aliases = {len(operands) + 1: 0}
        operands.append(dq)
    operands += list(more)
    scratch = []
    if index == 0:
        packed = (width // 128, width // 2, 3 * 128)
        out_shape = [sds((rows, width), f32)] + [sds(packed, bf)] * 2 + [sds((1, width), f32)] * 2
        scratch = [pltpu.VMEM((rows, 3 * width), bf)]
    else:
        out_shape = [sds((rows, width), f32), sds((rows, 2 * width), bf), sds((rows, width), bf)]
    return call(
        functools.partial(bwd_kernel, index=index, carried=dq is not None),
        "attention_grad_%d" % index,
        scalar,
        operands,
        out_shape,
        scratch,
        aliases,
    )


def feed_kernel(
    scalar_ref,
    mixed_ref,
    start_ref,
    dout_ref,
    wout_ref,
    rows_ref,
    wup_ref,
    bup_ref,
    wdown_ref,
    out_ref,
    middle_ref,
    second_ref,
    kept_ref,
    sent_ref,
    gbup_ref,
):
    first = scalar_ref[GROUPS + 4] == 0
    width = mixed_ref.shape[1]
    hidden = wup_ref.shape[1]
    dout = dout_ref[...]
    middle = start_ref[...] + (dg(mixed_ref[...], wout_ref[...], NN) + rows_ref[0:1])
    middle_ref[...] = middle
    n, _ = norm_parts(middle)
    normed = (n * rows_ref[1:2] + rows_ref[2:3]).astype(bf)
    turned = normed.T
    result = middle + rows_ref[3:4]
    second = jnp.zeros_like(middle)
    lines = hidden // SPREAD
    for h in range(hidden // width):
        at = slice(width * h, width * (h + 1))
        u = dg(normed, wup_ref[:, at], NN) + bup_ref[:, at]
        square = u * u
        t = jnp.tanh(u * (GELU_SCALE + (GELU_SCALE * GELU_CUBE) * square))
        near = 0.5 + 0.5 * t
        act = (u * near).astype(bf)
        result += dg(act, wdown_ref[at, :], NN)
        slope = near + u * (0.5 - 0.5 * (t * t)) * (GELU_SCALE + (3.0 * GELU_SCALE * GELU_CUBE) * square)
        gup = (dg(dout, wdown_ref[at, :], NT) * slope).astype(bf)
        second += dg(gup, wup_ref[:, at], NT)
        gbup_ref[:, at] = column_sum(gup)
        down = dg(act, dout, TN).astype(bf)
        up = dg(turned, gup, NN).astype(bf)
        chunks = (width // lines, lines, width)
        places = slice(h * chunks[0], (h + 1) * chunks[0])
        kept_ref[places] = jnp.where(first, down, up).reshape(chunks)
        sent_ref[places] = jnp.where(first, up, down).reshape(chunks)
    out_ref[...] = result.astype(bf)
    second_ref[...] = second


def feed_backward_kernel(
    scalar_ref,
    mixed_ref,
    middle_ref,
    second_ref,
    dout_ref,
    wout_ref,
    rows_ref,
    gmid_ref,
    gmix_ref,
    delta_ref,
    kept_ref,
    sent_ref,
    vec_ref,
):
    first = scalar_ref[GROUPS + 4] == 0
    mixed = mixed_ref[...]
    width = mixed.shape[1]
    second = second_ref[...]
    grad = dout_ref[...].astype(f32)
    n, inverse = norm_parts(middle_ref[...])
    gmid = grad + norm_pull(second, n, inverse, rows_ref[1:2])
    gmid_ref[...] = gmid
    branch = gmid.astype(bf)
    gmix = dg(branch, wout_ref[...], NT).astype(bf)
    gmix_ref[...] = gmix
    wout = dg(mixed, branch, TN)
    half = width // 2
    extra = (SPREAD, half // SPREAD, width)
    kept_ref[...] = jnp.where(first, wout[:half], wout[half:]).astype(bf).reshape(extra)
    sent_ref[...] = jnp.where(first, wout[half:], wout[:half]).astype(bf).reshape(extra)
    vec_ref[...] = jnp.concatenate(
        [
            column_sum(branch),
            column_sum(second * n),
            column_sum(second),
            column_sum(grad),
            jnp.zeros((4, width), f32),
        ],
        axis=0,
    )
    product = mixed.astype(f32) * gmix.astype(f32)
    head = lax.broadcasted_iota(jnp.int32, (HEADS, width), 0)
    lane = lax.broadcasted_iota(jnp.int32, (HEADS, width), 1) // DEPTH
    pick = (head == lane).astype(bf)
    high = product.astype(bf)
    low = (product - high.astype(f32)).astype(bf)
    delta = dg(pick, high, NT) + dg(pick, low, NT)
    for j in range(HEADS // QUAD):
        delta_ref[j] = jnp.concatenate([delta[QUAD * j + i : QUAD * j + i + 1] for i in range(QUAD)], axis=1)


def feed_forward(scalar, mixed, start, d_out, w_out, vectors, w_up, b_up, w_down):
    rows, width = mixed.shape
    hidden = w_up.shape[1]
    packed = (SPREAD, hidden // SPREAD, width)
    return call(
        feed_kernel,
        "feed_forward",
        scalar,
        [mixed, start, d_out, w_out, vectors, w_up, b_up, w_down],
        [sds((rows, width), bf)] + [sds((rows, width), f32)] * 2 + [sds(packed, bf)] * 2 + [sds((1, hidden), f32)],
    )


def feed_backward(scalar, mixed, middle, second, d_out, w_out, vectors):
    rows, width = mixed.shape
    packed = (SPREAD, width // 2 // SPREAD, width)
    return call(
        feed_backward_kernel,
        "feed_backward",
        scalar,
        [mixed, middle, second, d_out, w_out, vectors],
        [
            sds((rows, width), f32),
            sds((rows, width), bf),
            sds((HEADS // QUAD, 1, QUAD * rows), f32),
            sds(packed, bf),
            sds(packed, bf),
            sds((8, width), f32),
        ],
    )


def turn(place, steps):
    return lax.rem(place + steps, GROUPS)


def fold_feed_kernel(scalar_ref, a, b, c, d, *outs):
    first, y, z = scalar_ref[GROUPS + 4] == 0, scalar_ref[GROUPS + 6], scalar_ref[GROUPS + 7]
    near = jnp.where(first, y, z)
    lines = a.shape[1]
    for r, out_ref in enumerate(outs):
        place = turn(near, r)
        for i in range(GROUPS):
            at = jnp.where(first, GROUPS * i + place, GROUPS * place + i)
            out_ref[i, :lines] = (a[at].astype(f32) + b[at].astype(f32)).astype(bf)
            out_ref[i, lines:] = (c[at].astype(f32) + d[at].astype(f32)).astype(bf)


def fold_feed(scalar, a, b, c, d):
    shape = sds((GROUPS, a.shape[1] + c.shape[1], a.shape[2]), bf)
    return call(fold_feed_kernel, "fold_feed", scalar, [a, b, c, d], [shape] * GROUPS)


def fold_line_kernel(scalar_ref, *refs):
    sources, outs = refs[:GROUPS], refs[GROUPS:]
    far = jnp.where(scalar_ref[GROUPS + 4] == 0, scalar_ref[GROUPS + 7], scalar_ref[GROUPS + 6])
    for r, out_ref in enumerate(outs):
        at = turn(far, r)
        out_ref[...] = sum(ref[at].astype(f32) for ref in sources).astype(bf)


def fold_line(scalar, sources):
    return call(fold_line_kernel, "fold_line", scalar, sources, [sds(sources[0].shape[1:], bf)] * GROUPS)


def add_up_kernel(scalar_ref, *refs):
    *sources, out_ref = refs
    out_ref[...] = sum(ref[...].astype(f32) for ref in sources).astype(bf)


def add_up(scalar, name, arrays):
    return call(add_up_kernel, name, scalar, list(arrays), [sds(arrays[0].shape, bf)])[0]


def fold_rest_kernel(scalar_ref, a, b, c, d, out_ref):
    cut = a.shape[2]
    out_ref[:, :, :cut] = (a[...].astype(f32) + b[...].astype(f32)).astype(bf)
    out_ref[:, :, cut:] = (c[...].astype(f32) + d[...].astype(f32)).astype(bf)


def fold_rest(scalar, a, b, c, d):
    shape = a.shape[:2] + (a.shape[2] + c.shape[2],)
    return call(fold_rest_kernel, "fold_rest", scalar, [a, b, c, d], [sds(shape, bf)])[0]


def sum_space_kernel(scalar_ref, got_ref, out_ref):
    chunk = got_ref.shape[0] // GROUPS
    lanes = 3 * 128
    sums = []
    for x in range(GROUPS):
        acc = got_ref[chunk * x].astype(f32)
        for i in range(1, chunk):
            acc += got_ref[chunk * x + i].astype(f32)
        sums.append(acc)
    everything = functools.reduce(jnp.add, sums)
    shared = scalar_ref[GROUPS + 5] > 0
    for x in range(GROUPS):
        tail = jnp.where(shared, everything[:, lanes:], sums[x][:, lanes:])
        block = jnp.concatenate([everything[:, :lanes], tail], axis=1).astype(bf)
        for i in range(chunk):
            out_ref[chunk * x + i] = block


def sum_space(scalar, got):
    return call(sum_space_kernel, "sum_space", scalar, [got], [sds(got.shape, bf)])[0]


def finish_kernel(
    scalar_ref, part_ref, r3, r1, r2, start_ref, gmid_ref, rows_ref, bq_ref, bv_ref, feed_ref, bup_ref, *refs
):
    id_refs, (kept_ref, sent_ref), share_refs = refs[:GROUPS], refs[GROUPS : GROUPS + 2], refs[GROUPS + 2 :]
    rows, width = start_ref.shape
    first_grad = part_ref[...] + r3[...].astype(f32) + r1[...].astype(f32) + r2[...].astype(f32)
    n, inverse = norm_parts(start_ref[...])
    grad = gmid_ref[...] + norm_pull(first_grad, n, inverse, rows_ref[1:2])
    half = rows // 2
    first = scalar_ref[GROUPS + 4] == 0
    top, low = grad[:half], grad[half:]
    grad_low = grad.astype(bf)
    piece = id_refs[0].shape[1]
    slot = lax.broadcasted_iota(jnp.int32, (rows, piece), 0) + scalar_ref[GROUPS]
    seen = jnp.zeros((rows, 1), f32)
    for id_ref, share_ref in zip(id_refs, share_refs):
        hot = (slot == id_ref[...]).astype(f32)
        seen += jnp.sum(hot, axis=1, keepdims=True)
        share_ref[...] = dg(hot.astype(bf), grad_low, TN).astype(bf)
    lines = [
        column_sum((1.0 - seen) * grad),
        column_sum(first_grad * n),
        column_sum(first_grad),
        bq_ref[...],
        bv_ref[...],
        feed_ref[:4],
    ]
    blocks = bup_ref.shape[1] // width
    lines += [bup_ref[:, width * i : width * (i + 1)] for i in range(blocks)]
    spare = 16 - sum(a.shape[0] for a in lines)
    lines = jnp.concatenate(lines + [jnp.zeros((spare, width), f32)], axis=0)

    def narrow(values):
        cut = [a[:, 128 * i : 128 * (i + 1)] for a in (values, lines) for i in range(width // 128)]
        cut.append(jnp.zeros((kept_ref.shape[0] * kept_ref.shape[1] - sum(a.shape[0] for a in cut), 128), f32))
        return jnp.concatenate(cut, axis=0).reshape(kept_ref.shape).astype(bf)

    kept_ref[...] = narrow(jnp.where(first, top, low))
    sent_ref[...] = narrow(jnp.where(first, low, top))


def finish(scalar, part, received, start, gmid, vectors, bq, bv, feed_vec, grad_b_up, ids):
    rows, width = start.shape
    piece = ids[0].shape[1]
    tail = sds((GROUPS * SPREAD, 16, 128), bf)
    return call(
        finish_kernel,
        "finish",
        scalar,
        [part, *received, start, gmid, vectors, bq, bv, feed_vec, grad_b_up, *ids],
        [tail, tail] + [sds((piece, width), bf)] * GROUPS,
    )


def unpack_feed_kernel(scalar_ref, *refs):
    *sources, down_ref, up_ref, out_ref = refs
    mine, other = sources[:GROUPS], sources[GROUPS:]
    first = scalar_ref[GROUPS + 4] == 0
    y = scalar_ref[GROUPS + 6]
    lines = down_ref.shape[0] // GROUPS
    extra = out_ref.shape[1] // GROUPS

    def unpack(g):
        for k, far in enumerate(RELATIVE):
            place = turn(y, far)
            low = jnp.where(first, mine[k][g], other[k][g]).astype(f32)
            high = jnp.where(first, other[g][k], mine[g][k]).astype(f32)
            at = pl.ds(pl.multiple_of(lines * place, 16), lines)
            down_ref[at, :] = low[:lines]
            up_ref[at, :] = high[:lines]
            at = pl.ds(pl.multiple_of(extra * place, 16), extra)
            out_ref[0, at, :] = low[lines:]
            out_ref[1, at, :] = high[lines:]

    for g in range(GROUPS):
        pl.when(pl.program_id(0) == g)(functools.partial(unpack, g))


def unpack_feed(scalar, mine, other, width, hidden):
    block = pl.BlockSpec(mine[0].shape, lambda g, s: (0, 0, 0))
    extra = width // 2 // GROUPS
    return grid_call(
        unpack_feed_kernel,
        "unpack_feed",
        scalar,
        GROUPS,
        [block] * (2 * GROUPS),
        [
            pl.BlockSpec((width, width), lambda g, s: (s[GROUPS + 8 + g], 0)),
            pl.BlockSpec((width, width), lambda g, s: (0, s[GROUPS + 8 + g])),
            pl.BlockSpec((2, extra, width), lambda g, s: (0, s[GROUPS + 8 + g], 0)),
        ],
        [sds((hidden, width), f32), sds((width, hidden), f32), sds((2, width // 2, width), f32)],
        [*mine, *other],
    )


def unpack_rest_kernel(scalar_ref, mine_ref, other_ref, out_ref, pos_ref, vec_ref):
    core = scalar_ref[GROUPS + 4]
    half = out_ref.shape[0] // 2
    width = out_ref.shape[1] // 3
    rows = pos_ref.shape[0] // 2
    chunk = mine_ref.shape[0] // GROUPS
    for kept, ref in ((core, mine_ref), (1 - core, other_ref)):
        lines = pl.ds(pl.multiple_of(kept * half, half), half)
        for j in range(GROUPS):
            for w in range(3):
                lanes = slice(w * width + 128 * j, w * width + 128 * (j + 1))
                block = ref[chunk * j : chunk * (j + 1), :, 128 * w : 128 * (w + 1)]
                out_ref[lines, lanes] = block.reshape(half, 128).astype(f32)
        tail = ref[:, :, 3 * 128 :].astype(f32).reshape(-1, 128)
        lines = pl.ds(pl.multiple_of(kept * rows, 8), rows)
        blocks = width // 128
        for i in range(blocks):
            pos_ref[lines, 128 * i : 128 * (i + 1)] = tail[rows * i : rows * (i + 1)]
            if ref is mine_ref:
                vec_ref[:, 128 * i : 128 * (i + 1)] = tail[rows * blocks + 16 * i : rows * blocks + 16 * (i + 1)]


def unpack_rest(scalar, mine, other, rows, width):
    return call(
        unpack_rest_kernel,
        "unpack_rest",
        scalar,
        [mine, other],
        [sds((width, 3 * width), f32), sds((rows, width), f32), sds((16, width), f32)],
    )


def shift(array, axis, step):
    size = lax.axis_size(axis)
    return lax.ppermute(array, axis, [(i, (i + step) % size) for i in range(size)])


def peers(array, axis):
    return [shift(array, axis, step) for step in (1, 3, 2)]


def swap(array):
    return shift(array, "core", 1)


def total(parts):
    return functools.reduce(jnp.add, [p.astype(f32) for p in parts])


SPACE = ("x", "z", "y")
PLANE = ("z", "y", "core")


def step_plane(array, step, near):
    sizes = [lax.axis_size(name) for name in PLANE]
    pairs = []
    for z in range(sizes[0]):
        for y in range(sizes[1]):
            for core in range(sizes[2]):
                if (core == 0) == near:
                    target = (z, (y + step) % sizes[1], core)
                else:
                    target = ((z + step) % sizes[0], y, core)
                index = lambda p: (p[0] * sizes[1] + p[1]) * sizes[2] + p[2]
                pairs.append((index((z, y, core)), index(target)))
    return lax.ppermute(array, PLANE, pairs)


def plane_peers(array, near):
    return [step_plane(array, step, near) for step in (1, 3, 2)]


def exchange(array, axes):
    return lax.all_to_all(array, axes, 0, 0, tiled=True)


def body(
    vis,
    keep_slots,
    counts,
    band_mask,
    mask_token,
    pos,
    ln1_gain,
    ln1_bias,
    w_qkv,
    b_query,
    b_value,
    w_out,
    b_out,
    ln2_gain,
    ln2_bias,
    w_up,
    b_up,
    w_down,
    b_down,
    d_out,
):
    barrier = lax.optimization_barrier
    x = lax.axis_index("x")
    core = lax.axis_index("core")
    piece = keep_slots.shape[1]
    rows, width = pos.shape
    half = rows // 2
    hidden = w_up.shape[1]

    vis = vis[0]

    y, z = lax.axis_index("y"), lax.axis_index("z")
    relative = jnp.array(RELATIVE, jnp.int32)
    order = (x + relative) % GROUPS
    live = jnp.sum(jnp.where(order[:, None] == jnp.arange(GROUPS)[None, :], band_mask, 0), axis=1)
    here = (x * lax.axis_size("z") + z) * lax.axis_size("y") + y
    chunks = width // 128 * half // 16
    shared = (here >= chunks) & (here < chunks + width // 128)
    scalar = jnp.concatenate(
        [live, order * rows, jnp.stack([core, shared.astype(jnp.int32), y, z]), (z + relative) % GROUPS]
    ).astype(jnp.int32)
    pack = lambda *vs: jnp.pad(jnp.stack(vs), ((0, 8 - len(vs)), (0, 0)))
    vectors = pack(mask_token, ln1_gain, ln1_bias, b_query, b_value)
    feed_vectors = pack(b_out, ln2_gain, ln2_bias, b_down)

    index = lax.broadcasted_iota(jnp.int32, (1, piece), 1)
    code = jnp.where(index < counts, keep_slots, -1) + 1
    marks = jnp.concatenate([code // 64, code % 64], axis=0).astype(bf)
    marks = jnp.pad(marks, ((0, MARKS - 2), (0, width - piece)))
    message = jnp.concatenate([marks, vis], axis=0)
    pieces = [message] + peers(message, "x")
    pos_half = lax.dynamic_slice(pos, (half * core, 0), (half, width))
    pos_mine = peers(pos_half, "x")
    scalar, vectors, feed_vectors, pieces = barrier((scalar, vectors, feed_vectors, pieces))
    start, q, turned_own, k_own, v_own, *ids = front(scalar, pieces, pos, vectors, w_qkv, piece)
    k_own, pos_mine = barrier((k_own, pos_mine))
    pos_other = [swap(p) for p in pos_mine]
    state = attention_own(scalar, q, k_own, v_own)
    state, pos_other = barrier((state, pos_other))
    *rest, mixed, lse = middle(scalar, pieces, ids, pos_mine + pos_other, vectors, w_qkv, q, state)

    out, middle_rows, second, kept, sent, grad_b_up = feed_forward(
        scalar, mixed, start, d_out[0], w_out, feed_vectors, w_up, b_up[None], w_down
    )
    got = swap(sent)
    grad_middle, grad_mixed, delta, out_kept, out_sent, feed_vec = feed_backward(
        scalar, mixed, middle_rows, second, d_out[0], w_out, feed_vectors
    )
    feed = fold_feed(scalar, kept, got, out_kept, swap(out_sent))
    grad_mixed, feed = barrier((grad_mixed, feed))
    feed = [feed[0]] + [step_plane(feed[r], r, True) for r in (1, 2, 3)]

    def grad_group(group, dq):
        _, k, v = rest[3 * group - 3 : 3 * group]
        return attention_grad(scalar, group, q, grad_mixed, k, v, lse, delta, w_qkv, dq)

    dq, d_3, part = grad_group(3, None)
    dq, part = barrier((dq, part))
    from_3 = shift(part, "x", 2)
    dq, d_1, part = grad_group(1, dq)
    feed = fold_line(scalar, feed)
    dq, part, feed = barrier((dq, part, feed))
    feed = [feed[0]] + [step_plane(feed[r], r, False) for r in (1, 2, 3)]
    from_1 = shift(part, "x", 3)
    dq, d_2, part = grad_group(2, dq)
    feed = add_up(scalar, "fold_point", feed)
    dq, part, from_3, feed = barrier((dq, part, from_3, feed))
    from_2 = shift(part, "x", 1)
    feed_peers = peers(feed, "x")
    part, at_kept, at_sent, grad_b_query, grad_b_value = attention_grad(
        scalar, 0, q, grad_mixed, k_own, v_own, lse, delta, w_qkv, dq, [turned_own, *rest[0::3], d_3, d_1, d_2]
    )
    at_kept, at_sent, part, from_1, from_2, feed_peers = barrier(
        (at_kept, at_sent, part, from_1, from_2, feed_peers)
    )

    at_got = swap(at_sent)
    tail_kept, tail_sent, *shares = finish(
        scalar,
        part,
        (from_3, from_1, from_2),
        start,
        grad_middle,
        vectors,
        grad_b_query,
        grad_b_value,
        feed_vec,
        grad_b_up,
        ids,
    )
    feed = add_up(scalar, "sum_line", [feed] + feed_peers)
    spread = lambda a: a.reshape(GROUPS * SPREAD, 16, -1)
    bundle = fold_rest(scalar, spread(at_kept), spread(at_got), tail_kept, swap(tail_sent))
    feed = jnp.stack([feed] + plane_peers(feed, False))
    bundle, feed = barrier((bundle, feed))
    bundle = sum_space(scalar, exchange(bundle, SPACE))
    returned = [shares[0], shift(shares[1], "x", 3), shift(shares[2], "x", 1), shift(shares[3], "x", 2)]
    feed = [feed] + plane_peers(feed, True)
    bundle, returned = barrier((bundle, returned))
    rest_mine = exchange(bundle, SPACE)
    feed_other = [swap(a) for a in feed]
    grad_w_down, grad_w_up, grad_w_out = unpack_feed(scalar, feed, feed_other, width, hidden)
    grad_vis = total(returned).astype(bf)
    rest_mine, grad_w_down, grad_vis = barrier((rest_mine, grad_w_down, grad_vis))
    rest_other = swap(rest_mine)
    grad_w_qkv, grad_pos, sums = unpack_rest(scalar, rest_mine, rest_other, rows, width)
    blocks = hidden // width

    return (
        out[None],
        grad_vis[None],
        sums[0],
        grad_pos,
        sums[1],
        sums[2],
        grad_w_qkv,
        sums[3],
        sums[4],
        grad_w_out.reshape(width, width),
        sums[5],
        sums[6],
        sums[7],
        grad_w_up,
        sums[9 : 9 + blocks].reshape(hidden),
        grad_w_down,
        sums[8],
    )


CUBE = ("z", "y", "core")


def solution(mesh):
    fine = Mesh(mesh.devices.reshape(4, 4, 2, 4), ("z", "y", "core", "x"))
    return jax.shard_map(
        body,
        mesh=fine,
        in_specs=(
            P(CUBE, "x", None),
            P(CUBE, "x"),
            P(CUBE, "x"),
            P(CUBE, None),
            P(),
            P("x", None),
        )
        + (P(),) * 13
        + (P(CUBE, "x", None),),
        out_specs=(P(CUBE, "x", None), P(CUBE, "x", None), P(), P("x", None)) + (P(),) * 13,
        check_vma=False,
    )
```

```python
import functools

import jax
import jax.numpy as jnp
from jax import lax
from jax.experimental import pallas as pl
from jax.experimental.pallas import tpu as pltpu
from jax.sharding import Mesh, PartitionSpec as P

bf = jnp.bfloat16
f32 = jnp.float32

HEADS = 16
DEPTH = 32
QUAD = 4
GROUPS = 4
LOG2E = 1.4426950408889634
SCALE = DEPTH**-0.5
EPS = 1e-05
BIG = 1e30
GELU_SCALE = 0.7978845608028654
GELU_CUBE = 0.044715
RELATIVE = (0, 3, 1, 2)
MARKS = 16
SPREAD = 16

NT = (((1,), (1,)), ((), ()))
NN = (((1,), (0,)), ((), ()))
TN = (((0,), (0,)), ((), ()))
VMEM_LIMIT = 56 * 1024 * 1024


def dg(a, b, dims):
    return lax.dot_general(a, b, dims, preferred_element_type=f32)


def sds(shape, dtype):
    return jax.ShapeDtypeStruct(shape, dtype)


def call(kernel, name, scalar, operands, out_shape, scratch=(), aliases=None, limit=11, micro=0.001):
    inside = pl.BlockSpec(memory_space=pltpu.VMEM)
    return pl.pallas_call(
        kernel,
        in_specs=[pl.BlockSpec(memory_space=pltpu.SMEM)] + [inside] * len(operands),
        out_specs=[inside] * len(out_shape),
        out_shape=out_shape,
        scratch_shapes=list(scratch),
        compiler_params=pltpu.CompilerParams(vmem_limit_bytes=limit * 1024 * 1024),
        cost_estimate=pl.CostEstimate(flops=int(micro * 1e9), bytes_accessed=1000, transcendentals=0),
        input_output_aliases=aliases or {},
        name=name,
    )(scalar, *operands)


def grid_call(kernel, name, scalar, steps, in_specs, out_specs, out_shape, operands):
    return pl.pallas_call(
        kernel,
        grid_spec=pltpu.PrefetchScalarGridSpec(
            num_scalar_prefetch=1, grid=(steps,), in_specs=in_specs, out_specs=out_specs
        ),
        out_shape=out_shape,
        compiler_params=pltpu.CompilerParams(vmem_limit_bytes=32 * 1024 * 1024),
        cost_estimate=pl.CostEstimate(flops=1000, bytes_accessed=1000, transcendentals=0),
        name=name,
    )(scalar, *operands)


def column_sum(tensor):
    return jnp.sum(tensor.astype(f32), axis=0, keepdims=True)


def norm_parts(values):
    centered = values - jnp.mean(values, axis=-1, keepdims=True)
    variance = jnp.mean(centered * centered, axis=-1, keepdims=True)
    inverse = lax.rsqrt(variance + EPS)
    return centered * inverse, inverse


def norm_pull(grad, n, inverse, gain):
    g = grad * gain
    return inverse * (
        g - jnp.mean(g, axis=-1, keepdims=True) - n * jnp.mean(g * n, axis=-1, keepdims=True)
    )


def place_rows(base, pieces, ids, rows, rows_ref):
    piece, width = ids[0].shape[1], rows_ref.shape[1]
    slot = lax.broadcasted_iota(jnp.int32, (rows, piece), 0) + base
    placed = jnp.zeros((rows, width), f32)
    seen = jnp.zeros((rows, 1), f32)
    for v, i in zip(pieces, ids):
        hot = (slot == i[...]).astype(f32)
        seen += jnp.sum(hot, axis=1, keepdims=True)
        placed += dg(hot.astype(bf), v[MARKS : MARKS + piece, :], NN)
    unseen = 1.0 - seen
    return placed + unseen * rows_ref[0:1], unseen


def first_norm(start, rows_ref):
    n, _ = norm_parts(start)
    return (n * rows_ref[1:2] + rows_ref[2:3]).astype(bf)


def keys_values(normed, rows_ref, w_ref, turned_ref, k_ref, v_ref):
    width = normed.shape[1]
    k_ref[...] = dg(normed, w_ref[:, width : 2 * width], NN).astype(bf)
    v_ref[...] = (dg(normed, w_ref[:, 2 * width :], NN) + rows_ref[4:5]).astype(bf)
    turned_ref[...] = normed.T


def stack_heads(x):
    lane = lax.broadcasted_iota(jnp.int32, x.shape, 1) // DEPTH
    return jnp.concatenate([jnp.where(lane == h, x, jnp.zeros_like(x)) for h in range(QUAD)], axis=0)


def unstack_heads(xt):
    rows = xt.shape[1] // QUAD
    parts = [xt[DEPTH * h : DEPTH * (h + 1), rows * h : rows * (h + 1)] for h in range(QUAD)]
    return jnp.concatenate(parts, axis=0).T


def fwd_steps(steps, scalar_ref, query, key, value, state, keep_weights, finish):
    stacked = {}

    def scores(quad, group):
        if quad not in stacked:
            stacked[quad] = stack_heads(query(quad))
        return dg(key(quad, group), stacked[quad], NT)

    ahead = scores(*steps[0])
    for i, (quad, group) in enumerate(steps):
        s = ahead
        if i + 1 < len(steps):
            ahead = scores(*steps[i + 1])
        live = scalar_ref[group] > 0
        peak = jnp.where(live, jnp.max(s, axis=0, keepdims=True), -BIG)
        old = state(quad) if i == 0 or steps[i - 1][0] != quad else new
        if old is not None:
            peak = jnp.maximum(old[0], peak)
        p = jnp.exp2(s - jnp.where(live, peak, BIG)).astype(bf)
        keep_weights(quad, group, p, peak)
        v = value(quad, group)
        turned = jnp.concatenate([v.T, jnp.ones((16, v.shape[0]), bf)], axis=0)
        both = dg(turned, p, NN)
        o, l = both[: v.shape[1]], both[v.shape[1] : v.shape[1] + 1]
        if old is not None:
            keep = jnp.exp2(old[0] - peak)
            o += old[2] * keep
            l += old[1] * keep
        new = (peak, l, o)
        if i + 1 == len(steps) or steps[i + 1][0] != quad:
            finish(quad, new)


def quad_at(quad):
    return (slice(None), slice(128 * quad, 128 * (quad + 1)))


def front_kernel(scalar_ref, *refs):
    pieces, (pos_ref, rows_ref), refs = refs[:GROUPS], refs[GROUPS : GROUPS + 2], refs[GROUPS + 2 :]
    start_ref, normed_ref, unseen_ref, *refs = refs
    rests, ids = refs[: GROUPS - 1], refs[GROUPS - 1 :]
    rows = pos_ref.shape[0]
    piece = ids[0].shape[1]
    for v, i in zip(pieces, ids):
        marks = v[:MARKS, :].astype(f32)[:8, :piece]
        i[...] = (marks[0:1] * 64.0 + marks[1:2]).astype(jnp.int32) - 1
    start, unseen = place_rows(scalar_ref[GROUPS], pieces, ids, rows, rows_ref)
    start += pos_ref[...].astype(f32)
    start_ref[...] = start
    unseen_ref[...] = jnp.broadcast_to(unseen, unseen_ref.shape)
    normed_ref[...] = first_norm(start, rows_ref)
    for g, rest in enumerate(rests):
        rest[...], _ = place_rows(scalar_ref[GROUPS + 1 + g], pieces, ids, rows, rows_ref)


def front(scalar, pieces, pos, vectors, piece):
    rows, width = pos.shape
    return call(
        front_kernel,
        "front",
        scalar,
        [*pieces, pos, vectors],
        [sds((rows, width), f32), sds((rows, width), bf), sds((rows, 128), f32)]
        + [sds((rows, width), f32)] * (GROUPS - 1)
        + [sds((1, piece), jnp.int32)] * GROUPS,
        micro=4,
    )


def attention_own_kernel(
    scalar_ref, normed_ref, rows_ref, w_ref, q_ref, turned_ref, k_ref, v_ref, m_ref, l_ref, o_ref, p_ref
):
    normed = normed_ref[...]
    width = normed.shape[1]
    q_ref[...] = ((dg(normed, w_ref[:, :width], NN) + rows_ref[3:4]) * (SCALE * LOG2E)).astype(bf)
    keys_values(normed, rows_ref, w_ref, turned_ref, k_ref, v_ref)

    def keep_weights(quad, group, p, peak):
        p_ref[quad] = p

    def finish(quad, state):
        m_ref[quad], l_ref[quad], o_ref[quad] = state

    fwd_steps(
        [(quad, 0) for quad in range(m_ref.shape[0])],
        scalar_ref,
        lambda quad: q_ref[quad_at(quad)],
        lambda quad, group: k_ref[quad_at(quad)],
        lambda quad, group: v_ref[quad_at(quad)],
        lambda quad: None,
        keep_weights,
        finish,
    )


def attention_own(scalar, normed, vectors, w_qkv):
    rows, width = normed.shape
    quads, n = width // 128, rows * QUAD
    return call(
        attention_own_kernel,
        "attention_own",
        scalar,
        [normed, vectors, w_qkv],
        [
            sds((rows, width), bf),
            sds((width, rows), bf),
            sds((rows, width), bf),
            sds((rows, width), bf),
            sds((quads, 1, n), f32),
            sds((quads, 1, n), f32),
            sds((quads, 128, n), f32),
            sds((quads, rows, n), bf),
        ],
        micro=5,
    )


def middle_kernel(scalar_ref, *refs):
    bases, refs = refs[: GROUPS - 1], refs[GROUPS - 1 :]
    pos_refs, refs = refs[:4], refs[4:]
    rows_ref, w_ref, q_ref, m_ref, l_ref, o_ref, *refs = refs
    groups, (mixed_ref, lse_ref), kept = refs[: 3 * (GROUPS - 1)], refs[3 * (GROUPS - 1) :][:2], refs[3 * (GROUPS - 1) + 2 :]
    first = scalar_ref[GROUPS + GROUPS] == 0
    near, far, other_near, other_far = [ref[...].astype(f32) for ref in pos_refs]
    for g, base in enumerate(bases):
        if g < 2:
            pos = jnp.where(first == (g == 0), near, other_near)
        else:
            pos = jnp.concatenate([jnp.where(first, far, other_far), jnp.where(first, other_far, far)], axis=0)
        keys_values(first_norm(base[...] + pos, rows_ref), rows_ref, w_ref, *groups[3 * g : 3 * g + 3])

    def keep_weights(quad, group, p, peak):
        kept[2 * group - 2][quad] = p
        kept[2 * group - 1][quad] = peak

    def finish(quad, state):
        m, l, o = state
        mixed_ref[quad_at(quad)] = unstack_heads(o / l).astype(bf)
        lse_ref[quad] = m + jnp.log2(l)

    fwd_steps(
        [(quad, group) for quad in range(m_ref.shape[0]) for group in range(1, GROUPS)],
        scalar_ref,
        lambda quad: q_ref[quad_at(quad)],
        lambda quad, group: groups[3 * group - 2][quad_at(quad)],
        lambda quad, group: groups[3 * group - 1][quad_at(quad)],
        lambda quad: (m_ref[quad], l_ref[quad], o_ref[quad]),
        keep_weights,
        finish,
    )


def middle(scalar, bases, pos, vectors, w_qkv, q, state):
    rows, width = q.shape
    quads, n = width // 128, rows * QUAD
    group = [sds((width, rows), bf), sds((rows, width), bf), sds((rows, width), bf)]
    return call(
        middle_kernel,
        "middle",
        scalar,
        [*bases, *pos, vectors, w_qkv, q, *state],
        [*(group * (GROUPS - 1)), sds((rows, width), bf), sds((quads, 1, n), f32)]
        + [sds((quads, rows, n), bf), sds((quads, 1, n), f32)] * (GROUPS - 1),
    )


def bwd_kernel(scalar_ref, q_ref, w_ref, *refs, groups, carried):
    width = q_ref.shape[1]
    inputs, refs = [refs[5 * i : 5 * i + 5] for i in range(len(groups))], refs[5 * len(groups) :]
    if carried:
        dq_in, *refs = refs
    own = groups == (0,)
    if own:
        *turned_refs, d_3, d_1, d_2, part_ref, kept_ref, sent_ref, bq_ref, bv_ref, d_s = refs
        base, outs = width, [(d_s, part_ref)]
    else:
        dq_ref, *refs = refs
        base, outs = 0, [refs[2 * i : 2 * i + 2] for i in range(len(groups))]
    quads = width // 128
    for j in range(quads):
        at = quad_at(j)
        qs = stack_heads(q_ref[at])
        dq = dq_in[at] if carried else None
        for (do_ref, p_ref, k_ref, v_ref, delta_ref), (d_ref, _) in zip(inputs, outs):
            columns = lambda i: (
                slice(None),
                slice(base + (i - 1) * width + 128 * j, base + (i - 1) * width + 128 * (j + 1)),
            )
            dos = stack_heads(do_ref[at])
            k, p = k_ref[at], p_ref[j]
            ds = (p.astype(f32) * (dg(v_ref[at], dos, NT) - delta_ref[j])).astype(bf)
            d_ref[columns(2)] = dg(p, dos, NN).astype(bf)
            d_ref[columns(1)] = (dg(ds, qs, NN) * (1.0 / LOG2E)).astype(bf)
            term = unstack_heads(dg(k, ds, TN))
            dq = term if dq is None else dq + term
        if own:
            d_s[at] = (dq * SCALE).astype(bf)
        else:
            dq_ref[at] = dq
    for d_ref, part_ref in outs:
        grads = d_ref[...]
        part_ref[...] = dg(grads, w_ref[...] if own else w_ref[:, width:], NT).astype(part_ref.dtype)
    if not own:
        return
    own, *rest = turned_refs
    g = dg(own[...], grads[:, width:], NN)
    bv = column_sum(grads[:, 2 * width :])
    for turned, d_ref in zip(rest, (d_1, d_2, d_3)):
        d = d_ref[...]
        g += dg(turned[...], d, NN)
        bv += column_sum(d[:, width:])
    bv_ref[...] = bv
    bq_ref[...] = column_sum(grads[:, :width])
    gq = dg(own[...], grads[:, :width], NN)
    first = scalar_ref[GROUPS + 4] == 0
    half = width // 2
    for j in range(quads):
        at = slice(128 * j, 128 * (j + 1))
        block = jnp.concatenate([gq[:, at], g[:, at], g[:, width + 128 * j : width + 128 * (j + 1)]], axis=1)
        kept_ref[j] = jnp.where(first, block[:half], block[half:]).astype(bf)
        sent_ref[j] = jnp.where(first, block[half:], block[:half]).astype(bf)


def attention_grad(scalar, groups, q, w_qkv, inputs, dq, more=()):
    rows, width = q.shape
    quads = width // 128
    operands = [q, w_qkv] + [a for group in inputs for a in group]
    aliases = {}
    if dq is not None:
        aliases = {len(operands) + 1: 0}
        operands.append(dq)
    operands += list(more)
    scratch = []
    if groups == (0,):
        packed = (quads, width // 2, 3 * 128)
        out_shape = [sds((rows, width), f32)] + [sds(packed, bf)] * 2 + [sds((1, width), f32)] * 2
        scratch = [pltpu.VMEM((rows, 3 * width), bf)]
    else:
        out_shape = [sds((rows, width), f32)]
        out_shape += [sds((rows, 2 * width), bf), sds((rows, width), bf)] * len(groups)
    return call(
        functools.partial(bwd_kernel, groups=groups, carried=dq is not None),
        "attention_grad_" + "_".join(str(g) for g in groups),
        scalar,
        operands,
        out_shape,
        scratch,
        aliases,
    )


def feed_kernel(
    scalar_ref,
    mixed_ref,
    start_ref,
    dout_ref,
    wout_ref,
    rows_ref,
    wup_ref,
    bup_ref,
    wdown_ref,
    out_ref,
    middle_ref,
    second_ref,
    kept_ref,
    sent_ref,
    gbup_ref,
):
    first = scalar_ref[GROUPS + 4] == 0
    width = mixed_ref.shape[1]
    hidden = wup_ref.shape[1]
    dout = dout_ref[...]
    middle = start_ref[...] + (dg(mixed_ref[...], wout_ref[...], NN) + rows_ref[0:1])
    middle_ref[...] = middle
    n, _ = norm_parts(middle)
    normed = (n * rows_ref[1:2] + rows_ref[2:3]).astype(bf)
    turned = normed.T
    result = middle + rows_ref[3:4]
    second = jnp.zeros_like(middle)
    lines = hidden // SPREAD
    for h in range(hidden // width):
        at = slice(width * h, width * (h + 1))
        u = dg(normed, wup_ref[:, at], NN) + bup_ref[:, at]
        square = u * u
        t = jnp.tanh(u * (GELU_SCALE + (GELU_SCALE * GELU_CUBE) * square))
        near = 0.5 + 0.5 * t
        act = (u * near).astype(bf)
        result += dg(act, wdown_ref[at, :], NN)
        slope = near + u * (0.5 - 0.5 * (t * t)) * (GELU_SCALE + (3.0 * GELU_SCALE * GELU_CUBE) * square)
        gup = (dg(dout, wdown_ref[at, :], NT) * slope).astype(bf)
        second += dg(gup, wup_ref[:, at], NT)
        gbup_ref[:, at] = column_sum(gup)
        down = dg(act, dout, TN).astype(bf)
        up = dg(turned, gup, NN).astype(bf)
        chunks = (width // lines, lines, width)
        places = slice(h * chunks[0], (h + 1) * chunks[0])
        kept_ref[places] = jnp.where(first, down, up).reshape(chunks)
        sent_ref[places] = jnp.where(first, up, down).reshape(chunks)
    out_ref[...] = result.astype(bf)
    second_ref[...] = second


def feed_backward_kernel(
    scalar_ref,
    mixed_ref,
    middle_ref,
    second_ref,
    dout_ref,
    wout_ref,
    rows_ref,
    lse_ref,
    *refs,
):
    peaks, (gmid_ref, kept_ref, sent_ref, vec_ref), outs = refs[:GROUPS], refs[GROUPS : GROUPS + 4], refs[GROUPS + 4 :]
    first = scalar_ref[GROUPS + 4] == 0
    mixed = mixed_ref[...]
    width = mixed.shape[1]
    second = second_ref[...]
    grad = dout_ref[...].astype(f32)
    n, inverse = norm_parts(middle_ref[...])
    gmid = grad + norm_pull(second, n, inverse, rows_ref[1:2])
    gmid_ref[...] = gmid
    branch = gmid.astype(bf)
    gmix = dg(branch, wout_ref[...], NT).astype(bf).astype(f32)
    wout = dg(mixed, branch, TN)
    half = width // 2
    extra = (SPREAD, half // SPREAD, width)
    kept_ref[...] = jnp.where(first, wout[:half], wout[half:]).astype(bf).reshape(extra)
    sent_ref[...] = jnp.where(first, wout[half:], wout[:half]).astype(bf).reshape(extra)
    vec_ref[...] = jnp.concatenate(
        [
            column_sum(branch),
            column_sum(second * n),
            column_sum(second),
            column_sum(grad),
            jnp.zeros((4, width), f32),
        ],
        axis=0,
    )
    product = mixed.astype(f32) * gmix
    head = lax.broadcasted_iota(jnp.int32, (HEADS, width), 0)
    lane = lax.broadcasted_iota(jnp.int32, (HEADS, width), 1) // DEPTH
    pick = (head == lane).astype(bf)
    halves = lambda a: (a.astype(bf), (a - a.astype(bf).astype(f32)).astype(bf))
    high, low = halves(product)
    delta = dg(pick, high, NT) + dg(pick, low, NT)
    rows = delta.shape[1]
    for peak_ref, do_ref, delta_ref in zip(peaks, outs[:GROUPS], outs[GROUPS:]):
        lines = []
        for j in range(HEADS // QUAD):
            factor = jnp.exp2(peak_ref[j] - lse_ref[j])
            delta_ref[j] = factor * jnp.concatenate([delta[QUAD * j + i : QUAD * j + i + 1] for i in range(QUAD)], axis=1)
            lines += [factor[:, rows * i : rows * (i + 1)] for i in range(QUAD)]
        high, low = halves(jnp.concatenate(lines, axis=0))
        do_ref[...] = (gmix * (dg(high, pick, TN) + dg(low, pick, TN))).astype(bf)


def feed_forward(scalar, mixed, start, d_out, w_out, vectors, w_up, b_up, w_down):
    rows, width = mixed.shape
    hidden = w_up.shape[1]
    packed = (SPREAD, hidden // SPREAD, width)
    return call(
        feed_kernel,
        "feed_forward",
        scalar,
        [mixed, start, d_out, w_out, vectors, w_up, b_up, w_down],
        [sds((rows, width), bf)] + [sds((rows, width), f32)] * 2 + [sds(packed, bf)] * 2 + [sds((1, hidden), f32)],
    )


def feed_backward(scalar, mixed, middle, second, d_out, w_out, vectors, lse, peaks):
    rows, width = mixed.shape
    packed = (SPREAD, width // 2 // SPREAD, width)
    return call(
        feed_backward_kernel,
        "feed_backward",
        scalar,
        [mixed, middle, second, d_out, w_out, vectors, lse, *peaks],
        [sds((rows, width), f32), sds(packed, bf), sds(packed, bf), sds((8, width), f32)]
        + [sds((rows, width), bf)] * GROUPS
        + [sds(lse.shape, f32)] * GROUPS,
    )


def turn(place, steps):
    return lax.rem(place + steps, GROUPS)


def fold_feed_kernel(scalar_ref, a, b, c, d, *outs):
    first, y, z = scalar_ref[GROUPS + 4] == 0, scalar_ref[GROUPS + 6], scalar_ref[GROUPS + 7]
    near = jnp.where(first, y, z)
    lines = a.shape[1]
    for r, out_ref in enumerate(outs):
        place = turn(near, r)
        for i in range(GROUPS):
            at = jnp.where(first, GROUPS * i + place, GROUPS * place + i)
            out_ref[i, :lines] = (a[at].astype(f32) + b[at].astype(f32)).astype(bf)
            out_ref[i, lines:] = (c[at].astype(f32) + d[at].astype(f32)).astype(bf)


def fold_feed(scalar, a, b, c, d):
    shape = sds((GROUPS, a.shape[1] + c.shape[1], a.shape[2]), bf)
    return call(fold_feed_kernel, "fold_feed", scalar, [a, b, c, d], [shape] * GROUPS)


def fold_line_kernel(scalar_ref, *refs):
    sources, outs = refs[:GROUPS], refs[GROUPS:]
    for r, out_ref in enumerate(outs):
        at = turn(scalar_ref[GROUPS + 12], r)
        out_ref[...] = sum(ref[at].astype(f32) for ref in sources).astype(bf)


def fold_line(scalar, sources):
    return call(fold_line_kernel, "fold_line", scalar, sources, [sds(sources[0].shape[1:], bf)] * GROUPS)


def add_up_kernel(scalar_ref, *refs):
    *sources, out_ref = refs
    out_ref[...] = sum(ref[...].astype(f32) for ref in sources).astype(bf)


def add_up(scalar, name, arrays):
    return call(add_up_kernel, name, scalar, list(arrays), [sds(arrays[0].shape, bf)])[0]


def fold_rest_kernel(scalar_ref, a, b, c, d, out_ref):
    cut = a.shape[2]
    out_ref[:, :, :cut] = (a[...].astype(f32) + b[...].astype(f32)).astype(bf)
    out_ref[:, :, cut:] = (c[...].astype(f32) + d[...].astype(f32)).astype(bf)


def fold_rest(scalar, a, b, c, d):
    shape = a.shape[:2] + (a.shape[2] + c.shape[2],)
    return call(fold_rest_kernel, "fold_rest", scalar, [a, b, c, d], [sds(shape, bf)])[0]


def sum_space_kernel(scalar_ref, got_ref, out_ref):
    chunk = got_ref.shape[0] // GROUPS
    lanes = 3 * 128
    sums = []
    for x in range(GROUPS):
        acc = got_ref[chunk * x].astype(f32)
        for i in range(1, chunk):
            acc += got_ref[chunk * x + i].astype(f32)
        sums.append(acc)
    everything = functools.reduce(jnp.add, sums)
    shared = scalar_ref[GROUPS + 5] > 0
    for x in range(GROUPS):
        tail = jnp.where(shared, everything[:, lanes:], sums[x][:, lanes:])
        block = jnp.concatenate([everything[:, :lanes], tail], axis=1).astype(bf)
        for i in range(chunk):
            out_ref[chunk * x + i] = block


def sum_space(scalar, got):
    return call(sum_space_kernel, "sum_space", scalar, [got], [sds(got.shape, bf)])[0]


def finish_kernel(
    scalar_ref,
    part_ref,
    r3,
    r1,
    r2,
    start_ref,
    gmid_ref,
    rows_ref,
    unseen_ref,
    bq_ref,
    bv_ref,
    feed_ref,
    bup_ref,
    kept_ref,
    sent_ref,
    low_ref,
):
    rows, width = start_ref.shape
    first_grad = part_ref[...] + r3[...].astype(f32) + r1[...].astype(f32) + r2[...].astype(f32)
    n, inverse = norm_parts(start_ref[...])
    grad = gmid_ref[...] + norm_pull(first_grad, n, inverse, rows_ref[1:2])
    low_ref[...] = grad.astype(bf)
    half = rows // 2
    first = scalar_ref[GROUPS + 4] == 0
    top, low = grad[:half], grad[half:]
    lines = [
        column_sum(unseen_ref[:, :1] * grad),
        column_sum(first_grad * n),
        column_sum(first_grad),
        bq_ref[...],
        bv_ref[...],
        feed_ref[:4],
    ]
    blocks = bup_ref.shape[1] // width
    lines += [bup_ref[:, width * i : width * (i + 1)] for i in range(blocks)]
    spare = 16 - sum(a.shape[0] for a in lines)
    lines = jnp.concatenate(lines + [jnp.zeros((spare, width), f32)], axis=0)

    def narrow(values):
        cut = [a[:, 128 * i : 128 * (i + 1)] for a in (values, lines) for i in range(width // 128)]
        cut.append(jnp.zeros((kept_ref.shape[0] * kept_ref.shape[1] - sum(a.shape[0] for a in cut), 128), f32))
        return jnp.concatenate(cut, axis=0).reshape(kept_ref.shape).astype(bf)

    kept_ref[...] = narrow(jnp.where(first, top, low))
    sent_ref[...] = narrow(jnp.where(first, low, top))


def finish(scalar, part, received, start, gmid, vectors, unseen, bq, bv, feed_vec, grad_b_up):
    rows, width = start.shape
    tail = sds((GROUPS * SPREAD, 16, 128), bf)
    return call(
        finish_kernel,
        "finish",
        scalar,
        [part, *received, start, gmid, vectors, unseen, bq, bv, feed_vec, grad_b_up],
        [tail, tail, sds((rows, width), bf)],
    )


def share_kernel(scalar_ref, low_ref, *refs):
    id_refs, outs, (share_ref, sem) = refs[:GROUPS], refs[GROUPS : 2 * GROUPS], refs[2 * GROUPS :]
    rows = low_ref.shape[0]
    piece = id_refs[0].shape[1]
    slot = lax.broadcasted_iota(jnp.int32, (rows, piece), 0) + scalar_ref[GROUPS]
    for i, id_ref in enumerate(id_refs):
        hot = (slot == id_ref[...]).astype(bf)
        share_ref[i] = dg(hot, low_ref[...], TN).astype(bf)
    copies = [pltpu.make_async_copy(share_ref.at[i], out, sem.at[i]) for i, out in enumerate(outs)]
    for copy in copies:
        copy.start()
    for copy in copies:
        copy.wait()


def share(scalar, low, ids):
    shape = (ids[0].shape[1], low.shape[1])
    inside = pl.BlockSpec(memory_space=pltpu.VMEM)
    return pl.pallas_call(
        share_kernel,
        in_specs=[pl.BlockSpec(memory_space=pltpu.SMEM)] + [inside] * (1 + GROUPS),
        out_specs=[pl.BlockSpec(memory_space=pltpu.HBM)] * GROUPS,
        out_shape=[sds(shape, bf)] * GROUPS,
        scratch_shapes=[pltpu.VMEM((GROUPS,) + shape, bf), pltpu.SemaphoreType.DMA((GROUPS,))],
        compiler_params=pltpu.CompilerParams(vmem_limit_bytes=11 * 1024 * 1024),
        cost_estimate=pl.CostEstimate(flops=1000, bytes_accessed=1000, transcendentals=0),
        name="share",
    )(scalar, low, *ids)


def unpack_feed_kernel(scalar_ref, *refs):
    *sources, down_ref, up_ref, out_ref = refs
    mine, other = sources[:GROUPS], sources[GROUPS:]
    first = scalar_ref[GROUPS + 4] == 0
    lines = down_ref.shape[0] // GROUPS
    half = out_ref.shape[0] // 2
    extra = half // SPREAD

    def unpack(g):
        z_low, z_high = scalar_ref[GROUPS + 12 + g], scalar_ref[GROUPS + 8 + g]
        for k, far in enumerate(RELATIVE):
            low = jnp.where(first, mine[k][g], other[k][g]).astype(f32)
            high = jnp.where(first, other[g][k], mine[g][k]).astype(f32)
            y_low, y_high = turn(scalar_ref[GROUPS + 6], far), turn(scalar_ref[GROUPS + 12], far)
            down_ref[pl.ds(pl.multiple_of(lines * y_low, 16), lines), :] = low[:lines]
            up_ref[pl.ds(pl.multiple_of(lines * y_high, 16), lines), :] = high[:lines]
            at = extra * (GROUPS * z_low + y_low)
            out_ref[pl.ds(pl.multiple_of(at, 16), extra), :] = low[lines:]
            at = half + extra * (GROUPS * z_high + y_high)
            out_ref[pl.ds(pl.multiple_of(at, 16), extra), :] = high[lines:]

    for g in range(GROUPS):
        pl.when(pl.program_id(0) == g)(functools.partial(unpack, g))


def unpack_feed(scalar, mine, other, width, hidden):
    block = pl.BlockSpec(mine[0].shape, lambda g, s: (0, 0, 0))
    return grid_call(
        unpack_feed_kernel,
        "unpack_feed",
        scalar,
        GROUPS,
        [block] * (2 * GROUPS),
        [
            pl.BlockSpec((width, width), lambda g, s: (s[GROUPS + 12 + g], 0)),
            pl.BlockSpec((width, width), lambda g, s: (0, s[GROUPS + 8 + g])),
            pl.BlockSpec((width, width), lambda g, s: (0, 0)),
        ],
        [sds((hidden, width), f32), sds((width, hidden), f32), sds((width, width), f32)],
        [*mine, *other],
    )


def unpack_rest_kernel(scalar_ref, mine_ref, other_ref, out_ref, pos_ref, *vec_refs):
    core = scalar_ref[GROUPS + 4]
    half = out_ref.shape[0] // 2
    width = out_ref.shape[1] // 3
    rows = pos_ref.shape[0] // 2
    chunk = mine_ref.shape[0] // GROUPS
    for kept, ref in ((core, mine_ref), (1 - core, other_ref)):
        lines = pl.ds(pl.multiple_of(kept * half, half), half)
        for j in range(GROUPS):
            for w in range(3):
                lanes = slice(w * width + 128 * j, w * width + 128 * (j + 1))
                block = ref[chunk * j : chunk * (j + 1), :, 128 * w : 128 * (w + 1)]
                out_ref[lines, lanes] = block.reshape(half, 128).astype(f32)
        tail = ref[:, :, 3 * 128 :].astype(f32).reshape(-1, 128)
        lines = pl.ds(pl.multiple_of(kept * rows, 8), rows)
        blocks = width // 128
        for i in range(blocks):
            pos_ref[lines, 128 * i : 128 * (i + 1)] = tail[rows * i : rows * (i + 1)]
            if ref is mine_ref:
                base = rows * blocks + 16 * i
                for n, vec_ref in enumerate(vec_refs):
                    for line in range(vec_ref.shape[1] // width):
                        lanes = slice(width * line + 128 * i, width * line + 128 * (i + 1))
                        vec_ref[:, lanes] = tail[base + n + line : base + n + line + 1]


def unpack_rest(scalar, mine, other, rows, width, hidden):
    return call(
        unpack_rest_kernel,
        "unpack_rest",
        scalar,
        [mine, other],
        [sds((width, 3 * width), f32), sds((rows, width), f32)]
        + [sds((1, width), f32)] * 9
        + [sds((1, hidden), f32)],
    )


def shift(array, axis, step):
    size = lax.axis_size(axis)
    return lax.ppermute(array, axis, [(i, (i + step) % size) for i in range(size)])


def peers(array, axis):
    return [shift(array, axis, step) for step in (1, 3, 2)]


def swap(array):
    return shift(array, "core", 1)


def total(parts):
    return functools.reduce(jnp.add, [p.astype(f32) for p in parts])


SPACE = ("x", "z", "y")
PLANE = ("z", "y", "core")


def step_plane(array, step, near):
    sizes = [lax.axis_size(name) for name in PLANE]
    pairs = []
    for z in range(sizes[0]):
        for y in range(sizes[1]):
            for core in range(sizes[2]):
                if (core == 0) == near:
                    target = (z, (y + step) % sizes[1], core)
                else:
                    target = ((z + step) % sizes[0], y, core)
                index = lambda p: (p[0] * sizes[1] + p[1]) * sizes[2] + p[2]
                pairs.append((index((z, y, core)), index(target)))
    return lax.ppermute(array, PLANE, pairs)


def step_cores(array):
    size = lax.axis_size("x")
    pairs = []
    for core in range(2):
        for x in range(size):
            pairs.append((core * size + x, core * size + (x + 1 - 2 * core) % size))
    return lax.ppermute(array, ("core", "x"), pairs)


def plane_peers(array, near):
    return [step_plane(array, step, near) for step in (1, 3, 2)]


def exchange(array, axes):
    return lax.all_to_all(array, axes, 0, 0, tiled=True)


def body(
    vis,
    keep_slots,
    counts,
    band_mask,
    mask_token,
    pos,
    ln1_gain,
    ln1_bias,
    w_qkv,
    b_query,
    b_value,
    w_out,
    b_out,
    ln2_gain,
    ln2_bias,
    w_up,
    b_up,
    w_down,
    b_down,
    d_out,
):
    barrier = lax.optimization_barrier
    x = lax.axis_index("x")
    core = lax.axis_index("core")
    piece = keep_slots.shape[1]
    rows, width = pos.shape
    half = rows // 2
    hidden = w_up.shape[1]

    vis = vis[0]

    y, z = lax.axis_index("y"), lax.axis_index("z")
    relative = jnp.array(RELATIVE, jnp.int32)
    order = (x + relative) % GROUPS
    live = jnp.sum(jnp.where(order[:, None] == jnp.arange(GROUPS)[None, :], band_mask, 0), axis=1)
    here = (x * lax.axis_size("z") + z) * lax.axis_size("y") + y
    chunks = width // 128 * half // 16
    shared = (here >= chunks) & (here < chunks + width // 128)
    scalar = jnp.concatenate(
        [live, order * rows, jnp.stack([core, shared.astype(jnp.int32), y, z]), (z + relative) % GROUPS, order]
    ).astype(jnp.int32)
    pack = lambda *vs: jnp.pad(jnp.stack(vs), ((0, 8 - len(vs)), (0, 0)))
    vectors = pack(mask_token, ln1_gain, ln1_bias, b_query, b_value)
    feed_vectors = pack(b_out, ln2_gain, ln2_bias, b_down)

    index = lax.broadcasted_iota(jnp.int32, (1, piece), 1)
    code = jnp.where(index < counts, keep_slots, -1) + 1
    marks = jnp.concatenate([code // 64, code % 64], axis=0).astype(bf)
    marks = jnp.pad(marks, ((0, MARKS - 2), (0, width - piece)))
    message = jnp.concatenate([marks, vis], axis=0)
    pieces = [message] + peers(message, "x")
    pos_half = lax.dynamic_slice(pos, (half * core, 0), (half, width))
    pos_mine = [step_cores(pos), shift(pos_half, "x", 2)]
    scalar, vectors, feed_vectors, pieces = barrier((scalar, vectors, feed_vectors, pieces))
    start, normed, unseen, *bases = front(scalar, pieces, pos, vectors, piece)
    bases, ids = bases[: GROUPS - 1], bases[GROUPS - 1 :]
    q, turned_own, k_own, v_own, *state, p_own = attention_own(scalar, normed, vectors, w_qkv)
    state, pos_mine = barrier((state, pos_mine))
    pos_other = [swap(p) for p in pos_mine]
    out = middle(scalar, bases, pos_mine + pos_other, vectors, w_qkv, q, state)
    rest, (mixed, lse), kept = out[: 3 * (GROUPS - 1)], out[3 * (GROUPS - 1) :][:2], out[3 * (GROUPS - 1) + 2 :]
    keys, values = [k_own, *rest[1::3]], [v_own, *rest[2::3]]
    weights, peaks = [p_own, *kept[0::2]], [state[0], *kept[1::2]]

    out, middle_rows, second, kept, sent, grad_b_up = feed_forward(
        scalar, mixed, start, d_out[0], w_out, feed_vectors, w_up, b_up[None], w_down
    )
    got = swap(sent)
    grad_middle, out_kept, out_sent, feed_vec, *factors = feed_backward(
        scalar, mixed, middle_rows, second, d_out[0], w_out, feed_vectors, lse, peaks
    )
    inputs = list(zip(factors[:GROUPS], weights, keys, values, factors[GROUPS:]))
    feed = fold_feed(scalar, kept, got, out_kept, swap(out_sent))
    q, feed = barrier((q, feed))
    feed = [feed[0]] + [step_plane(feed[r], r, True) for r in (1, 2, 3)]
    dq, d_3, part = attention_grad(scalar, (3,), q, w_qkv, [inputs[3]], None)
    dq, part = barrier((dq, part))
    from_3 = shift(part, "x", 2)
    dq, d_1, part = attention_grad(scalar, (1,), q, w_qkv, [inputs[1]], dq)
    feed = fold_line(scalar, feed)
    dq, part, feed = barrier((dq, part, feed))
    feed = [feed[0]] + [shift(feed[r], "x", r) for r in (1, 2, 3)]
    from_1 = shift(part, "x", 3)
    dq, d_2, part = attention_grad(scalar, (2,), q, w_qkv, [inputs[2]], dq)
    feed = add_up(scalar, "fold_point", feed)
    dq, part, from_3, feed = barrier((dq, part, from_3, feed))
    feed_peers = plane_peers(feed, False)
    from_2 = shift(part, "x", 1)
    part, at_kept, at_sent, grad_b_query, grad_b_value = attention_grad(
        scalar, (0,), q, w_qkv, [inputs[0]], dq, [turned_own, *rest[0::3], d_3, d_1, d_2]
    )
    at_kept, at_sent, part, from_1, from_2, feed_peers = barrier(
        (at_kept, at_sent, part, from_1, from_2, feed_peers)
    )

    at_got = swap(at_sent)
    feed = add_up(scalar, "sum_line", [feed] + feed_peers)
    gathered = peers(feed, "x")
    tail_kept, tail_sent, low = finish(
        scalar,
        part,
        (from_3, from_1, from_2),
        start,
        grad_middle,
        vectors,
        unseen,
        grad_b_query,
        grad_b_value,
        feed_vec,
        grad_b_up,
    )
    spread = lambda a: a.reshape(GROUPS * SPREAD, 16, -1)
    bundle = fold_rest(scalar, spread(at_kept), spread(at_got), tail_kept, swap(tail_sent))
    bundle, feed = barrier((bundle, [feed] + gathered))
    bundle = exchange(bundle, SPACE)
    feed = jnp.stack(feed)
    feed = [feed] + plane_peers(feed, True)
    bundle, shares = barrier((bundle, share(scalar, low, ids)))
    bundle = sum_space(scalar, bundle)
    feed, _ = barrier((feed, bundle))
    rest_mine = exchange(bundle, SPACE)
    feed_other = [swap(a) for a in feed]
    feed_other, shares = barrier((feed_other, shares))
    returned = [shares[0], shift(shares[1], "x", 3), shift(shares[2], "x", 1), shift(shares[3], "x", 2)]
    grad_w_down, grad_w_up, grad_w_out = unpack_feed(scalar, feed, feed_other, width, hidden)
    rest_mine, grad_w_down, returned = barrier((rest_mine, grad_w_down, returned))
    rest_other = swap(rest_mine)
    grad_vis = total(returned).astype(bf)
    grad_w_qkv, grad_pos, *sums = unpack_rest(scalar, rest_mine, rest_other, rows, width, hidden)
    sums = [a[0] for a in sums]

    return (
        out[None],
        grad_vis[None],
        sums[0],
        grad_pos,
        sums[1],
        sums[2],
        grad_w_qkv,
        sums[3],
        sums[4],
        grad_w_out,
        sums[5],
        sums[6],
        sums[7],
        grad_w_up,
        sums[9],
        grad_w_down,
        sums[8],
    )


CUBE = ("z", "y", "core")


def solution(mesh):
    fine = Mesh(mesh.devices.reshape(4, 4, 2, 4), ("z", "y", "core", "x"))
    return jax.shard_map(
        body,
        mesh=fine,
        in_specs=(
            P(CUBE, "x", None),
            P(CUBE, "x"),
            P(CUBE, "x"),
            P(CUBE, None),
            P(),
            P("x", None),
        )
        + (P(),) * 13
        + (P(CUBE, "x", None),),
        out_specs=(P(CUBE, "x", None), P(CUBE, "x", None), P(), P("x", None)) + (P(),) * 13,
        check_vma=False,
    )
```

```python
import functools

import jax
import jax.numpy as jnp
from jax import lax
from jax.experimental import pallas as pl
from jax.experimental.pallas import tpu as pltpu
from jax.sharding import Mesh, PartitionSpec as P

bf = jnp.bfloat16
f32 = jnp.float32

HEADS = 16
DEPTH = 32
QUAD = 4
GROUPS = 4
LOG2E = 1.4426950408889634
SCALE = DEPTH**-0.5
EPS = 1e-05
BIG = 1e30
GELU_SCALE = 0.7978845608028654
GELU_CUBE = 0.044715
RELATIVE = (0, 3, 1, 2)
CAP = 80
MARKS = 16
SPREAD = 16

NT = (((1,), (1,)), ((), ()))
NN = (((1,), (0,)), ((), ()))
TN = (((0,), (0,)), ((), ()))
VMEM_LIMIT = 56 * 1024 * 1024


def dg(a, b, dims):
    return lax.dot_general(a, b, dims, preferred_element_type=f32)


def sds(shape, dtype):
    return jax.ShapeDtypeStruct(shape, dtype)


def call(kernel, name, scalar, operands, out_shape, scratch=(), aliases=None, limit=11, micro=0.001):
    inside = pl.BlockSpec(memory_space=pltpu.VMEM)
    return pl.pallas_call(
        kernel,
        in_specs=[pl.BlockSpec(memory_space=pltpu.SMEM)] + [inside] * len(operands),
        out_specs=[inside] * len(out_shape),
        out_shape=out_shape,
        scratch_shapes=list(scratch),
        compiler_params=pltpu.CompilerParams(vmem_limit_bytes=limit * 1024 * 1024),
        cost_estimate=pl.CostEstimate(flops=int(micro * 1e9), bytes_accessed=1000, transcendentals=0),
        input_output_aliases=aliases or {},
        name=name,
    )(scalar, *operands)


def grid_call(kernel, name, scalar, steps, in_specs, out_specs, out_shape, operands):
    return pl.pallas_call(
        kernel,
        grid_spec=pltpu.PrefetchScalarGridSpec(
            num_scalar_prefetch=1, grid=(steps,), in_specs=in_specs, out_specs=out_specs
        ),
        out_shape=out_shape,
        compiler_params=pltpu.CompilerParams(vmem_limit_bytes=32 * 1024 * 1024),
        cost_estimate=pl.CostEstimate(flops=1000, bytes_accessed=1000, transcendentals=0),
        name=name,
    )(scalar, *operands)


def column_sum(tensor):
    return jnp.sum(tensor.astype(f32), axis=0, keepdims=True)


def norm_parts(values):
    centered = values - jnp.mean(values, axis=-1, keepdims=True)
    variance = jnp.mean(centered * centered, axis=-1, keepdims=True)
    inverse = lax.rsqrt(variance + EPS)
    return centered * inverse, inverse


def norm_pull(grad, n, inverse, gain):
    g = grad * gain
    return inverse * (
        g - jnp.mean(g, axis=-1, keepdims=True) - n * jnp.mean(g * n, axis=-1, keepdims=True)
    )


def place_rows(base, pieces, ids, rows, rows_ref):
    piece, width = ids[0].shape[1], rows_ref.shape[1]
    slot = lax.broadcasted_iota(jnp.int32, (rows, piece), 0) + base
    placed = jnp.zeros((rows, width), f32)
    seen = jnp.zeros((rows, 1), f32)
    for v, i in zip(pieces, ids):
        hot = (slot == i[...]).astype(f32)
        seen += jnp.sum(hot, axis=1, keepdims=True)
        placed += dg(hot.astype(bf), v[MARKS : MARKS + piece, :], NN)
    unseen = 1.0 - seen
    return placed + unseen * rows_ref[0:1], unseen


def first_norm(start, rows_ref):
    n, _ = norm_parts(start)
    return (n * rows_ref[1:2] + rows_ref[2:3]).astype(bf)


def keys_values(normed, rows_ref, w_ref, turned_ref, k_ref, v_ref):
    width = normed.shape[1]
    k_ref[...] = dg(normed, w_ref[:, width : 2 * width], NN).astype(bf)
    v_ref[...] = (dg(normed, w_ref[:, 2 * width :], NN) + rows_ref[4:5]).astype(bf)
    turned_ref[...] = normed.T


def stack_heads(x):
    lane = lax.broadcasted_iota(jnp.int32, x.shape, 1) // DEPTH
    return jnp.concatenate([jnp.where(lane == h, x, jnp.zeros_like(x)) for h in range(QUAD)], axis=0)


def unstack_heads(xt):
    rows = xt.shape[1] // QUAD
    parts = [xt[DEPTH * h : DEPTH * (h + 1), rows * h : rows * (h + 1)] for h in range(QUAD)]
    return jnp.concatenate(parts, axis=0).T


def fwd_steps(steps, scalar_ref, query, key, value, state, keep_weights, finish):
    stacked = {}

    def scores(quad, group):
        if quad not in stacked:
            stacked[quad] = stack_heads(query(quad))
        return dg(key(quad, group), stacked[quad], NT)

    ahead = scores(*steps[0])
    for i, (quad, group) in enumerate(steps):
        s = ahead
        if i + 1 < len(steps):
            ahead = scores(*steps[i + 1])
        live = scalar_ref[group] > 0
        peak = jnp.where(live, jnp.max(s, axis=0, keepdims=True), -BIG)
        old = state(quad) if i == 0 or steps[i - 1][0] != quad else new
        if old is not None:
            peak = jnp.maximum(old[0], peak)
        p = jnp.exp2(s - jnp.where(live, peak, BIG)).astype(bf)
        keep_weights(quad, group, p, peak)
        v = value(quad, group)
        turned = jnp.concatenate([v.T, jnp.ones((16, v.shape[0]), bf)], axis=0)
        both = dg(turned, p, NN)
        o, l = both[: v.shape[1]], both[v.shape[1] : v.shape[1] + 1]
        if old is not None:
            keep = jnp.exp2(old[0] - peak)
            o += old[2] * keep
            l += old[1] * keep
        new = (peak, l, o)
        if i + 1 == len(steps) or steps[i + 1][0] != quad:
            finish(quad, new)


def quad_at(quad):
    return (slice(None), slice(128 * quad, 128 * (quad + 1)))


def front_kernel(scalar_ref, *refs):
    pieces, (pos_ref, rows_ref), refs = refs[:GROUPS], refs[GROUPS : GROUPS + 2], refs[GROUPS + 2 :]
    start_ref, normed_ref, unseen_ref, *refs = refs
    rests, ids = refs[: GROUPS - 1], refs[GROUPS - 1 :]
    rows = pos_ref.shape[0]
    piece = ids[0].shape[1]
    for v, i in zip(pieces, ids):
        marks = v[:MARKS, :].astype(f32)[:8, :piece]
        i[...] = (marks[0:1] * 64.0 + marks[1:2]).astype(jnp.int32) - 1
    start, unseen = place_rows(scalar_ref[GROUPS], pieces, ids, rows, rows_ref)
    start += pos_ref[...].astype(f32)
    start_ref[...] = start
    unseen_ref[...] = jnp.broadcast_to(unseen, unseen_ref.shape)
    normed_ref[...] = first_norm(start, rows_ref)
    for g, rest in enumerate(rests):
        rest[...], _ = place_rows(scalar_ref[GROUPS + 1 + g], pieces, ids, rows, rows_ref)


def front(scalar, pieces, pos, vectors, piece):
    rows, width = pos.shape
    return call(
        front_kernel,
        "front",
        scalar,
        [*pieces, pos, vectors],
        [sds((rows, width), f32), sds((rows, width), bf), sds((rows, 128), f32)]
        + [sds((rows, width), f32)] * (GROUPS - 1)
        + [sds((1, piece), jnp.int32)] * GROUPS,
        micro=4,
    )


def attention_own_kernel(
    scalar_ref, normed_ref, rows_ref, w_ref, q_ref, turned_ref, k_ref, v_ref, m_ref, l_ref, o_ref, p_ref
):
    normed = normed_ref[...]
    width = normed.shape[1]
    q_ref[...] = ((dg(normed, w_ref[:, :width], NN) + rows_ref[3:4]) * (SCALE * LOG2E)).astype(bf)
    keys_values(normed, rows_ref, w_ref, turned_ref, k_ref, v_ref)

    def keep_weights(quad, group, p, peak):
        p_ref[quad] = p

    def finish(quad, state):
        m_ref[quad], l_ref[quad], o_ref[quad] = state

    fwd_steps(
        [(quad, 0) for quad in range(m_ref.shape[0])],
        scalar_ref,
        lambda quad: q_ref[quad_at(quad)],
        lambda quad, group: k_ref[quad_at(quad)],
        lambda quad, group: v_ref[quad_at(quad)],
        lambda quad: None,
        keep_weights,
        finish,
    )


def attention_own(scalar, normed, vectors, w_qkv):
    rows, width = normed.shape
    quads, n = width // 128, rows * QUAD
    return call(
        attention_own_kernel,
        "attention_own",
        scalar,
        [normed, vectors, w_qkv],
        [
            sds((rows, width), bf),
            sds((width, rows), bf),
            sds((rows, width), bf),
            sds((rows, width), bf),
            sds((quads, 1, n), f32),
            sds((quads, 1, n), f32),
            sds((quads, 128, n), f32),
            sds((quads, rows, n), bf),
        ],
        micro=5,
    )


def middle_kernel(scalar_ref, *refs):
    bases, refs = refs[: GROUPS - 1], refs[GROUPS - 1 :]
    pos_refs, refs = refs[:4], refs[4:]
    rows_ref, w_ref, q_ref, m_ref, l_ref, o_ref, *refs = refs
    groups, (mixed_ref, lse_ref), kept = refs[: 3 * (GROUPS - 1)], refs[3 * (GROUPS - 1) :][:2], refs[3 * (GROUPS - 1) + 2 :]
    first = scalar_ref[GROUPS + GROUPS] == 0
    near, far, other_near, other_far = [ref[...].astype(f32) for ref in pos_refs]
    for g, base in enumerate(bases):
        if g < 2:
            pos = jnp.where(first == (g == 0), near, other_near)
        else:
            pos = jnp.concatenate([jnp.where(first, far, other_far), jnp.where(first, other_far, far)], axis=0)
        keys_values(first_norm(base[...] + pos, rows_ref), rows_ref, w_ref, *groups[3 * g : 3 * g + 3])

    def keep_weights(quad, group, p, peak):
        kept[2 * group - 2][quad] = p
        kept[2 * group - 1][quad] = peak

    def finish(quad, state):
        m, l, o = state
        mixed_ref[quad_at(quad)] = unstack_heads(o / l).astype(bf)
        lse_ref[quad] = m + jnp.log2(l)

    fwd_steps(
        [(quad, group) for quad in range(m_ref.shape[0]) for group in range(1, GROUPS)],
        scalar_ref,
        lambda quad: q_ref[quad_at(quad)],
        lambda quad, group: groups[3 * group - 2][quad_at(quad)],
        lambda quad, group: groups[3 * group - 1][quad_at(quad)],
        lambda quad: (m_ref[quad], l_ref[quad], o_ref[quad]),
        keep_weights,
        finish,
    )


def middle(scalar, bases, pos, vectors, w_qkv, q, state):
    rows, width = q.shape
    quads, n = width // 128, rows * QUAD
    group = [sds((width, rows), bf), sds((rows, width), bf), sds((rows, width), bf)]
    return call(
        middle_kernel,
        "middle",
        scalar,
        [*bases, *pos, vectors, w_qkv, q, *state],
        [*(group * (GROUPS - 1)), sds((rows, width), bf), sds((quads, 1, n), f32)]
        + [sds((quads, rows, n), bf), sds((quads, 1, n), f32)] * (GROUPS - 1),
    )


def bwd_kernel(scalar_ref, q_ref, w_ref, *refs, groups, carried):
    width = q_ref.shape[1]
    inputs, refs = [refs[5 * i : 5 * i + 5] for i in range(len(groups))], refs[5 * len(groups) :]
    if carried:
        dq_in, *refs = refs
    own = groups == (0,)
    if own:
        *turned_refs, d_3, d_1, d_2, part_ref, kept_ref, sent_ref, bq_ref, bv_ref, d_s = refs
        base, outs = width, [(d_s, part_ref)]
    else:
        dq_ref, *refs = refs
        base, outs = 0, [refs[2 * i : 2 * i + 2] for i in range(len(groups))]
    quads = width // 128
    for j in range(quads):
        at = quad_at(j)
        qs = stack_heads(q_ref[at])
        dq = dq_in[at] if carried else None
        for (do_ref, p_ref, k_ref, v_ref, delta_ref), (d_ref, _) in zip(inputs, outs):
            columns = lambda i: (
                slice(None),
                slice(base + (i - 1) * width + 128 * j, base + (i - 1) * width + 128 * (j + 1)),
            )
            dos = stack_heads(do_ref[at])
            k, p = k_ref[at], p_ref[j]
            ds = (p.astype(f32) * (dg(v_ref[at], dos, NT) - delta_ref[j])).astype(bf)
            d_ref[columns(2)] = dg(p, dos, NN).astype(bf)
            d_ref[columns(1)] = (dg(ds, qs, NN) * (1.0 / LOG2E)).astype(bf)
            term = unstack_heads(dg(k, ds, TN))
            dq = term if dq is None else dq + term
        if own:
            d_s[at] = (dq * SCALE).astype(bf)
        else:
            dq_ref[at] = dq
    for d_ref, part_ref in outs:
        grads = d_ref[...]
        part_ref[...] = dg(grads, w_ref[...] if own else w_ref[:, width:], NT).astype(part_ref.dtype)
    if not own:
        return
    own, *rest = turned_refs
    g = dg(own[...], grads[:, width:], NN)
    bv = column_sum(grads[:, 2 * width :])
    for turned, d_ref in zip(rest, (d_1, d_2, d_3)):
        d = d_ref[...]
        g += dg(turned[...], d, NN)
        bv += column_sum(d[:, width:])
    bv_ref[...] = bv
    bq_ref[...] = column_sum(grads[:, :width])
    gq = dg(own[...], grads[:, :width], NN)
    first = scalar_ref[GROUPS + 4] == 0
    half = width // 2
    for j in range(quads):
        at = slice(128 * j, 128 * (j + 1))
        block = jnp.concatenate([gq[:, at], g[:, at], g[:, width + 128 * j : width + 128 * (j + 1)]], axis=1)
        kept_ref[j] = jnp.where(first, block[:half], block[half:]).astype(bf)
        sent_ref[j] = jnp.where(first, block[half:], block[:half]).astype(bf)


def attention_grad(scalar, groups, q, w_qkv, inputs, dq, more=()):
    rows, width = q.shape
    quads = width // 128
    operands = [q, w_qkv] + [a for group in inputs for a in group]
    aliases = {}
    if dq is not None:
        aliases = {len(operands) + 1: 0}
        operands.append(dq)
    operands += list(more)
    scratch = []
    if groups == (0,):
        packed = (quads, width // 2, 3 * 128)
        out_shape = [sds((rows, width), f32)] + [sds(packed, bf)] * 2 + [sds((1, width), f32)] * 2
        scratch = [pltpu.VMEM((rows, 3 * width), bf)]
    else:
        out_shape = [sds((rows, width), f32)]
        out_shape += [sds((rows, 2 * width), bf), sds((rows, width), bf)] * len(groups)
    return call(
        functools.partial(bwd_kernel, groups=groups, carried=dq is not None),
        "attention_grad_" + "_".join(str(g) for g in groups),
        scalar,
        operands,
        out_shape,
        scratch,
        aliases,
    )


def feed_kernel(
    scalar_ref,
    mixed_ref,
    start_ref,
    dout_ref,
    wout_ref,
    rows_ref,
    wup_ref,
    bup_ref,
    wdown_ref,
    out_ref,
    middle_ref,
    second_ref,
    kept_ref,
    sent_ref,
    gbup_ref,
):
    first = scalar_ref[GROUPS + 4] == 0
    width = mixed_ref.shape[1]
    hidden = wup_ref.shape[1]
    dout = dout_ref[...]
    middle = start_ref[...] + (dg(mixed_ref[...], wout_ref[...], NN) + rows_ref[0:1])
    middle_ref[...] = middle
    n, _ = norm_parts(middle)
    normed = (n * rows_ref[1:2] + rows_ref[2:3]).astype(bf)
    turned = normed.T
    result = middle + rows_ref[3:4]
    second = jnp.zeros_like(middle)
    lines = hidden // SPREAD
    for h in range(hidden // width):
        at = slice(width * h, width * (h + 1))
        u = dg(normed, wup_ref[:, at], NN) + bup_ref[:, at]
        square = u * u
        t = jnp.tanh(u * (GELU_SCALE + (GELU_SCALE * GELU_CUBE) * square))
        near = 0.5 + 0.5 * t
        act = (u * near).astype(bf)
        result += dg(act, wdown_ref[at, :], NN)
        slope = near + u * (0.5 - 0.5 * (t * t)) * (GELU_SCALE + (3.0 * GELU_SCALE * GELU_CUBE) * square)
        gup = (dg(dout, wdown_ref[at, :], NT) * slope).astype(bf)
        second += dg(gup, wup_ref[:, at], NT)
        gbup_ref[:, at] = column_sum(gup)
        down = dg(act, dout, TN).astype(bf)
        up = dg(turned, gup, NN).astype(bf)
        chunks = (width // lines, lines, width)
        places = slice(h * chunks[0], (h + 1) * chunks[0])
        kept_ref[places] = jnp.where(first, down, up).reshape(chunks)
        sent_ref[places] = jnp.where(first, up, down).reshape(chunks)
    out_ref[...] = result.astype(bf)
    second_ref[...] = second


def feed_backward_kernel(
    scalar_ref,
    mixed_ref,
    middle_ref,
    second_ref,
    dout_ref,
    wout_ref,
    rows_ref,
    lse_ref,
    *refs,
):
    peaks, (gmid_ref, kept_ref, sent_ref, vec_ref), outs = refs[:GROUPS], refs[GROUPS : GROUPS + 4], refs[GROUPS + 4 :]
    first = scalar_ref[GROUPS + 4] == 0
    mixed = mixed_ref[...]
    width = mixed.shape[1]
    second = second_ref[...]
    grad = dout_ref[...].astype(f32)
    n, inverse = norm_parts(middle_ref[...])
    gmid = grad + norm_pull(second, n, inverse, rows_ref[1:2])
    gmid_ref[...] = gmid
    branch = gmid.astype(bf)
    gmix = dg(branch, wout_ref[...], NT).astype(bf).astype(f32)
    wout = dg(mixed, branch, TN)
    half = width // 2
    extra = (SPREAD, half // SPREAD, width)
    kept_ref[...] = jnp.where(first, wout[:half], wout[half:]).astype(bf).reshape(extra)
    sent_ref[...] = jnp.where(first, wout[half:], wout[:half]).astype(bf).reshape(extra)
    vec_ref[...] = jnp.concatenate(
        [
            column_sum(branch),
            column_sum(second * n),
            column_sum(second),
            column_sum(grad),
            jnp.zeros((4, width), f32),
        ],
        axis=0,
    )
    product = mixed.astype(f32) * gmix
    head = lax.broadcasted_iota(jnp.int32, (HEADS, width), 0)
    lane = lax.broadcasted_iota(jnp.int32, (HEADS, width), 1) // DEPTH
    pick = (head == lane).astype(bf)
    halves = lambda a: (a.astype(bf), (a - a.astype(bf).astype(f32)).astype(bf))
    high, low = halves(product)
    delta = dg(pick, high, NT) + dg(pick, low, NT)
    rows = delta.shape[1]
    for peak_ref, do_ref, delta_ref in zip(peaks, outs[:GROUPS], outs[GROUPS:]):
        lines = []
        for j in range(HEADS // QUAD):
            factor = jnp.exp2(peak_ref[j] - lse_ref[j])
            delta_ref[j] = factor * jnp.concatenate([delta[QUAD * j + i : QUAD * j + i + 1] for i in range(QUAD)], axis=1)
            lines += [factor[:, rows * i : rows * (i + 1)] for i in range(QUAD)]
        high, low = halves(jnp.concatenate(lines, axis=0))
        do_ref[...] = (gmix * (dg(high, pick, TN) + dg(low, pick, TN))).astype(bf)


def feed_forward(scalar, mixed, start, d_out, w_out, vectors, w_up, b_up, w_down):
    rows, width = mixed.shape
    hidden = w_up.shape[1]
    packed = (SPREAD, hidden // SPREAD, width)
    return call(
        feed_kernel,
        "feed_forward",
        scalar,
        [mixed, start, d_out, w_out, vectors, w_up, b_up, w_down],
        [sds((rows, width), bf)] + [sds((rows, width), f32)] * 2 + [sds(packed, bf)] * 2 + [sds((1, hidden), f32)],
    )


def feed_backward(scalar, mixed, middle, second, d_out, w_out, vectors, lse, peaks):
    rows, width = mixed.shape
    packed = (SPREAD, width // 2 // SPREAD, width)
    return call(
        feed_backward_kernel,
        "feed_backward",
        scalar,
        [mixed, middle, second, d_out, w_out, vectors, lse, *peaks],
        [sds((rows, width), f32), sds(packed, bf), sds(packed, bf), sds((8, width), f32)]
        + [sds((rows, width), bf)] * GROUPS
        + [sds(lse.shape, f32)] * GROUPS,
    )


def turn(place, steps):
    return lax.rem(place + steps, GROUPS)


def fold_feed_kernel(scalar_ref, a, b, c, d, *outs):
    first, y, z = scalar_ref[GROUPS + 4] == 0, scalar_ref[GROUPS + 6], scalar_ref[GROUPS + 7]
    near = jnp.where(first, y, z)
    lines = a.shape[1]
    for r, out_ref in enumerate(outs):
        place = turn(near, r)
        for i in range(GROUPS):
            at = jnp.where(first, GROUPS * i + place, GROUPS * place + i)
            out_ref[i, :lines] = a[at] + b[at]
            out_ref[i, lines:] = c[at] + d[at]


def fold_feed(scalar, a, b, c, d):
    shape = sds((GROUPS, a.shape[1] + c.shape[1], a.shape[2]), bf)
    return call(fold_feed_kernel, "fold_feed", scalar, [a, b, c, d], [shape] * GROUPS)


def fold_line_kernel(scalar_ref, *refs):
    sources, outs = refs[:GROUPS], refs[GROUPS:]
    for r, out_ref in enumerate(outs):
        at = turn(scalar_ref[GROUPS + 12], r)
        out_ref[...] = sum(ref[at].astype(f32) for ref in sources).astype(bf)


def fold_line(scalar, sources):
    return call(fold_line_kernel, "fold_line", scalar, sources, [sds(sources[0].shape[1:], bf)] * GROUPS)


def add_up_kernel(scalar_ref, *refs):
    *sources, out_ref = refs
    out_ref[...] = sum(ref[...].astype(f32) for ref in sources).astype(bf)


def add_up(scalar, name, arrays):
    return call(add_up_kernel, name, scalar, list(arrays), [sds(arrays[0].shape, bf)])[0]


def fold_rest_kernel(scalar_ref, a, b, c, d, out_ref):
    cut = a.shape[2]
    out_ref[:, :, :cut] = a[...] + b[...]
    out_ref[:, :, cut:] = c[...] + d[...]


def fold_rest(scalar, a, b, c, d):
    shape = a.shape[:2] + (a.shape[2] + c.shape[2],)
    return call(fold_rest_kernel, "fold_rest", scalar, [a, b, c, d], [sds(shape, bf)])[0]


def sum_space_kernel(scalar_ref, got_ref, out_ref):
    chunk = got_ref.shape[0] // GROUPS
    lanes = 3 * 128
    sums = []
    for x in range(GROUPS):
        acc = got_ref[chunk * x].astype(f32)
        for i in range(1, chunk):
            acc += got_ref[chunk * x + i].astype(f32)
        sums.append(acc)
    everything = functools.reduce(jnp.add, sums)
    shared = scalar_ref[GROUPS + 5] > 0
    for x in range(GROUPS):
        tail = jnp.where(shared, everything[:, lanes:], sums[x][:, lanes:])
        block = jnp.concatenate([everything[:, :lanes], tail], axis=1).astype(bf)
        for i in range(chunk):
            out_ref[chunk * x + i] = block


def sum_space(scalar, got):
    return call(sum_space_kernel, "sum_space", scalar, [got], [sds(got.shape, bf)])[0]


def finish_kernel(
    scalar_ref,
    part_ref,
    r3,
    r1,
    r2,
    start_ref,
    gmid_ref,
    rows_ref,
    unseen_ref,
    bq_ref,
    bv_ref,
    feed_ref,
    bup_ref,
    kept_ref,
    sent_ref,
    low_ref,
):
    rows, width = start_ref.shape
    first_grad = part_ref[...] + r3[...].astype(f32) + r1[...].astype(f32) + r2[...].astype(f32)
    n, inverse = norm_parts(start_ref[...])
    grad = gmid_ref[...] + norm_pull(first_grad, n, inverse, rows_ref[1:2])
    low_ref[...] = grad.astype(bf)
    half = rows // 2
    first = scalar_ref[GROUPS + 4] == 0
    top, low = grad[:half], grad[half:]
    lines = [
        column_sum(unseen_ref[:, :1] * grad),
        column_sum(first_grad * n),
        column_sum(first_grad),
        bq_ref[...],
        bv_ref[...],
        feed_ref[:4],
    ]
    blocks = bup_ref.shape[1] // width
    lines += [bup_ref[:, width * i : width * (i + 1)] for i in range(blocks)]
    spare = 16 - sum(a.shape[0] for a in lines)
    lines = jnp.concatenate(lines + [jnp.zeros((spare, width), f32)], axis=0)

    def narrow(values):
        cut = [a[:, 128 * i : 128 * (i + 1)] for a in (values, lines) for i in range(width // 128)]
        cut.append(jnp.zeros((kept_ref.shape[0] * kept_ref.shape[1] - sum(a.shape[0] for a in cut), 128), f32))
        return jnp.concatenate(cut, axis=0).reshape(kept_ref.shape).astype(bf)

    kept_ref[...] = narrow(jnp.where(first, top, low))
    sent_ref[...] = narrow(jnp.where(first, low, top))


def finish(scalar, part, received, start, gmid, vectors, unseen, bq, bv, feed_vec, grad_b_up):
    rows, width = start.shape
    tail = sds((GROUPS * SPREAD, 16, 128), bf)
    return call(
        finish_kernel,
        "finish",
        scalar,
        [part, *received, start, gmid, vectors, unseen, bq, bv, feed_vec, grad_b_up],
        [tail, tail, sds((rows, width), bf)],
    )


def ranked(lines, bases, rows):
    piece = lines[0].shape[1]
    flags = [((ids >= base) & (ids < base + rows)).astype(f32) for ids, base in zip(lines, bases)]
    flags = jnp.concatenate(flags + [jnp.zeros((8 - len(flags), piece), f32)], axis=0).astype(bf)
    row = lax.broadcasted_iota(jnp.int32, (piece, piece), 0)
    column = lax.broadcasted_iota(jnp.int32, (piece, piece), 1)
    rank = dg((column < row).astype(bf), flags, NT)
    here = dg((column == row).astype(bf), flags, NT)
    place = lax.broadcasted_iota(jnp.int32, (piece, CAP), 1).astype(f32)
    return [jnp.where(rank[:, i : i + 1] == place, here[:, i : i + 1], 0.0).astype(bf) for i in range(len(lines))]


def share_kernel(scalar_ref, low_ref, *refs):
    id_refs, outs, (share_ref, sem) = refs[:GROUPS], refs[GROUPS : 2 * GROUPS], refs[2 * GROUPS :]
    rows = low_ref.shape[0]
    piece = id_refs[0].shape[1]
    base = scalar_ref[GROUPS]
    slot = lax.broadcasted_iota(jnp.int32, (rows, piece), 0) + base
    lines = [id_ref[...] for id_ref in id_refs]
    for i, (ids, rank) in enumerate(zip(lines, ranked(lines, [base] * GROUPS, rows))):
        pick = dg((slot == ids).astype(bf), rank, NN).astype(bf)
        share_ref[i] = dg(pick, low_ref[...], TN).astype(bf)
    copies = [pltpu.make_async_copy(share_ref.at[i], out, sem.at[i]) for i, out in enumerate(outs)]
    for copy in copies:
        copy.start()
    for copy in copies:
        copy.wait()


def share(scalar, low, ids):
    shape = (CAP, low.shape[1])
    inside = pl.BlockSpec(memory_space=pltpu.VMEM)
    return pl.pallas_call(
        share_kernel,
        in_specs=[pl.BlockSpec(memory_space=pltpu.SMEM)] + [inside] * (1 + GROUPS),
        out_specs=[pl.BlockSpec(memory_space=pltpu.HBM)] * GROUPS,
        out_shape=[sds(shape, bf)] * GROUPS,
        scratch_shapes=[pltpu.VMEM((GROUPS,) + shape, bf), pltpu.SemaphoreType.DMA((GROUPS,))],
        compiler_params=pltpu.CompilerParams(vmem_limit_bytes=11 * 1024 * 1024),
        cost_estimate=pl.CostEstimate(flops=1000, bytes_accessed=1000, transcendentals=0),
        name="share",
    )(scalar, low, *ids)


def collect_kernel(scalar_ref, id_ref, *refs, rows):
    *shares, out_ref = refs
    ids = id_ref[...]
    ranks = ranked([ids] * GROUPS, [scalar_ref[GROUPS + i] for i in range(GROUPS)], rows)
    out_ref[...] = sum(dg(rank, ref[...], NN) for rank, ref in zip(ranks, shares)).astype(bf)


def collect(scalar, ids, shares, rows):
    shape = (ids.shape[1], shares[0].shape[1])
    return call(
        functools.partial(collect_kernel, rows=rows), "collect", scalar, [ids, *shares], [sds(shape, bf)]
    )[0]


def unpack_feed_kernel(scalar_ref, *refs):
    *sources, down_ref, up_ref, out_ref = refs
    mine, other = sources[:GROUPS], sources[GROUPS:]
    first = scalar_ref[GROUPS + 4] == 0
    lines = down_ref.shape[0] // GROUPS
    half = out_ref.shape[0] // 2
    extra = half // SPREAD

    def unpack(g):
        z_low, z_high = scalar_ref[GROUPS + 12 + g], scalar_ref[GROUPS + 8 + g]
        for k, far in enumerate(RELATIVE):
            low = jnp.where(first, mine[k][g], other[k][g]).astype(f32)
            high = jnp.where(first, other[g][k], mine[g][k]).astype(f32)
            y_low, y_high = turn(scalar_ref[GROUPS + 6], far), turn(scalar_ref[GROUPS + 12], far)
            down_ref[pl.ds(pl.multiple_of(lines * y_low, 16), lines), :] = low[:lines]
            up_ref[pl.ds(pl.multiple_of(lines * y_high, 16), lines), :] = high[:lines]
            at = extra * (GROUPS * z_low + y_low)
            out_ref[pl.ds(pl.multiple_of(at, 16), extra), :] = low[lines:]
            at = half + extra * (GROUPS * z_high + y_high)
            out_ref[pl.ds(pl.multiple_of(at, 16), extra), :] = high[lines:]

    for g in range(GROUPS):
        pl.when(pl.program_id(0) == g)(functools.partial(unpack, g))


def unpack_feed(scalar, mine, other, width, hidden):
    block = pl.BlockSpec(mine[0].shape, lambda g, s: (0, 0, 0))
    return grid_call(
        unpack_feed_kernel,
        "unpack_feed",
        scalar,
        GROUPS,
        [block] * (2 * GROUPS),
        [
            pl.BlockSpec((width, width), lambda g, s: (s[GROUPS + 12 + g], 0)),
            pl.BlockSpec((width, width), lambda g, s: (0, s[GROUPS + 8 + g])),
            pl.BlockSpec((width, width), lambda g, s: (0, 0)),
        ],
        [sds((hidden, width), f32), sds((width, hidden), f32), sds((width, width), f32)],
        [*mine, *other],
    )


def unpack_rest_kernel(scalar_ref, mine_ref, other_ref, out_ref, pos_ref, *vec_refs):
    core = scalar_ref[GROUPS + 4]
    half = out_ref.shape[0] // 2
    width = out_ref.shape[1] // 3
    rows = pos_ref.shape[0] // 2
    chunk = mine_ref.shape[0] // GROUPS
    for kept, ref in ((core, mine_ref), (1 - core, other_ref)):
        lines = pl.ds(pl.multiple_of(kept * half, half), half)
        for j in range(GROUPS):
            for w in range(3):
                lanes = slice(w * width + 128 * j, w * width + 128 * (j + 1))
                block = ref[chunk * j : chunk * (j + 1), :, 128 * w : 128 * (w + 1)]
                out_ref[lines, lanes] = block.reshape(half, 128).astype(f32)
        tail = ref[:, :, 3 * 128 :].astype(f32).reshape(-1, 128)
        lines = pl.ds(pl.multiple_of(kept * rows, 8), rows)
        blocks = width // 128
        for i in range(blocks):
            pos_ref[lines, 128 * i : 128 * (i + 1)] = tail[rows * i : rows * (i + 1)]
            if ref is mine_ref:
                base = rows * blocks + 16 * i
                for n, vec_ref in enumerate(vec_refs):
                    for line in range(vec_ref.shape[1] // width):
                        lanes = slice(width * line + 128 * i, width * line + 128 * (i + 1))
                        vec_ref[:, lanes] = tail[base + n + line : base + n + line + 1]


def unpack_rest(scalar, mine, other, rows, width, hidden):
    return call(
        unpack_rest_kernel,
        "unpack_rest",
        scalar,
        [mine, other],
        [sds((width, 3 * width), f32), sds((rows, width), f32)]
        + [sds((1, width), f32)] * 9
        + [sds((1, hidden), f32)],
    )


def shift(array, axis, step):
    size = lax.axis_size(axis)
    return lax.ppermute(array, axis, [(i, (i + step) % size) for i in range(size)])


def peers(array, axis):
    return [shift(array, axis, step) for step in (1, 3, 2)]


def swap(array):
    return shift(array, "core", 1)


def total(parts):
    return functools.reduce(jnp.add, [p.astype(f32) for p in parts])


SPACE = ("x", "z", "y")
PLANE = ("z", "y", "core")


def step_plane(array, step, near):
    sizes = [lax.axis_size(name) for name in PLANE]
    pairs = []
    for z in range(sizes[0]):
        for y in range(sizes[1]):
            for core in range(sizes[2]):
                if (core == 0) == near:
                    target = (z, (y + step) % sizes[1], core)
                else:
                    target = ((z + step) % sizes[0], y, core)
                index = lambda p: (p[0] * sizes[1] + p[1]) * sizes[2] + p[2]
                pairs.append((index((z, y, core)), index(target)))
    return lax.ppermute(array, PLANE, pairs)


def step_cores(array):
    size = lax.axis_size("x")
    pairs = []
    for core in range(2):
        for x in range(size):
            pairs.append((core * size + x, core * size + (x + 1 - 2 * core) % size))
    return lax.ppermute(array, ("core", "x"), pairs)


def plane_peers(array, near):
    return [step_plane(array, step, near) for step in (1, 3, 2)]


def exchange(array, axes):
    return lax.all_to_all(array, axes, 0, 0, tiled=True)


def body(
    vis,
    keep_slots,
    counts,
    band_mask,
    mask_token,
    pos,
    ln1_gain,
    ln1_bias,
    w_qkv,
    b_query,
    b_value,
    w_out,
    b_out,
    ln2_gain,
    ln2_bias,
    w_up,
    b_up,
    w_down,
    b_down,
    d_out,
):
    barrier = lax.optimization_barrier
    x = lax.axis_index("x")
    core = lax.axis_index("core")
    piece = keep_slots.shape[1]
    rows, width = pos.shape
    half = rows // 2
    hidden = w_up.shape[1]

    vis = vis[0]

    y, z = lax.axis_index("y"), lax.axis_index("z")
    relative = jnp.array(RELATIVE, jnp.int32)
    order = (x + relative) % GROUPS
    live = jnp.sum(jnp.where(order[:, None] == jnp.arange(GROUPS)[None, :], band_mask, 0), axis=1)
    here = (x * lax.axis_size("z") + z) * lax.axis_size("y") + y
    chunks = width // 128 * half // 16
    shared = (here >= chunks) & (here < chunks + width // 128)
    scalar = jnp.concatenate(
        [live, order * rows, jnp.stack([core, shared.astype(jnp.int32), y, z]), (z + relative) % GROUPS, order]
    ).astype(jnp.int32)
    pack = lambda *vs: jnp.pad(jnp.stack(vs), ((0, 8 - len(vs)), (0, 0)))
    vectors = pack(mask_token, ln1_gain, ln1_bias, b_query, b_value)
    feed_vectors = pack(b_out, ln2_gain, ln2_bias, b_down)

    index = lax.broadcasted_iota(jnp.int32, (1, piece), 1)
    code = jnp.where(index < counts, keep_slots, -1) + 1
    marks = jnp.concatenate([code // 64, code % 64], axis=0).astype(bf)
    marks = jnp.pad(marks, ((0, MARKS - 2), (0, width - piece)))
    message = jnp.concatenate([marks, vis], axis=0)
    pieces = [message] + peers(message, "x")
    pos_half = lax.dynamic_slice(pos, (half * core, 0), (half, width))
    pos_mine = [step_cores(pos), shift(pos_half, "x", 2)]
    scalar, vectors, feed_vectors, pieces = barrier((scalar, vectors, feed_vectors, pieces))
    start, normed, unseen, *bases = front(scalar, pieces, pos, vectors, piece)
    bases, ids = bases[: GROUPS - 1], bases[GROUPS - 1 :]
    q, turned_own, k_own, v_own, *state, p_own = attention_own(scalar, normed, vectors, w_qkv)
    state, pos_mine = barrier((state, pos_mine))
    pos_other = [swap(p) for p in pos_mine]
    out = middle(scalar, bases, pos_mine + pos_other, vectors, w_qkv, q, state)
    rest, (mixed, lse), kept = out[: 3 * (GROUPS - 1)], out[3 * (GROUPS - 1) :][:2], out[3 * (GROUPS - 1) + 2 :]
    keys, values = [k_own, *rest[1::3]], [v_own, *rest[2::3]]
    weights, peaks = [p_own, *kept[0::2]], [state[0], *kept[1::2]]

    out, middle_rows, second, kept, sent, grad_b_up = feed_forward(
        scalar, mixed, start, d_out[0], w_out, feed_vectors, w_up, b_up[None], w_down
    )
    got = swap(sent)
    grad_middle, out_kept, out_sent, feed_vec, *factors = feed_backward(
        scalar, mixed, middle_rows, second, d_out[0], w_out, feed_vectors, lse, peaks
    )
    inputs = list(zip(factors[:GROUPS], weights, keys, values, factors[GROUPS:]))
    feed = fold_feed(scalar, kept, got, out_kept, swap(out_sent))
    q, feed = barrier((q, feed))
    feed = [feed[0]] + [step_plane(feed[r], r, True) for r in (1, 2, 3)]
    dq, d_3, part = attention_grad(scalar, (3,), q, w_qkv, [inputs[3]], None)
    dq, part = barrier((dq, part))
    from_3 = shift(part, "x", 2)
    dq, d_1, part = attention_grad(scalar, (1,), q, w_qkv, [inputs[1]], dq)
    feed = fold_line(scalar, feed)
    dq, part, feed = barrier((dq, part, feed))
    feed = [feed[0]] + [shift(feed[r], "x", r) for r in (1, 2, 3)]
    from_1 = shift(part, "x", 3)
    dq, d_2, part = attention_grad(scalar, (2,), q, w_qkv, [inputs[2]], dq)
    feed = add_up(scalar, "fold_point", feed)
    dq, part, from_3, feed = barrier((dq, part, from_3, feed))
    feed_peers = plane_peers(feed, False)
    from_2 = shift(part, "x", 1)
    part, at_kept, at_sent, grad_b_query, grad_b_value = attention_grad(
        scalar, (0,), q, w_qkv, [inputs[0]], dq, [turned_own, *rest[0::3], d_3, d_1, d_2]
    )
    at_kept, at_sent, part, from_1, from_2, feed_peers = barrier(
        (at_kept, at_sent, part, from_1, from_2, feed_peers)
    )

    at_got = swap(at_sent)
    feed = add_up(scalar, "sum_line", [feed] + feed_peers)
    gathered = peers(feed, "x")
    tail_kept, tail_sent, low = finish(
        scalar,
        part,
        (from_3, from_1, from_2),
        start,
        grad_middle,
        vectors,
        unseen,
        grad_b_query,
        grad_b_value,
        feed_vec,
        grad_b_up,
    )
    spread = lambda a: a.reshape(GROUPS * SPREAD, 16, -1)
    bundle = fold_rest(scalar, spread(at_kept), spread(at_got), tail_kept, swap(tail_sent))
    bundle, feed = barrier((bundle, [feed] + gathered))
    bundle = exchange(bundle, SPACE)
    feed = jnp.stack(feed)
    feed_other = [swap(feed)]
    feed = [feed] + plane_peers(feed, True)
    bundle, shares, feed_other = barrier((bundle, share(scalar, low, ids), feed_other))
    bundle = sum_space(scalar, bundle)
    feed, _ = barrier((feed, bundle))
    rest_mine = exchange(bundle, SPACE)
    feed_other += [swap(a) for a in feed[1:]]
    feed_other[1], shares = barrier((feed_other[1], shares))
    returned = [shares[0], shift(shares[2], "x", 1), shift(shares[1], "x", 3), shift(shares[3], "x", 2)]
    grad_w_down, grad_w_up, grad_w_out = unpack_feed(scalar, feed, feed_other, width, hidden)
    grad_vis = collect(scalar, ids[0], returned, rows)
    rest_mine, grad_w_down, grad_vis = barrier((rest_mine, grad_w_down, grad_vis))
    rest_other = swap(rest_mine)
    grad_w_qkv, grad_pos, *sums = unpack_rest(scalar, rest_mine, rest_other, rows, width, hidden)
    sums = [a[0] for a in sums]

    return (
        out[None],
        grad_vis[None],
        sums[0],
        grad_pos,
        sums[1],
        sums[2],
        grad_w_qkv,
        sums[3],
        sums[4],
        grad_w_out,
        sums[5],
        sums[6],
        sums[7],
        grad_w_up,
        sums[9],
        grad_w_down,
        sums[8],
    )


CUBE = ("z", "y", "core")


def solution(mesh):
    fine = Mesh(mesh.devices.reshape(4, 4, 2, 4), ("z", "y", "core", "x"))
    return jax.shard_map(
        body,
        mesh=fine,
        in_specs=(
            P(CUBE, "x", None),
            P(CUBE, "x"),
            P(CUBE, "x"),
            P(CUBE, None),
            P(),
            P("x", None),
        )
        + (P(),) * 13
        + (P(CUBE, "x", None),),
        out_specs=(P(CUBE, "x", None), P(CUBE, "x", None), P(), P("x", None)) + (P(),) * 13,
        check_vma=False,
    )
```

```python
import functools

import jax
import jax.numpy as jnp
from jax import lax
from jax.experimental import pallas as pl
from jax.experimental.pallas import tpu as pltpu
from jax.sharding import Mesh, PartitionSpec as P

bf = jnp.bfloat16
f32 = jnp.float32

HEADS = 16
DEPTH = 32
QUAD = 4
GROUPS = 4
LOG2E = 1.4426950408889634
SCALE = DEPTH**-0.5
EPS = 1e-05
BIG = 1e30
GELU_SCALE = 0.7978845608028654
GELU_CUBE = 0.044715
RELATIVE = (0, 3, 1, 2)
OPPOSITE = (0, 2, 3, 1)
CAP = 80
MARKS = 16
SPREAD = 16

NT = (((1,), (1,)), ((), ()))
NN = (((1,), (0,)), ((), ()))
TN = (((0,), (0,)), ((), ()))
VMEM_LIMIT = 56 * 1024 * 1024


def dg(a, b, dims):
    return lax.dot_general(a, b, dims, preferred_element_type=f32)


def sds(shape, dtype):
    return jax.ShapeDtypeStruct(shape, dtype)


def call(kernel, name, scalar, operands, out_shape, scratch=(), aliases=None, limit=5, micro=0.001):
    inside = pl.BlockSpec(memory_space=pltpu.VMEM)
    return pl.pallas_call(
        kernel,
        in_specs=[pl.BlockSpec(memory_space=pltpu.SMEM)] + [inside] * len(operands),
        out_specs=[inside] * len(out_shape),
        out_shape=out_shape,
        scratch_shapes=list(scratch),
        compiler_params=pltpu.CompilerParams(vmem_limit_bytes=limit * 1024 * 1024),
        cost_estimate=pl.CostEstimate(flops=int(micro * 1e9), bytes_accessed=1000, transcendentals=0),
        input_output_aliases=aliases or {},
        name=name,
    )(scalar, *operands)


def grid_call(kernel, name, scalar, steps, in_specs, out_specs, out_shape, operands):
    return pl.pallas_call(
        kernel,
        grid_spec=pltpu.PrefetchScalarGridSpec(
            num_scalar_prefetch=1, grid=(steps,), in_specs=in_specs, out_specs=out_specs
        ),
        out_shape=out_shape,
        compiler_params=pltpu.CompilerParams(vmem_limit_bytes=32 * 1024 * 1024),
        cost_estimate=pl.CostEstimate(flops=1000, bytes_accessed=1000, transcendentals=0),
        name=name,
    )(scalar, *operands)


def column_sum(tensor):
    return jnp.sum(tensor.astype(f32), axis=0, keepdims=True)


def norm_parts(values):
    centered = values - jnp.mean(values, axis=-1, keepdims=True)
    variance = jnp.mean(centered * centered, axis=-1, keepdims=True)
    inverse = lax.rsqrt(variance + EPS)
    return centered * inverse, inverse


def norm_pull(grad, n, inverse, gain):
    g = grad * gain
    return inverse * (
        g - jnp.mean(g, axis=-1, keepdims=True) - n * jnp.mean(g * n, axis=-1, keepdims=True)
    )


def place_rows(base, pieces, ids, rows, rows_ref):
    piece, width = ids[0].shape[1], rows_ref.shape[1]
    slot = lax.broadcasted_iota(jnp.int32, (rows, piece), 0) + base
    placed = jnp.zeros((rows, width), f32)
    seen = jnp.zeros((rows, 1), f32)
    for v, i in zip(pieces, ids):
        hot = (slot == i).astype(f32)
        seen += jnp.sum(hot, axis=1, keepdims=True)
        placed += dg(hot.astype(bf), v[MARKS : MARKS + piece, :], NN)
    unseen = 1.0 - seen
    return placed + unseen * rows_ref[0:1], unseen


def first_norm(start, rows_ref):
    n, _ = norm_parts(start)
    return (n * rows_ref[1:2] + rows_ref[2:3]).astype(bf)


def keys_values(normed, rows_ref, w_ref, turned_ref, k_ref, v_ref):
    width = normed.shape[1]
    k_ref[...] = dg(normed, w_ref[:, width : 2 * width], NN).astype(bf)
    v_ref[...] = (dg(normed, w_ref[:, 2 * width :], NN) + rows_ref[4:5]).astype(bf)
    turned_ref[...] = normed.T


def stack_heads(x):
    lane = lax.broadcasted_iota(jnp.int32, x.shape, 1) // DEPTH
    return jnp.concatenate([jnp.where(lane == h, x, jnp.zeros_like(x)) for h in range(QUAD)], axis=0)


def unstack_heads(xt):
    rows = xt.shape[1] // QUAD
    parts = [xt[DEPTH * h : DEPTH * (h + 1), rows * h : rows * (h + 1)] for h in range(QUAD)]
    return jnp.concatenate(parts, axis=0).T


def fwd_steps(steps, scalar_ref, query, key, value, state, keep_weights, finish):
    stacked = {}

    def scores(quad, group):
        if quad not in stacked:
            stacked[quad] = stack_heads(query(quad))
        return dg(key(quad, group), stacked[quad], NT)

    ahead = scores(*steps[0])
    for i, (quad, group) in enumerate(steps):
        s = ahead
        if i + 1 < len(steps):
            ahead = scores(*steps[i + 1])
        live = scalar_ref[group] > 0
        peak = jnp.where(live, jnp.max(s, axis=0, keepdims=True), -BIG)
        old = state(quad) if i == 0 or steps[i - 1][0] != quad else new
        if old is not None:
            peak = jnp.maximum(old[0], peak)
        p = jnp.exp2(s - jnp.where(live, peak, BIG)).astype(bf)
        keep_weights(quad, group, p, peak)
        v = value(quad, group)
        turned = jnp.concatenate([v.T, jnp.ones((16, v.shape[0]), bf)], axis=0)
        both = dg(turned, p, NN)
        o, l = both[: v.shape[1]], both[v.shape[1] : v.shape[1] + 1]
        if old is not None:
            keep = jnp.exp2(old[0] - peak)
            o += old[2] * keep
            l += old[1] * keep
        new = (peak, l, o)
        if i + 1 == len(steps) or steps[i + 1][0] != quad:
            finish(quad, new)


def quad_at(quad):
    return (slice(None), slice(128 * quad, 128 * (quad + 1)))


def front_kernel(scalar_ref, *refs):
    pieces, (pos_ref, rows_ref), refs = refs[:GROUPS], refs[GROUPS : GROUPS + 2], refs[GROUPS + 2 :]
    start_ref, normed_ref, aux_ref, *rests = refs
    rows = pos_ref.shape[0]
    piece = pieces[0].shape[0] - MARKS
    ids = []
    for i, v in enumerate(pieces):
        marks = v[:MARKS, :].astype(f32)[:8, :piece]
        line = marks[0:1] * 64.0 + marks[1:2] - 1.0
        aux_ref[rows + i : rows + i + 1, :piece] = line
        ids.append(line.astype(jnp.int32))
    start, unseen = place_rows(scalar_ref[GROUPS], pieces, ids, rows, rows_ref)
    start += pos_ref[...].astype(f32)
    start_ref[...] = start
    aux_ref[:rows, :128] = jnp.broadcast_to(unseen, (rows, 128))
    normed_ref[...] = first_norm(start, rows_ref)
    for g, rest in enumerate(rests):
        rest[...], _ = place_rows(scalar_ref[GROUPS + 1 + g], pieces, ids, rows, rows_ref)


def read_slots(aux_ref, count, piece):
    rows = aux_ref.shape[0] - 8
    return [aux_ref[rows + i : rows + i + 1, :piece].astype(jnp.int32) for i in range(count)]


def front(scalar, pieces, pos, vectors):
    rows, width = pos.shape
    return call(
        front_kernel,
        "front",
        scalar,
        [*pieces, pos, vectors],
        [sds((rows, width), f32), sds((rows, width), bf), sds((rows + 8, 256), f32)]
        + [sds((rows, width), f32)] * (GROUPS - 1),
        micro=4,
    )


def attention_own_kernel(
    scalar_ref, normed_ref, rows_ref, w_ref, q_ref, turned_ref, k_ref, v_ref, m_ref, l_ref, o_ref, p_ref
):
    normed = normed_ref[...]
    width = normed.shape[1]
    q_ref[...] = ((dg(normed, w_ref[:, :width], NN) + rows_ref[3:4]) * (SCALE * LOG2E)).astype(bf)
    keys_values(normed, rows_ref, w_ref, turned_ref, k_ref, v_ref)

    def keep_weights(quad, group, p, peak):
        p_ref[quad] = p

    def finish(quad, state):
        m_ref[quad], l_ref[quad], o_ref[quad] = state

    fwd_steps(
        [(quad, 0) for quad in range(m_ref.shape[0])],
        scalar_ref,
        lambda quad: q_ref[quad_at(quad)],
        lambda quad, group: k_ref[quad_at(quad)],
        lambda quad, group: v_ref[quad_at(quad)],
        lambda quad: None,
        keep_weights,
        finish,
    )


def attention_own(scalar, normed, vectors, w_qkv):
    rows, width = normed.shape
    quads, n = width // 128, rows * QUAD
    return call(
        attention_own_kernel,
        "attention_own",
        scalar,
        [normed, vectors, w_qkv],
        [
            sds((rows, width), bf),
            sds((width, rows), bf),
            sds((rows, width), bf),
            sds((rows, width), bf),
            sds((quads, 1, n), f32),
            sds((quads, 1, n), f32),
            sds((quads, 128, n), f32),
            sds((quads, rows, n), bf),
        ],
        limit=7,
        micro=5,
    )


def middle_kernel(scalar_ref, *refs):
    bases, refs = refs[: GROUPS - 1], refs[GROUPS - 1 :]
    pos_refs, refs = refs[:4], refs[4:]
    rows_ref, w_ref, q_ref, m_ref, l_ref, o_ref, *refs = refs
    groups, (mixed_ref, lse_ref), kept = refs[: 3 * (GROUPS - 1)], refs[3 * (GROUPS - 1) :][:2], refs[3 * (GROUPS - 1) + 2 :]
    first = scalar_ref[GROUPS + GROUPS] == 0
    near, far, other_near, other_far = [ref[...].astype(f32) for ref in pos_refs]
    for g, base in enumerate(bases):
        if g < 2:
            pos = jnp.where(first == (g == 0), near, other_near)
        else:
            pos = jnp.concatenate([jnp.where(first, far, other_far), jnp.where(first, other_far, far)], axis=0)
        keys_values(first_norm(base[...] + pos, rows_ref), rows_ref, w_ref, *groups[3 * g : 3 * g + 3])

    def keep_weights(quad, group, p, peak):
        kept[2 * group - 2][quad] = p
        kept[2 * group - 1][quad] = peak

    def finish(quad, state):
        m, l, o = state
        mixed_ref[quad_at(quad)] = unstack_heads(o / l).astype(bf)
        lse_ref[quad] = m + jnp.log2(l)

    fwd_steps(
        [(quad, group) for quad in range(m_ref.shape[0]) for group in range(1, GROUPS)],
        scalar_ref,
        lambda quad: q_ref[quad_at(quad)],
        lambda quad, group: groups[3 * group - 2][quad_at(quad)],
        lambda quad, group: groups[3 * group - 1][quad_at(quad)],
        lambda quad: (m_ref[quad], l_ref[quad], o_ref[quad]),
        keep_weights,
        finish,
    )


def middle(scalar, bases, pos, vectors, w_qkv, q, state):
    rows, width = q.shape
    quads, n = width // 128, rows * QUAD
    group = [sds((width, rows), bf), sds((rows, width), bf), sds((rows, width), bf)]
    return call(
        middle_kernel,
        "middle",
        scalar,
        [*bases, *pos, vectors, w_qkv, q, *state],
        [*(group * (GROUPS - 1)), sds((rows, width), bf), sds((quads, 1, n), f32)]
        + [sds((quads, rows, n), bf), sds((quads, 1, n), f32)] * (GROUPS - 1),
        limit=9,
    )


def bwd_kernel(scalar_ref, q_ref, w_ref, *refs, groups, carried):
    width = q_ref.shape[1]
    inputs, refs = [refs[5 * i : 5 * i + 5] for i in range(len(groups))], refs[5 * len(groups) :]
    if carried:
        dq_in, *refs = refs
    own = groups == (0,)
    if own:
        *turned_refs, d_3, d_1, d_2, part_ref, kept_ref, sent_ref, bq_ref, bv_ref, d_s = refs
        base, outs = width, [(d_s, part_ref)]
    else:
        dq_ref, *refs = refs
        base, outs = 0, [refs[2 * i : 2 * i + 2] for i in range(len(groups))]
    quads = width // 128
    for j in range(quads):
        at = quad_at(j)
        qs = stack_heads(q_ref[at])
        dq = dq_in[at] if carried else None
        for (do_ref, p_ref, k_ref, v_ref, delta_ref), (d_ref, _) in zip(inputs, outs):
            columns = lambda i: (
                slice(None),
                slice(base + (i - 1) * width + 128 * j, base + (i - 1) * width + 128 * (j + 1)),
            )
            dos = stack_heads(do_ref[at])
            k, p = k_ref[at], p_ref[j]
            ds = (p.astype(f32) * (dg(v_ref[at], dos, NT) - delta_ref[j])).astype(bf)
            d_ref[columns(2)] = dg(p, dos, NN).astype(bf)
            d_ref[columns(1)] = (dg(ds, qs, NN) * (1.0 / LOG2E)).astype(bf)
            term = unstack_heads(dg(k, ds, TN))
            dq = term if dq is None else dq + term
        if own:
            d_s[at] = (dq * SCALE).astype(bf)
        else:
            dq_ref[at] = dq
    for d_ref, part_ref in outs:
        grads = d_ref[...]
        part_ref[...] = dg(grads, w_ref[...] if own else w_ref[:, width:], NT).astype(part_ref.dtype)
    if not own:
        return
    own, *rest = turned_refs
    g = dg(own[...], grads[:, width:], NN)
    bv = column_sum(grads[:, 2 * width :])
    for turned, d_ref in zip(rest, (d_1, d_2, d_3)):
        d = d_ref[...]
        g += dg(turned[...], d, NN)
        bv += column_sum(d[:, width:])
    bv_ref[...] = bv
    bq_ref[...] = column_sum(grads[:, :width])
    gq = dg(own[...], grads[:, :width], NN)
    first = scalar_ref[GROUPS + 4] == 0
    half = width // 2
    for j in range(quads):
        at = slice(128 * j, 128 * (j + 1))
        block = jnp.concatenate([gq[:, at], g[:, at], g[:, width + 128 * j : width + 128 * (j + 1)]], axis=1)
        kept_ref[j] = jnp.where(first, block[:half], block[half:]).astype(bf)
        sent_ref[j] = jnp.where(first, block[half:], block[:half]).astype(bf)


def attention_grad(scalar, groups, q, w_qkv, inputs, dq, more=()):
    rows, width = q.shape
    quads = width // 128
    operands = [q, w_qkv] + [a for group in inputs for a in group]
    aliases = {}
    if dq is not None:
        aliases = {len(operands) + 1: 0}
        operands.append(dq)
    operands += list(more)
    scratch = []
    if groups == (0,):
        packed = (quads, width // 2, 3 * 128)
        out_shape = [sds((rows, width), f32)] + [sds(packed, bf)] * 2 + [sds((1, width), f32)] * 2
        scratch = [pltpu.VMEM((rows, 3 * width), bf)]
    else:
        out_shape = [sds((rows, width), f32)]
        out_shape += [sds((rows, 2 * width), bf), sds((rows, width), bf)] * len(groups)
    return call(
        functools.partial(bwd_kernel, groups=groups, carried=dq is not None),
        "attention_grad_" + "_".join(str(g) for g in groups),
        scalar,
        operands,
        out_shape,
        scratch,
        aliases,
    )


def feed_kernel(
    scalar_ref,
    mixed_ref,
    start_ref,
    dout_ref,
    wout_ref,
    rows_ref,
    wup_ref,
    bup_ref,
    wdown_ref,
    out_ref,
    middle_ref,
    second_ref,
    kept_ref,
    sent_ref,
    gbup_ref,
):
    first = scalar_ref[GROUPS + 4] == 0
    width = mixed_ref.shape[1]
    hidden = wup_ref.shape[1]
    dout = dout_ref[...]
    middle = start_ref[...] + (dg(mixed_ref[...], wout_ref[...], NN) + rows_ref[0:1])
    middle_ref[...] = middle
    n, _ = norm_parts(middle)
    normed = (n * rows_ref[1:2] + rows_ref[2:3]).astype(bf)
    turned = normed.T
    result = middle + rows_ref[3:4]
    second = jnp.zeros_like(middle)
    lines = hidden // SPREAD
    for h in range(hidden // width):
        at = slice(width * h, width * (h + 1))
        u = dg(normed, wup_ref[:, at], NN) + bup_ref[:, at]
        square = u * u
        t = jnp.tanh(u * (GELU_SCALE + (GELU_SCALE * GELU_CUBE) * square))
        near = 0.5 + 0.5 * t
        act = (u * near).astype(bf)
        result += dg(act, wdown_ref[at, :], NN)
        slope = near + u * (0.5 - 0.5 * (t * t)) * (GELU_SCALE + (3.0 * GELU_SCALE * GELU_CUBE) * square)
        gup = (dg(dout, wdown_ref[at, :], NT) * slope).astype(bf)
        second += dg(gup, wup_ref[:, at], NT)
        gbup_ref[:, at] = column_sum(gup)
        down = dg(act, dout, TN).astype(bf)
        up = dg(turned, gup, NN).astype(bf)
        chunks = (width // lines, lines, width)
        places = slice(h * chunks[0], (h + 1) * chunks[0])
        kept_ref[places] = jnp.where(first, down, up).reshape(chunks)
        sent_ref[places] = jnp.where(first, up, down).reshape(chunks)
    out_ref[...] = result.astype(bf)
    second_ref[...] = second


def feed_backward_kernel(
    scalar_ref,
    mixed_ref,
    middle_ref,
    second_ref,
    dout_ref,
    wout_ref,
    rows_ref,
    gmid_ref,
    gmix_ref,
    kept_ref,
    sent_ref,
    vec_ref,
):
    first = scalar_ref[GROUPS + 4] == 0
    mixed = mixed_ref[...]
    width = mixed.shape[1]
    second = second_ref[...]
    grad = dout_ref[...].astype(f32)
    n, inverse = norm_parts(middle_ref[...])
    gmid = grad + norm_pull(second, n, inverse, rows_ref[1:2])
    gmid_ref[...] = gmid
    branch = gmid.astype(bf)
    gmix_ref[...] = dg(branch, wout_ref[...], NT).astype(bf)
    wout = dg(mixed, branch, TN)
    half = width // 2
    extra = (SPREAD, half // SPREAD, width)
    kept_ref[...] = jnp.where(first, wout[:half], wout[half:]).astype(bf).reshape(extra)
    sent_ref[...] = jnp.where(first, wout[half:], wout[:half]).astype(bf).reshape(extra)
    vec_ref[...] = jnp.concatenate(
        [
            column_sum(branch),
            column_sum(second * n),
            column_sum(second),
            column_sum(grad),
            jnp.zeros((4, width), f32),
        ],
        axis=0,
    )


def factor_kernel(scalar_ref, mixed_ref, gmix_ref, lse_ref, *refs):
    peaks, outs = refs[:GROUPS], refs[GROUPS:]
    gmix = gmix_ref[...].astype(f32)
    width = gmix.shape[1]
    product = mixed_ref[...].astype(f32) * gmix
    head = lax.broadcasted_iota(jnp.int32, (HEADS, width), 0)
    lane = lax.broadcasted_iota(jnp.int32, (HEADS, width), 1) // DEPTH
    pick = (head == lane).astype(bf)
    halves = lambda a: (a.astype(bf), (a - a.astype(bf).astype(f32)).astype(bf))
    high, low = halves(product)
    delta = dg(pick, high, NT) + dg(pick, low, NT)
    rows = delta.shape[1]
    for peak_ref, do_ref, delta_ref in zip(peaks, outs[:GROUPS], outs[GROUPS:]):
        lines = []
        for j in range(HEADS // QUAD):
            factor = jnp.exp2(peak_ref[j] - lse_ref[j])
            delta_ref[j] = factor * jnp.concatenate([delta[QUAD * j + i : QUAD * j + i + 1] for i in range(QUAD)], axis=1)
            lines += [factor[:, rows * i : rows * (i + 1)] for i in range(QUAD)]
        high, low = halves(jnp.concatenate(lines, axis=0))
        do_ref[...] = (gmix * (dg(high, pick, TN) + dg(low, pick, TN))).astype(bf)


def feed_forward(scalar, mixed, start, d_out, w_out, vectors, w_up, b_up, w_down):
    rows, width = mixed.shape
    hidden = w_up.shape[1]
    packed = (SPREAD, hidden // SPREAD, width)
    return call(
        feed_kernel,
        "feed_forward",
        scalar,
        [mixed, start, d_out, w_out, vectors, w_up, b_up, w_down],
        [sds((rows, width), bf)] + [sds((rows, width), f32)] * 2 + [sds(packed, bf)] * 2 + [sds((1, hidden), f32)],
        limit=8,
    )


def feed_backward(scalar, mixed, middle, second, d_out, w_out, vectors):
    rows, width = mixed.shape
    packed = (SPREAD, width // 2 // SPREAD, width)
    return call(
        feed_backward_kernel,
        "feed_backward",
        scalar,
        [mixed, middle, second, d_out, w_out, vectors],
        [sds((rows, width), f32), sds((rows, width), bf), sds(packed, bf), sds(packed, bf), sds((8, width), f32)],
    )


def softmax_factors(scalar, mixed, gmix, lse, peaks):
    return call(
        factor_kernel,
        "softmax_factors",
        scalar,
        [mixed, gmix, lse, *peaks],
        [sds(gmix.shape, bf)] * GROUPS + [sds(lse.shape, f32)] * GROUPS,
        micro=2,
    )


def turn(place, steps):
    return lax.rem(place + steps, GROUPS)


def fold_feed_kernel(scalar_ref, a, b, c, d, *outs):
    first, y, z = scalar_ref[GROUPS + 4] == 0, scalar_ref[GROUPS + 6], scalar_ref[GROUPS + 7]
    near = jnp.where(first, y, z)
    lines = a.shape[1]
    for r, out_ref in enumerate(outs):
        place = turn(near, r)
        for i in range(GROUPS):
            at = jnp.where(first, GROUPS * i + place, GROUPS * place + i)
            out_ref[i, :lines] = a[at] + b[at]
            out_ref[i, lines:] = c[at] + d[at]


def fold_feed(scalar, a, b, c, d):
    shape = sds((GROUPS, a.shape[1] + c.shape[1], a.shape[2]), bf)
    return call(fold_feed_kernel, "fold_feed", scalar, [a, b, c, d], [shape] * GROUPS)


def fold_line_kernel(scalar_ref, *refs):
    sources, outs = refs[:GROUPS], refs[GROUPS:]
    for r, out_ref in enumerate(outs):
        at = turn(scalar_ref[GROUPS + 12], r)
        out_ref[...] = sum(ref[at].astype(f32) for ref in sources).astype(bf)


def fold_line(scalar, sources):
    return call(fold_line_kernel, "fold_line", scalar, sources, [sds(sources[0].shape[1:], bf)] * GROUPS)


def add_up_kernel(scalar_ref, *refs):
    *sources, out_ref = refs
    out_ref[...] = sum(ref[...].astype(f32) for ref in sources).astype(bf)


def add_up(scalar, name, arrays):
    return call(add_up_kernel, name, scalar, list(arrays), [sds(arrays[0].shape, bf)])[0]


def fold_rest_kernel(scalar_ref, a, b, c, d, out_ref):
    cut = a.shape[2]
    out_ref[:, :, :cut] = a[...] + b[...]
    out_ref[:, :, cut:] = c[...] + d[...]


def fold_rest(scalar, a, b, c, d):
    shape = a.shape[:2] + (a.shape[2] + c.shape[2],)
    return call(fold_rest_kernel, "fold_rest", scalar, [a, b, c, d], [sds(shape, bf)])[0]


def sum_space_kernel(scalar_ref, got_ref, out_ref):
    chunk = got_ref.shape[0] // GROUPS
    lanes = 3 * 128
    sums = []
    for x in range(GROUPS):
        acc = got_ref[chunk * x].astype(f32)
        for i in range(1, chunk):
            acc += got_ref[chunk * x + i].astype(f32)
        sums.append(acc)
    everything = functools.reduce(jnp.add, sums)
    shared = scalar_ref[GROUPS + 5] > 0
    for x in range(GROUPS):
        tail = jnp.where(shared, everything[:, lanes:], sums[x][:, lanes:])
        block = jnp.concatenate([everything[:, :lanes], tail], axis=1).astype(bf)
        for i in range(chunk):
            out_ref[chunk * x + i] = block


def sum_space(scalar, got):
    return call(sum_space_kernel, "sum_space", scalar, [got], [sds(got.shape, bf)])[0]


def finish_kernel(
    scalar_ref,
    part_ref,
    r3,
    r1,
    r2,
    start_ref,
    gmid_ref,
    rows_ref,
    unseen_ref,
    bq_ref,
    bv_ref,
    feed_ref,
    bup_ref,
    kept_ref,
    sent_ref,
    low_ref,
):
    rows, width = start_ref.shape
    first_grad = part_ref[...] + r3[...].astype(f32) + r1[...].astype(f32) + r2[...].astype(f32)
    n, inverse = norm_parts(start_ref[...])
    grad = gmid_ref[...] + norm_pull(first_grad, n, inverse, rows_ref[1:2])
    low_ref[...] = grad.astype(bf)
    half = rows // 2
    first = scalar_ref[GROUPS + 4] == 0
    top, low = grad[:half], grad[half:]
    lines = [
        column_sum(unseen_ref[:rows, :1] * grad),
        column_sum(first_grad * n),
        column_sum(first_grad),
        bq_ref[...],
        bv_ref[...],
        feed_ref[:4],
    ]
    blocks = bup_ref.shape[1] // width
    lines += [bup_ref[:, width * i : width * (i + 1)] for i in range(blocks)]
    spare = 16 - sum(a.shape[0] for a in lines)
    lines = jnp.concatenate(lines + [jnp.zeros((spare, width), f32)], axis=0)

    def narrow(values):
        cut = [a[:, 128 * i : 128 * (i + 1)] for a in (values, lines) for i in range(width // 128)]
        cut.append(jnp.zeros((kept_ref.shape[0] * kept_ref.shape[1] - sum(a.shape[0] for a in cut), 128), f32))
        return jnp.concatenate(cut, axis=0).reshape(kept_ref.shape).astype(bf)

    kept_ref[...] = narrow(jnp.where(first, top, low))
    sent_ref[...] = narrow(jnp.where(first, low, top))


def finish(scalar, part, received, start, gmid, vectors, unseen, bq, bv, feed_vec, grad_b_up):
    rows, width = start.shape
    tail = sds((GROUPS * SPREAD, 16, 128), bf)
    return call(
        finish_kernel,
        "finish",
        scalar,
        [part, *received, start, gmid, vectors, unseen, bq, bv, feed_vec, grad_b_up],
        [tail, tail, sds((rows, width), bf)],
    )


def ranked(lines, bases, rows):
    piece = lines[0].shape[1]
    flags = [((ids >= base) & (ids < base + rows)).astype(f32) for ids, base in zip(lines, bases)]
    flags = jnp.concatenate(flags + [jnp.zeros((8 - len(flags), piece), f32)], axis=0).astype(bf)
    row = lax.broadcasted_iota(jnp.int32, (piece, piece), 0)
    column = lax.broadcasted_iota(jnp.int32, (piece, piece), 1)
    rank = dg((column < row).astype(bf), flags, NT)
    here = dg((column == row).astype(bf), flags, NT)
    place = lax.broadcasted_iota(jnp.int32, (piece, CAP), 1).astype(f32)
    return [jnp.where(rank[:, i : i + 1] == place, here[:, i : i + 1], 0.0).astype(bf) for i in range(len(lines))]


def share_kernel(scalar_ref, low_ref, aux_ref, *refs, piece):
    outs, (share_ref, sem) = refs[:GROUPS], refs[GROUPS:]
    rows = low_ref.shape[0]
    base = scalar_ref[GROUPS]
    slot = lax.broadcasted_iota(jnp.int32, (rows, piece), 0) + base
    lines = read_slots(aux_ref, GROUPS, piece)
    for i, (ids, rank) in enumerate(zip(lines, ranked(lines, [base] * GROUPS, rows))):
        pick = dg((slot == ids).astype(bf), rank, NN).astype(bf)
        share_ref[i] = dg(pick, low_ref[...], TN).astype(bf)
    copies = [pltpu.make_async_copy(share_ref.at[i], out, sem.at[i]) for i, out in enumerate(outs)]
    for copy in copies:
        copy.start()
    for copy in copies:
        copy.wait()


def share(scalar, low, aux, piece):
    shape = (CAP, low.shape[1])
    inside = pl.BlockSpec(memory_space=pltpu.VMEM)
    return pl.pallas_call(
        functools.partial(share_kernel, piece=piece),
        in_specs=[pl.BlockSpec(memory_space=pltpu.SMEM), inside, inside],
        out_specs=[pl.BlockSpec(memory_space=pltpu.HBM)] * GROUPS,
        out_shape=[sds(shape, bf)] * GROUPS,
        scratch_shapes=[pltpu.VMEM((GROUPS,) + shape, bf), pltpu.SemaphoreType.DMA((GROUPS,))],
        compiler_params=pltpu.CompilerParams(vmem_limit_bytes=11 * 1024 * 1024),
        cost_estimate=pl.CostEstimate(flops=1000, bytes_accessed=1000, transcendentals=0),
        name="share",
    )(scalar, low, aux)


def collect_kernel(scalar_ref, aux_ref, *refs, rows):
    *shares, out_ref = refs
    (ids,) = read_slots(aux_ref, 1, out_ref.shape[0])
    ranks = ranked([ids] * GROUPS, [scalar_ref[GROUPS + i] for i in range(GROUPS)], rows)
    out_ref[...] = sum(dg(rank, ref[...], NN) for rank, ref in zip(ranks, shares)).astype(bf)


def collect(scalar, aux, shares, rows, piece):
    shape = (piece, shares[0].shape[1])
    return call(
        functools.partial(collect_kernel, rows=rows), "collect", scalar, [aux, *shares], [sds(shape, bf)]
    )[0]


def unpack_feed_kernel(scalar_ref, *refs):
    *sources, down_ref, up_ref, out_ref = refs
    mine, other = sources[:GROUPS], sources[GROUPS:]
    first = scalar_ref[GROUPS + 4] == 0
    lines = down_ref.shape[0] // GROUPS
    half = out_ref.shape[0] // 2
    extra = half // SPREAD

    def unpack(g):
        z_low, z_high = scalar_ref[GROUPS + 12 + g], scalar_ref[GROUPS + 8 + g]
        for k, far in enumerate(OPPOSITE):
            low = jnp.where(first, mine[k][g], other[k][g]).astype(f32)
            high = jnp.where(first, other[g][k], mine[g][k]).astype(f32)
            y_low, y_high = turn(scalar_ref[GROUPS + 6], far), turn(scalar_ref[GROUPS + 12], far)
            down_ref[pl.ds(pl.multiple_of(lines * y_low, 16), lines), :] = low[:lines]
            up_ref[pl.ds(pl.multiple_of(lines * y_high, 16), lines), :] = high[:lines]
            at = extra * (GROUPS * z_low + y_low)
            out_ref[pl.ds(pl.multiple_of(at, 16), extra), :] = low[lines:]
            at = half + extra * (GROUPS * z_high + y_high)
            out_ref[pl.ds(pl.multiple_of(at, 16), extra), :] = high[lines:]

    for g in range(GROUPS):
        pl.when(pl.program_id(0) == g)(functools.partial(unpack, g))


def unpack_feed(scalar, mine, other, width, hidden):
    block = pl.BlockSpec(mine[0].shape, lambda g, s: (0, 0, 0))
    return grid_call(
        unpack_feed_kernel,
        "unpack_feed",
        scalar,
        GROUPS,
        [block] * (2 * GROUPS),
        [
            pl.BlockSpec((width, width), lambda g, s: (s[GROUPS + 12 + g], 0)),
            pl.BlockSpec((width, width), lambda g, s: (0, s[GROUPS + 8 + g])),
            pl.BlockSpec((width, width), lambda g, s: (0, 0)),
        ],
        [sds((hidden, width), f32), sds((width, hidden), f32), sds((width, width), f32)],
        [*mine, *other],
    )


def unpack_rest_kernel(scalar_ref, mine_ref, other_ref, out_ref, pos_ref, vec_ref):
    core = scalar_ref[GROUPS + 4]
    half = out_ref.shape[0] // 2
    width = out_ref.shape[1] // 3
    rows = pos_ref.shape[0] // 2
    chunk = mine_ref.shape[0] // GROUPS
    for kept, ref in ((core, mine_ref), (1 - core, other_ref)):
        lines = pl.ds(pl.multiple_of(kept * half, half), half)
        for j in range(GROUPS):
            for w in range(3):
                lanes = slice(w * width + 128 * j, w * width + 128 * (j + 1))
                block = ref[chunk * j : chunk * (j + 1), :, 128 * w : 128 * (w + 1)]
                out_ref[lines, lanes] = block.reshape(half, 128).astype(f32)
        tail = ref[:, :, 3 * 128 :].astype(f32).reshape(-1, 128)
        lines = pl.ds(pl.multiple_of(kept * rows, 8), rows)
        blocks = width // 128
        for i in range(blocks):
            pos_ref[lines, 128 * i : 128 * (i + 1)] = tail[rows * i : rows * (i + 1)]
            if ref is mine_ref:
                vec_ref[:, 128 * i : 128 * (i + 1)] = tail[rows * blocks + 16 * i : rows * blocks + 16 * (i + 1)]


def unpack_rest(scalar, mine, other, rows, width):
    return call(
        unpack_rest_kernel,
        "unpack_rest",
        scalar,
        [mine, other],
        [sds((width, 3 * width), f32), sds((rows, width), f32), sds((16, width), f32)],
    )


def shift(array, axis, step):
    size = lax.axis_size(axis)
    return lax.ppermute(array, axis, [(i, (i + step) % size) for i in range(size)])


def peers(array, axis):
    return [shift(array, axis, step) for step in (1, 3, 2)]


def swap(array):
    return shift(array, "core", 1)


def total(parts):
    return functools.reduce(jnp.add, [p.astype(f32) for p in parts])


SPACE = ("x", "z", "y")
PLANE = ("z", "y", "core")


def step_plane(array, step, near):
    sizes = [lax.axis_size(name) for name in PLANE]
    pairs = []
    for z in range(sizes[0]):
        for y in range(sizes[1]):
            for core in range(sizes[2]):
                if (core == 0) == near:
                    target = (z, (y + step) % sizes[1], core)
                else:
                    target = ((z + step) % sizes[0], y, core)
                index = lambda p: (p[0] * sizes[1] + p[1]) * sizes[2] + p[2]
                pairs.append((index((z, y, core)), index(target)))
    return lax.ppermute(array, PLANE, pairs)


def step_cores(array):
    size = lax.axis_size("x")
    pairs = []
    for core in range(2):
        for x in range(size):
            pairs.append((core * size + x, core * size + (x + 1 - 2 * core) % size))
    return lax.ppermute(array, ("core", "x"), pairs)


def plane_peers(array, near):
    return [step_plane(array, step, near) for step in (2, 1, 3)]


def exchange(array, axes):
    return lax.all_to_all(array, axes, 0, 0, tiled=True)


def body(
    vis,
    keep_slots,
    counts,
    band_mask,
    mask_token,
    pos,
    ln1_gain,
    ln1_bias,
    w_qkv,
    b_query,
    b_value,
    w_out,
    b_out,
    ln2_gain,
    ln2_bias,
    w_up,
    b_up,
    w_down,
    b_down,
    d_out,
):
    barrier = lax.optimization_barrier
    x = lax.axis_index("x")
    core = lax.axis_index("core")
    piece = keep_slots.shape[1]
    rows, width = pos.shape
    half = rows // 2
    hidden = w_up.shape[1]

    vis = vis[0]

    y, z = lax.axis_index("y"), lax.axis_index("z")
    relative, far = jnp.array(RELATIVE, jnp.int32), jnp.array(OPPOSITE, jnp.int32)
    order = (x + relative) % GROUPS
    live = jnp.sum(jnp.where(order[:, None] == jnp.arange(GROUPS)[None, :], band_mask, 0), axis=1)
    here = (x * lax.axis_size("z") + z) * lax.axis_size("y") + y
    chunks = width // 128 * half // 16
    shared = (here >= chunks) & (here < chunks + width // 128)
    scalar = jnp.concatenate(
        [live, order * rows, jnp.stack([core, shared.astype(jnp.int32), y, z]), (z + far) % GROUPS, (x + far) % GROUPS]
    ).astype(jnp.int32)
    pack = lambda *vs: jnp.pad(jnp.stack(vs), ((0, 8 - len(vs)), (0, 0)))
    vectors = pack(mask_token, ln1_gain, ln1_bias, b_query, b_value)
    feed_vectors = pack(b_out, ln2_gain, ln2_bias, b_down)

    index = lax.broadcasted_iota(jnp.int32, (1, piece), 1)
    code = jnp.where(index < counts, keep_slots, -1) + 1
    marks = jnp.concatenate([code // 64, code % 64], axis=0).astype(bf)
    marks = jnp.pad(marks, ((0, MARKS - 2), (0, width - piece)))
    message = jnp.concatenate([marks, vis], axis=0)
    pieces = [message] + [shift(message, "x", step) for step in (2, 1, 3)]
    pos_half = lax.dynamic_slice(pos, (half * core, 0), (half, width))
    pos_mine = [step_cores(pos), shift(pos_half, "x", 2)]
    scalar, vectors, feed_vectors, pieces = barrier((scalar, vectors, feed_vectors, pieces))
    start, normed, aux, *bases = front(scalar, pieces, pos, vectors)
    q, turned_own, k_own, v_own, *state, p_own = attention_own(scalar, normed, vectors, w_qkv)
    state, pos_mine = barrier((state, pos_mine))
    pos_other = [swap(p) for p in pos_mine]
    out = middle(scalar, bases, pos_mine + pos_other, vectors, w_qkv, q, state)
    rest, (mixed, lse), kept = out[: 3 * (GROUPS - 1)], out[3 * (GROUPS - 1) :][:2], out[3 * (GROUPS - 1) + 2 :]
    keys, values = [k_own, *rest[1::3]], [v_own, *rest[2::3]]
    weights, peaks = [p_own, *kept[0::2]], [state[0], *kept[1::2]]

    out, middle_rows, second, kept, sent, grad_b_up = feed_forward(
        scalar, mixed, start, d_out[0], w_out, feed_vectors, w_up, b_up[None], w_down
    )
    got = swap(sent)
    grad_middle, grad_mixed, out_kept, out_sent, feed_vec = feed_backward(
        scalar, mixed, middle_rows, second, d_out[0], w_out, feed_vectors
    )
    factors = softmax_factors(scalar, mixed, grad_mixed, lse, peaks)
    inputs = list(zip(factors[:GROUPS], weights, keys, values, factors[GROUPS:]))
    feed = fold_feed(scalar, kept, got, out_kept, swap(out_sent))
    inputs, feed = barrier((inputs, feed))
    feed = [feed[0]] + [step_plane(feed[r], r, True) for r in (1, 2, 3)]
    dq, d_3, part = attention_grad(scalar, (3,), q, w_qkv, [inputs[3]], None)
    dq, part = barrier((dq, part))
    from_3 = shift(part, "x", 2)
    dq, d_1, part = attention_grad(scalar, (1,), q, w_qkv, [inputs[1]], dq)
    feed = fold_line(scalar, feed)
    dq, part, feed = barrier((dq, part, feed))
    feed = [feed[0]] + [shift(feed[r], "x", r) for r in (2, 1, 3)]
    from_1 = shift(part, "x", 3)
    dq, d_2, part = attention_grad(scalar, (2,), q, w_qkv, [inputs[2]], dq)
    feed = add_up(scalar, "fold_point", feed)
    dq, part, from_3, feed = barrier((dq, part, from_3, feed))
    feed_peers = plane_peers(feed, False)
    from_2 = shift(part, "x", 1)
    part, at_kept, at_sent, grad_b_query, grad_b_value = attention_grad(
        scalar, (0,), q, w_qkv, [inputs[0]], dq, [turned_own, *rest[0::3], d_3, d_1, d_2]
    )
    at_kept, at_sent, part, from_1, from_2, feed_peers = barrier(
        (at_kept, at_sent, part, from_1, from_2, feed_peers)
    )

    at_got = swap(at_sent)
    feed = add_up(scalar, "sum_line", [feed] + feed_peers)
    gathered = [shift(feed, "x", step) for step in (2, 1, 3)]
    tail_kept, tail_sent, low = finish(
        scalar,
        part,
        (from_3, from_1, from_2),
        start,
        grad_middle,
        vectors,
        aux,
        grad_b_query,
        grad_b_value,
        feed_vec,
        grad_b_up,
    )
    spread = lambda a: a.reshape(GROUPS * SPREAD, 16, -1)
    bundle = fold_rest(scalar, spread(at_kept), spread(at_got), tail_kept, swap(tail_sent))
    bundle, feed = barrier((bundle, jnp.stack([feed] + gathered)))
    bundle = exchange(bundle, SPACE)
    feed_other = [swap(feed)]
    feed = [feed] + plane_peers(feed, True)
    bundle, shares, feed_other = barrier((bundle, share(scalar, low, aux, piece), feed_other))
    bundle = sum_space(scalar, bundle)
    feed, _ = barrier((feed, bundle))
    rest_mine = exchange(bundle, SPACE)
    feed_other += [swap(a) for a in feed[1:]]
    feed_other[1], shares = barrier((feed_other[1], shares))
    returned = [shares[0], shift(shares[3], "x", 1), shift(shares[2], "x", 3), shift(shares[1], "x", 2)]
    grad_w_down, grad_w_up, grad_w_out = unpack_feed(scalar, feed, feed_other, width, hidden)
    grad_vis = collect(scalar, aux, returned, rows, piece)
    rest_mine, grad_w_down, grad_vis = barrier((rest_mine, grad_w_down, grad_vis))
    rest_other = swap(rest_mine)
    grad_w_qkv, grad_pos, sums = unpack_rest(scalar, rest_mine, rest_other, rows, width)

    return (
        out[None],
        grad_vis[None],
        sums[0],
        grad_pos,
        sums[1],
        sums[2],
        grad_w_qkv,
        sums[3],
        sums[4],
        grad_w_out,
        sums[5],
        sums[6],
        sums[7],
        grad_w_up,
        sums[9 : 9 + hidden // width].reshape(hidden),
        grad_w_down,
        sums[8],
    )


CUBE = ("z", "y", "core")


def solution(mesh):
    fine = Mesh(mesh.devices.reshape(4, 4, 2, 4), ("z", "y", "core", "x"))
    return jax.shard_map(
        body,
        mesh=fine,
        in_specs=(
            P(CUBE, "x", None),
            P(CUBE, "x"),
            P(CUBE, "x"),
            P(CUBE, None),
            P(),
            P("x", None),
        )
        + (P(),) * 13
        + (P(CUBE, "x", None),),
        out_specs=(P(CUBE, "x", None), P(CUBE, "x", None), P(), P("x", None)) + (P(),) * 13,
        check_vma=False,
    )
```

```python
import functools

import jax
import jax.numpy as jnp
from jax import lax
from jax.experimental import pallas as pl
from jax.experimental.pallas import tpu as pltpu
from jax.sharding import Mesh, PartitionSpec as P

bf = jnp.bfloat16
f32 = jnp.float32

HEADS = 16
DEPTH = 32
QUAD = 4
GROUPS = 4
LOG2E = 1.4426950408889634
SCALE = DEPTH**-0.5
EPS = 1e-05
BIG = 1e30
GELU_SCALE = 0.7978845608028654
GELU_CUBE = 0.044715
RELATIVE = (0, 3, 1, 2)
OPPOSITE = (0, 2, 3, 1)
CAP = 80
MARKS = 16
SPREAD = 16

NT = (((1,), (1,)), ((), ()))
NN = (((1,), (0,)), ((), ()))
TN = (((0,), (0,)), ((), ()))
VMEM_LIMIT = 56 * 1024 * 1024


def dg(a, b, dims):
    return lax.dot_general(a, b, dims, preferred_element_type=f32)


def sds(shape, dtype):
    return jax.ShapeDtypeStruct(shape, dtype)


def call(kernel, name, scalar, operands, out_shape, scratch=(), aliases=None, limit=5, micro=0.001):
    inside = pl.BlockSpec(memory_space=pltpu.VMEM)
    return pl.pallas_call(
        kernel,
        in_specs=[pl.BlockSpec(memory_space=pltpu.SMEM)] + [inside] * len(operands),
        out_specs=[inside] * len(out_shape),
        out_shape=out_shape,
        scratch_shapes=list(scratch),
        compiler_params=pltpu.CompilerParams(vmem_limit_bytes=limit * 1024 * 1024),
        cost_estimate=pl.CostEstimate(flops=int(micro * 1e9), bytes_accessed=1000, transcendentals=0),
        input_output_aliases=aliases or {},
        name=name,
    )(scalar, *operands)


def grid_call(kernel, name, scalar, steps, in_specs, out_specs, out_shape, operands):
    return pl.pallas_call(
        kernel,
        grid_spec=pltpu.PrefetchScalarGridSpec(
            num_scalar_prefetch=1, grid=(steps,), in_specs=in_specs, out_specs=out_specs
        ),
        out_shape=out_shape,
        compiler_params=pltpu.CompilerParams(vmem_limit_bytes=32 * 1024 * 1024),
        cost_estimate=pl.CostEstimate(flops=1000, bytes_accessed=1000, transcendentals=0),
        name=name,
    )(scalar, *operands)


def column_sum(tensor):
    return jnp.sum(tensor.astype(f32), axis=0, keepdims=True)


def norm_parts(values):
    centered = values - jnp.mean(values, axis=-1, keepdims=True)
    variance = jnp.mean(centered * centered, axis=-1, keepdims=True)
    inverse = lax.rsqrt(variance + EPS)
    return centered * inverse, inverse


def norm_pull(grad, n, inverse, gain):
    g = grad * gain
    return inverse * (
        g - jnp.mean(g, axis=-1, keepdims=True) - n * jnp.mean(g * n, axis=-1, keepdims=True)
    )


def place_rows(base, pieces, ids, rows, rows_ref):
    piece, width = ids[0].shape[1], rows_ref.shape[1]
    slot = lax.broadcasted_iota(jnp.int32, (rows, piece), 0) + base
    placed = jnp.zeros((rows, width), f32)
    seen = jnp.zeros((rows, 1), f32)
    for v, i in zip(pieces, ids):
        hot = (slot == i).astype(f32)
        seen += jnp.sum(hot, axis=1, keepdims=True)
        placed += dg(hot.astype(bf), v[MARKS : MARKS + piece, :], NN)
    unseen = 1.0 - seen
    return placed + unseen * rows_ref[0:1], unseen


def first_norm(start, rows_ref):
    n, _ = norm_parts(start)
    return (n * rows_ref[1:2] + rows_ref[2:3]).astype(bf)


def keys_values(normed, rows_ref, w_ref, turned_ref, k_ref, v_ref):
    width = normed.shape[1]
    k_ref[...] = dg(normed, w_ref[:, width : 2 * width], NN).astype(bf)
    v_ref[...] = (dg(normed, w_ref[:, 2 * width :], NN) + rows_ref[4:5]).astype(bf)
    turned_ref[...] = normed.T


def stack_heads(x):
    lane = lax.broadcasted_iota(jnp.int32, x.shape, 1) // DEPTH
    return jnp.concatenate([jnp.where(lane == h, x, jnp.zeros_like(x)) for h in range(QUAD)], axis=0)


def unstack_heads(xt):
    rows = xt.shape[1] // QUAD
    parts = [xt[DEPTH * h : DEPTH * (h + 1), rows * h : rows * (h + 1)] for h in range(QUAD)]
    return jnp.concatenate(parts, axis=0).T


def fwd_steps(steps, scalar_ref, query, key, value, state, keep_weights, finish):
    stacked = {}

    def scores(quad, group):
        if quad not in stacked:
            stacked[quad] = stack_heads(query(quad))
        return dg(key(quad, group), stacked[quad], NT)

    ahead = scores(*steps[0])
    for i, (quad, group) in enumerate(steps):
        s = ahead
        if i + 1 < len(steps):
            ahead = scores(*steps[i + 1])
        live = scalar_ref[group] > 0
        peak = jnp.where(live, jnp.max(s, axis=0, keepdims=True), -BIG)
        old = state(quad) if i == 0 or steps[i - 1][0] != quad else new
        if old is not None:
            peak = jnp.maximum(old[0], peak)
        p = jnp.exp2(s - jnp.where(live, peak, BIG)).astype(bf)
        keep_weights(quad, group, p, peak)
        v = value(quad, group)
        turned = jnp.concatenate([v.T, jnp.ones((16, v.shape[0]), bf)], axis=0)
        both = dg(turned, p, NN)
        o, l = both[: v.shape[1]], both[v.shape[1] : v.shape[1] + 1]
        if old is not None:
            keep = jnp.exp2(old[0] - peak)
            o += old[2] * keep
            l += old[1] * keep
        new = (peak, l, o)
        if i + 1 == len(steps) or steps[i + 1][0] != quad:
            finish(quad, new)


def quad_at(quad):
    return (slice(None), slice(128 * quad, 128 * (quad + 1)))


def front_kernel(scalar_ref, *refs):
    pieces, (rows_ref, aux_ref), bases = refs[:GROUPS], refs[GROUPS : GROUPS + 2], refs[GROUPS + 2 :]
    rows = bases[0].shape[0]
    piece = pieces[0].shape[0] - MARKS
    ids = []
    for i, v in enumerate(pieces):
        marks = v[:MARKS, :].astype(f32)[:8, :piece]
        line = marks[0:1] * 64.0 + marks[1:2] - 1.0
        aux_ref[rows + i : rows + i + 1, :piece] = line
        ids.append(line.astype(jnp.int32))
    for g, base in enumerate(bases):
        base[...], unseen = place_rows(scalar_ref[GROUPS + g], pieces, ids, rows, rows_ref)
        if g == 0:
            aux_ref[:rows, :128] = jnp.broadcast_to(unseen, (rows, 128))


def read_slots(aux_ref, count, piece):
    rows = aux_ref.shape[0] - 8
    return [aux_ref[rows + i : rows + i + 1, :piece].astype(jnp.int32) for i in range(count)]


def front(scalar, pieces, vectors, rows):
    width = vectors.shape[1]
    return call(
        front_kernel,
        "front",
        scalar,
        [*pieces, vectors],
        [sds((rows + 8, 256), f32)] + [sds((rows, width), f32)] * GROUPS,
        micro=4,
    )


def attention_own_kernel(
    scalar_ref,
    base_ref,
    pos_ref,
    rows_ref,
    w_ref,
    start_ref,
    q_ref,
    turned_ref,
    k_ref,
    v_ref,
    m_ref,
    l_ref,
    o_ref,
    p_ref,
):
    start = base_ref[...] + pos_ref[...].astype(f32)
    start_ref[...] = start
    normed = first_norm(start, rows_ref)
    width = normed.shape[1]
    q_ref[...] = ((dg(normed, w_ref[:, :width], NN) + rows_ref[3:4]) * (SCALE * LOG2E)).astype(bf)
    keys_values(normed, rows_ref, w_ref, turned_ref, k_ref, v_ref)

    def keep_weights(quad, group, p, peak):
        p_ref[quad] = p

    def finish(quad, state):
        m_ref[quad], l_ref[quad], o_ref[quad] = state

    fwd_steps(
        [(quad, 0) for quad in range(m_ref.shape[0])],
        scalar_ref,
        lambda quad: q_ref[quad_at(quad)],
        lambda quad, group: k_ref[quad_at(quad)],
        lambda quad, group: v_ref[quad_at(quad)],
        lambda quad: None,
        keep_weights,
        finish,
    )


def attention_own(scalar, base, pos, vectors, w_qkv):
    rows, width = pos.shape
    quads, n = width // 128, rows * QUAD
    return call(
        attention_own_kernel,
        "attention_own",
        scalar,
        [base, pos, vectors, w_qkv],
        [
            sds((rows, width), f32),
            sds((rows, width), bf),
            sds((width, rows), bf),
            sds((rows, width), bf),
            sds((rows, width), bf),
            sds((quads, 1, n), f32),
            sds((quads, 1, n), f32),
            sds((quads, 128, n), f32),
            sds((quads, rows, n), bf),
        ],
        limit=7,
        micro=5,
    )


def middle_kernel(scalar_ref, *refs):
    bases, refs = refs[: GROUPS - 1], refs[GROUPS - 1 :]
    pos_refs, refs = refs[:4], refs[4:]
    rows_ref, w_ref, q_ref, m_ref, l_ref, o_ref, *refs = refs
    groups, (mixed_ref, lse_ref), kept = refs[: 3 * (GROUPS - 1)], refs[3 * (GROUPS - 1) :][:2], refs[3 * (GROUPS - 1) + 2 :]
    first = scalar_ref[GROUPS + GROUPS] == 0
    near, far, other_near, other_far = [ref[...].astype(f32) for ref in pos_refs]
    for g, base in enumerate(bases):
        if g < 2:
            pos = jnp.where(first == (g == 0), near, other_near)
        else:
            pos = jnp.concatenate([jnp.where(first, far, other_far), jnp.where(first, other_far, far)], axis=0)
        keys_values(first_norm(base[...] + pos, rows_ref), rows_ref, w_ref, *groups[3 * g : 3 * g + 3])

    def keep_weights(quad, group, p, peak):
        kept[2 * group - 2][quad] = p
        kept[2 * group - 1][quad] = peak

    def finish(quad, state):
        m, l, o = state
        mixed_ref[quad_at(quad)] = unstack_heads(o / l).astype(bf)
        lse_ref[quad] = m + jnp.log2(l)

    fwd_steps(
        [(quad, group) for quad in range(m_ref.shape[0]) for group in range(1, GROUPS)],
        scalar_ref,
        lambda quad: q_ref[quad_at(quad)],
        lambda quad, group: groups[3 * group - 2][quad_at(quad)],
        lambda quad, group: groups[3 * group - 1][quad_at(quad)],
        lambda quad: (m_ref[quad], l_ref[quad], o_ref[quad]),
        keep_weights,
        finish,
    )


def middle(scalar, bases, pos, vectors, w_qkv, q, state):
    rows, width = q.shape
    quads, n = width // 128, rows * QUAD
    group = [sds((width, rows), bf), sds((rows, width), bf), sds((rows, width), bf)]
    return call(
        middle_kernel,
        "middle",
        scalar,
        [*bases, *pos, vectors, w_qkv, q, *state],
        [*(group * (GROUPS - 1)), sds((rows, width), bf), sds((quads, 1, n), f32)]
        + [sds((quads, rows, n), bf), sds((quads, 1, n), f32)] * (GROUPS - 1),
        limit=9,
    )


def bwd_kernel(scalar_ref, q_ref, w_ref, *refs, groups, carried):
    width = q_ref.shape[1]
    inputs, refs = [refs[5 * i : 5 * i + 5] for i in range(len(groups))], refs[5 * len(groups) :]
    if carried:
        dq_in, *refs = refs
    own = groups == (0,)
    if own:
        *turned_refs, d_3, d_1, d_2, part_ref, kept_ref, sent_ref, bq_ref, bv_ref, d_s = refs
        base, outs = width, [(d_s, part_ref)]
    else:
        dq_ref, *refs = refs
        base, outs = 0, [refs[2 * i : 2 * i + 2] for i in range(len(groups))]
    quads = width // 128
    for j in range(quads):
        at = quad_at(j)
        qs = stack_heads(q_ref[at])
        dq = dq_in[at] if carried else None
        for (do_ref, p_ref, k_ref, v_ref, delta_ref), (d_ref, _) in zip(inputs, outs):
            columns = lambda i: (
                slice(None),
                slice(base + (i - 1) * width + 128 * j, base + (i - 1) * width + 128 * (j + 1)),
            )
            dos = stack_heads(do_ref[at])
            k, p = k_ref[at], p_ref[j]
            ds = (p.astype(f32) * (dg(v_ref[at], dos, NT) - delta_ref[j])).astype(bf)
            d_ref[columns(2)] = dg(p, dos, NN).astype(bf)
            d_ref[columns(1)] = (dg(ds, qs, NN) * (1.0 / LOG2E)).astype(bf)
            term = unstack_heads(dg(k, ds, TN))
            dq = term if dq is None else dq + term
        if own:
            d_s[at] = (dq * SCALE).astype(bf)
        else:
            dq_ref[at] = dq
    for d_ref, part_ref in outs:
        grads = d_ref[...]
        part_ref[...] = dg(grads, w_ref[...] if own else w_ref[:, width:], NT).astype(part_ref.dtype)
    if not own:
        return
    own, *rest = turned_refs
    g = dg(own[...], grads[:, width:], NN)
    bv = column_sum(grads[:, 2 * width :])
    for turned, d_ref in zip(rest, (d_1, d_2, d_3)):
        d = d_ref[...]
        g += dg(turned[...], d, NN)
        bv += column_sum(d[:, width:])
    bv_ref[...] = bv
    bq_ref[...] = column_sum(grads[:, :width])
    gq = dg(own[...], grads[:, :width], NN)
    first = scalar_ref[GROUPS + 4] == 0
    half = width // 2
    for j in range(quads):
        at = slice(128 * j, 128 * (j + 1))
        block = jnp.concatenate([gq[:, at], g[:, at], g[:, width + 128 * j : width + 128 * (j + 1)]], axis=1)
        kept_ref[j] = jnp.where(first, block[:half], block[half:]).astype(bf)
        sent_ref[j] = jnp.where(first, block[half:], block[:half]).astype(bf)


def attention_grad(scalar, groups, q, w_qkv, inputs, dq, more=()):
    rows, width = q.shape
    quads = width // 128
    operands = [q, w_qkv] + [a for group in inputs for a in group]
    aliases = {}
    if dq is not None:
        aliases = {len(operands) + 1: 0}
        operands.append(dq)
    operands += list(more)
    scratch = []
    if groups == (0,):
        packed = (quads, width // 2, 3 * 128)
        out_shape = [sds((rows, width), f32)] + [sds(packed, bf)] * 2 + [sds((1, width), f32)] * 2
        scratch = [pltpu.VMEM((rows, 3 * width), bf)]
    else:
        out_shape = [sds((rows, width), f32)]
        out_shape += [sds((rows, 2 * width), bf), sds((rows, width), bf)] * len(groups)
    return call(
        functools.partial(bwd_kernel, groups=groups, carried=dq is not None),
        "attention_grad_" + "_".join(str(g) for g in groups),
        scalar,
        operands,
        out_shape,
        scratch,
        aliases,
    )


def feed_kernel(
    scalar_ref,
    mixed_ref,
    start_ref,
    dout_ref,
    wout_ref,
    rows_ref,
    wup_ref,
    bup_ref,
    wdown_ref,
    out_ref,
    middle_ref,
    second_ref,
    kept_ref,
    sent_ref,
    gbup_ref,
):
    first = scalar_ref[GROUPS + 4] == 0
    width = mixed_ref.shape[1]
    hidden = wup_ref.shape[1]
    dout = dout_ref[...]
    middle = start_ref[...] + (dg(mixed_ref[...], wout_ref[...], NN) + rows_ref[0:1])
    middle_ref[...] = middle
    n, _ = norm_parts(middle)
    normed = (n * rows_ref[1:2] + rows_ref[2:3]).astype(bf)
    turned = normed.T
    result = middle + rows_ref[3:4]
    second = jnp.zeros_like(middle)
    lines = hidden // SPREAD
    for h in range(hidden // width):
        at = slice(width * h, width * (h + 1))
        u = dg(normed, wup_ref[:, at], NN) + bup_ref[:, at]
        square = u * u
        t = jnp.tanh(u * (GELU_SCALE + (GELU_SCALE * GELU_CUBE) * square))
        near = 0.5 + 0.5 * t
        act = (u * near).astype(bf)
        result += dg(act, wdown_ref[at, :], NN)
        slope = near + u * (0.5 - 0.5 * (t * t)) * (GELU_SCALE + (3.0 * GELU_SCALE * GELU_CUBE) * square)
        gup = (dg(dout, wdown_ref[at, :], NT) * slope).astype(bf)
        second += dg(gup, wup_ref[:, at], NT)
        gbup_ref[:, at] = column_sum(gup)
        down = dg(act, dout, TN).astype(bf)
        up = dg(turned, gup, NN).astype(bf)
        chunks = (width // lines, lines, width)
        places = slice(h * chunks[0], (h + 1) * chunks[0])
        kept_ref[places] = jnp.where(first, down, up).reshape(chunks)
        sent_ref[places] = jnp.where(first, up, down).reshape(chunks)
    out_ref[...] = result.astype(bf)
    second_ref[...] = second


def feed_backward_kernel(
    scalar_ref,
    mixed_ref,
    middle_ref,
    second_ref,
    dout_ref,
    wout_ref,
    rows_ref,
    gmid_ref,
    gmix_ref,
    kept_ref,
    sent_ref,
    vec_ref,
):
    first = scalar_ref[GROUPS + 4] == 0
    mixed = mixed_ref[...]
    width = mixed.shape[1]
    second = second_ref[...]
    grad = dout_ref[...].astype(f32)
    n, inverse = norm_parts(middle_ref[...])
    gmid = grad + norm_pull(second, n, inverse, rows_ref[1:2])
    gmid_ref[...] = gmid
    branch = gmid.astype(bf)
    gmix_ref[...] = dg(branch, wout_ref[...], NT).astype(bf)
    wout = dg(mixed, branch, TN)
    half = width // 2
    extra = (SPREAD, half // SPREAD, width)
    kept_ref[...] = jnp.where(first, wout[:half], wout[half:]).astype(bf).reshape(extra)
    sent_ref[...] = jnp.where(first, wout[half:], wout[:half]).astype(bf).reshape(extra)
    vec_ref[...] = jnp.concatenate(
        [
            column_sum(branch),
            column_sum(second * n),
            column_sum(second),
            column_sum(grad),
            jnp.zeros((4, width), f32),
        ],
        axis=0,
    )


def factor_kernel(scalar_ref, mixed_ref, gmix_ref, lse_ref, *refs):
    peaks, outs = refs[:GROUPS], refs[GROUPS:]
    gmix = gmix_ref[...].astype(f32)
    width = gmix.shape[1]
    product = mixed_ref[...].astype(f32) * gmix
    head = lax.broadcasted_iota(jnp.int32, (HEADS, width), 0)
    lane = lax.broadcasted_iota(jnp.int32, (HEADS, width), 1) // DEPTH
    pick = (head == lane).astype(bf)
    halves = lambda a: (a.astype(bf), (a - a.astype(bf).astype(f32)).astype(bf))
    high, low = halves(product)
    delta = dg(pick, high, NT) + dg(pick, low, NT)
    rows = delta.shape[1]
    for peak_ref, do_ref, delta_ref in zip(peaks, outs[:GROUPS], outs[GROUPS:]):
        lines = []
        for j in range(HEADS // QUAD):
            factor = jnp.exp2(peak_ref[j] - lse_ref[j])
            delta_ref[j] = factor * jnp.concatenate([delta[QUAD * j + i : QUAD * j + i + 1] for i in range(QUAD)], axis=1)
            lines += [factor[:, rows * i : rows * (i + 1)] for i in range(QUAD)]
        high, low = halves(jnp.concatenate(lines, axis=0))
        do_ref[...] = (gmix * (dg(high, pick, TN) + dg(low, pick, TN))).astype(bf)


def feed_forward(scalar, mixed, start, d_out, w_out, vectors, w_up, b_up, w_down):
    rows, width = mixed.shape
    hidden = w_up.shape[1]
    packed = (SPREAD, hidden // SPREAD, width)
    return call(
        feed_kernel,
        "feed_forward",
        scalar,
        [mixed, start, d_out, w_out, vectors, w_up, b_up, w_down],
        [sds((rows, width), bf)] + [sds((rows, width), f32)] * 2 + [sds(packed, bf)] * 2 + [sds((1, hidden), f32)],
        limit=8,
    )


def feed_backward(scalar, mixed, middle, second, d_out, w_out, vectors):
    rows, width = mixed.shape
    packed = (SPREAD, width // 2 // SPREAD, width)
    return call(
        feed_backward_kernel,
        "feed_backward",
        scalar,
        [mixed, middle, second, d_out, w_out, vectors],
        [sds((rows, width), f32), sds((rows, width), bf), sds(packed, bf), sds(packed, bf), sds((8, width), f32)],
    )


def softmax_factors(scalar, mixed, gmix, lse, peaks):
    return call(
        factor_kernel,
        "softmax_factors",
        scalar,
        [mixed, gmix, lse, *peaks],
        [sds(gmix.shape, bf)] * GROUPS + [sds(lse.shape, f32)] * GROUPS,
        micro=2,
    )


def turn(place, steps):
    return lax.rem(place + steps, GROUPS)


def fold_feed_kernel(scalar_ref, a, b, c, d, *outs):
    first, y, z = scalar_ref[GROUPS + 4] == 0, scalar_ref[GROUPS + 6], scalar_ref[GROUPS + 7]
    near = jnp.where(first, y, z)
    lines = a.shape[1]
    for r, out_ref in enumerate(outs):
        place = turn(near, r)
        for i in range(GROUPS):
            at = jnp.where(first, GROUPS * i + place, GROUPS * place + i)
            out_ref[i, :lines] = a[at] + b[at]
            out_ref[i, lines:] = c[at] + d[at]


def fold_feed(scalar, a, b, c, d):
    shape = sds((GROUPS, a.shape[1] + c.shape[1], a.shape[2]), bf)
    return call(fold_feed_kernel, "fold_feed", scalar, [a, b, c, d], [shape] * GROUPS)


def fold_line_kernel(scalar_ref, *refs):
    sources, outs = refs[:GROUPS], refs[GROUPS:]
    for r, out_ref in enumerate(outs):
        at = turn(scalar_ref[GROUPS + 12], r)
        out_ref[...] = sum(ref[at].astype(f32) for ref in sources).astype(bf)


def fold_line(scalar, sources):
    return call(fold_line_kernel, "fold_line", scalar, sources, [sds(sources[0].shape[1:], bf)] * GROUPS)


def add_up_kernel(scalar_ref, *refs):
    *sources, out_ref = refs
    out_ref[...] = sum(ref[...].astype(f32) for ref in sources).astype(bf)


def add_up(scalar, name, arrays):
    return call(add_up_kernel, name, scalar, list(arrays), [sds(arrays[0].shape, bf)])[0]


def fold_rest_kernel(scalar_ref, a, b, c, d, out_ref):
    cut = a.shape[2]
    out_ref[:, :, :cut] = a[...] + b[...]
    out_ref[:, :, cut:] = c[...] + d[...]


def fold_rest(scalar, a, b, c, d):
    shape = a.shape[:2] + (a.shape[2] + c.shape[2],)
    return call(fold_rest_kernel, "fold_rest", scalar, [a, b, c, d], [sds(shape, bf)])[0]


def sum_space_kernel(scalar_ref, got_ref, out_ref):
    chunk = got_ref.shape[0] // GROUPS
    lanes = 3 * 128
    sums = []
    for x in range(GROUPS):
        acc = got_ref[chunk * x].astype(f32)
        for i in range(1, chunk):
            acc += got_ref[chunk * x + i].astype(f32)
        sums.append(acc)
    everything = functools.reduce(jnp.add, sums)
    shared = scalar_ref[GROUPS + 5] > 0
    for x in range(GROUPS):
        tail = jnp.where(shared, everything[:, lanes:], sums[x][:, lanes:])
        block = jnp.concatenate([everything[:, :lanes], tail], axis=1).astype(bf)
        for i in range(chunk):
            out_ref[chunk * x + i] = block


def sum_space(scalar, got):
    return call(sum_space_kernel, "sum_space", scalar, [got], [sds(got.shape, bf)])[0]


def finish_kernel(
    scalar_ref,
    part_ref,
    r3,
    r1,
    r2,
    start_ref,
    gmid_ref,
    rows_ref,
    unseen_ref,
    bq_ref,
    bv_ref,
    feed_ref,
    bup_ref,
    kept_ref,
    sent_ref,
    low_hbm,
    low_ref,
    sem,
):
    rows, width = start_ref.shape
    first_grad = part_ref[...] + r3[...].astype(f32) + r1[...].astype(f32) + r2[...].astype(f32)
    n, inverse = norm_parts(start_ref[...])
    grad = gmid_ref[...] + norm_pull(first_grad, n, inverse, rows_ref[1:2])
    low_ref[...] = grad.astype(bf)
    copy = pltpu.make_async_copy(low_ref, low_hbm, sem)
    copy.start()
    half = rows // 2
    first = scalar_ref[GROUPS + 4] == 0
    top, low = grad[:half], grad[half:]
    lines = [
        column_sum(unseen_ref[:rows, :1] * grad),
        column_sum(first_grad * n),
        column_sum(first_grad),
        bq_ref[...],
        bv_ref[...],
        feed_ref[:4],
    ]
    blocks = bup_ref.shape[1] // width
    lines += [bup_ref[:, width * i : width * (i + 1)] for i in range(blocks)]
    spare = 16 - sum(a.shape[0] for a in lines)
    lines = jnp.concatenate(lines + [jnp.zeros((spare, width), f32)], axis=0)

    def narrow(values):
        cut = [a[:, 128 * i : 128 * (i + 1)] for a in (values, lines) for i in range(width // 128)]
        cut.append(jnp.zeros((kept_ref.shape[0] * kept_ref.shape[1] - sum(a.shape[0] for a in cut), 128), f32))
        return jnp.concatenate(cut, axis=0).reshape(kept_ref.shape).astype(bf)

    kept_ref[...] = narrow(jnp.where(first, top, low))
    sent_ref[...] = narrow(jnp.where(first, low, top))
    copy.wait()


def finish(scalar, part, received, start, gmid, vectors, unseen, bq, bv, feed_vec, grad_b_up):
    rows, width = start.shape
    tail = sds((GROUPS * SPREAD, 16, 128), bf)
    operands = [part, *received, start, gmid, vectors, unseen, bq, bv, feed_vec, grad_b_up]
    inside = pl.BlockSpec(memory_space=pltpu.VMEM)
    return pl.pallas_call(
        finish_kernel,
        in_specs=[pl.BlockSpec(memory_space=pltpu.SMEM)] + [inside] * len(operands),
        out_specs=[inside, inside, pl.BlockSpec(memory_space=pltpu.HBM)],
        out_shape=[tail, tail, sds((rows, width), bf)],
        scratch_shapes=[pltpu.VMEM((rows, width), bf), pltpu.SemaphoreType.DMA(())],
        compiler_params=pltpu.CompilerParams(vmem_limit_bytes=6 * 1024 * 1024),
        cost_estimate=pl.CostEstimate(flops=8000000000, bytes_accessed=1000, transcendentals=0),
        name="finish",
    )(scalar, *operands)


def ranked(lines, bases, rows):
    piece = lines[0].shape[1]
    flags = [((ids >= base) & (ids < base + rows)).astype(f32) for ids, base in zip(lines, bases)]
    flags = jnp.concatenate(flags + [jnp.zeros((8 - len(flags), piece), f32)], axis=0).astype(bf)
    row = lax.broadcasted_iota(jnp.int32, (piece, piece), 0)
    column = lax.broadcasted_iota(jnp.int32, (piece, piece), 1)
    rank = dg((column < row).astype(bf), flags, NT)
    here = dg((column == row).astype(bf), flags, NT)
    place = lax.broadcasted_iota(jnp.int32, (piece, CAP), 1).astype(f32)
    return [jnp.where(rank[:, i : i + 1] == place, here[:, i : i + 1], 0.0).astype(bf) for i in range(len(lines))]


def share_kernel(scalar_ref, low_ref, aux_ref, *refs, piece):
    outs, (share_ref, sem) = refs[:GROUPS], refs[GROUPS:]
    rows = low_ref.shape[0]
    base = scalar_ref[GROUPS]
    slot = lax.broadcasted_iota(jnp.int32, (rows, piece), 0) + base
    lines = read_slots(aux_ref, GROUPS, piece)
    for i, (ids, rank) in enumerate(zip(lines, ranked(lines, [base] * GROUPS, rows))):
        pick = dg((slot == ids).astype(bf), rank, NN).astype(bf)
        share_ref[i] = dg(pick, low_ref[...], TN).astype(bf)
    copies = [pltpu.make_async_copy(share_ref.at[i], out, sem.at[i]) for i, out in enumerate(outs)]
    for copy in copies:
        copy.start()
    for copy in copies:
        copy.wait()


def share(scalar, low, aux, piece):
    shape = (CAP, low.shape[1])
    inside = pl.BlockSpec(memory_space=pltpu.VMEM)
    return pl.pallas_call(
        functools.partial(share_kernel, piece=piece),
        in_specs=[pl.BlockSpec(memory_space=pltpu.SMEM), inside, inside],
        out_specs=[pl.BlockSpec(memory_space=pltpu.HBM)] * GROUPS,
        out_shape=[sds(shape, bf)] * GROUPS,
        scratch_shapes=[pltpu.VMEM((GROUPS,) + shape, bf), pltpu.SemaphoreType.DMA((GROUPS,))],
        compiler_params=pltpu.CompilerParams(vmem_limit_bytes=11 * 1024 * 1024),
        cost_estimate=pl.CostEstimate(flops=1000, bytes_accessed=1000, transcendentals=0),
        name="share",
    )(scalar, low, aux)


def collect_kernel(scalar_ref, aux_ref, *refs, rows):
    *shares, out_ref = refs
    (ids,) = read_slots(aux_ref, 1, out_ref.shape[0])
    ranks = ranked([ids] * GROUPS, [scalar_ref[GROUPS + i] for i in range(GROUPS)], rows)
    out_ref[...] = sum(dg(rank, ref[...], NN) for rank, ref in zip(ranks, shares)).astype(bf)


def collect(scalar, aux, shares, rows, piece):
    shape = (piece, shares[0].shape[1])
    return call(
        functools.partial(collect_kernel, rows=rows), "collect", scalar, [aux, *shares], [sds(shape, bf)]
    )[0]


def unpack_feed_kernel(scalar_ref, *refs):
    *sources, down_ref, up_ref, out_ref = refs
    mine, other = sources[:GROUPS], sources[GROUPS:]
    first = scalar_ref[GROUPS + 4] == 0
    lines = down_ref.shape[0] // GROUPS
    half = out_ref.shape[0] // 2
    extra = half // SPREAD

    def unpack(g):
        z_low, z_high = scalar_ref[GROUPS + 12 + g], scalar_ref[GROUPS + 8 + g]
        for k, far in enumerate(OPPOSITE):
            low = jnp.where(first, mine[k][g], other[k][g]).astype(f32)
            high = jnp.where(first, other[g][k], mine[g][k]).astype(f32)
            y_low, y_high = turn(scalar_ref[GROUPS + 6], far), turn(scalar_ref[GROUPS + 12], far)
            down_ref[pl.ds(pl.multiple_of(lines * y_low, 16), lines), :] = low[:lines]
            up_ref[pl.ds(pl.multiple_of(lines * y_high, 16), lines), :] = high[:lines]
            at = extra * (GROUPS * z_low + y_low)
            out_ref[pl.ds(pl.multiple_of(at, 16), extra), :] = low[lines:]
            at = half + extra * (GROUPS * z_high + y_high)
            out_ref[pl.ds(pl.multiple_of(at, 16), extra), :] = high[lines:]

    for g in range(GROUPS):
        pl.when(pl.program_id(0) == g)(functools.partial(unpack, g))


def unpack_feed(scalar, mine, other, width, hidden):
    block = pl.BlockSpec(mine[0].shape, lambda g, s: (0, 0, 0))
    return grid_call(
        unpack_feed_kernel,
        "unpack_feed",
        scalar,
        GROUPS,
        [block] * (2 * GROUPS),
        [
            pl.BlockSpec((width, width), lambda g, s: (s[GROUPS + 12 + g], 0)),
            pl.BlockSpec((width, width), lambda g, s: (0, s[GROUPS + 8 + g])),
            pl.BlockSpec((width, width), lambda g, s: (0, 0)),
        ],
        [sds((hidden, width), f32), sds((width, hidden), f32), sds((width, width), f32)],
        [*mine, *other],
    )


def unpack_rest_kernel(scalar_ref, mine_ref, other_ref, out_ref, pos_ref, *vec_refs):
    core = scalar_ref[GROUPS + 4]
    half = out_ref.shape[0] // 2
    width = out_ref.shape[1] // 3
    rows = pos_ref.shape[0] // 2
    chunk = mine_ref.shape[0] // GROUPS
    for kept, ref in ((core, mine_ref), (1 - core, other_ref)):
        lines = pl.ds(pl.multiple_of(kept * half, half), half)
        for j in range(GROUPS):
            for w in range(3):
                lanes = slice(w * width + 128 * j, w * width + 128 * (j + 1))
                block = ref[chunk * j : chunk * (j + 1), :, 128 * w : 128 * (w + 1)]
                out_ref[lines, lanes] = block.reshape(half, 128).astype(f32)
        tail = ref[:, :, 3 * 128 :].astype(f32).reshape(-1, 128)
        lines = pl.ds(pl.multiple_of(kept * rows, 8), rows)
        blocks = width // 128
        for i in range(blocks):
            pos_ref[lines, 128 * i : 128 * (i + 1)] = tail[rows * i : rows * (i + 1)]
            if ref is mine_ref:
                base = rows * blocks + 16 * i
                for n, vec_ref in enumerate(vec_refs):
                    for line in range(vec_ref.shape[1] // width):
                        lanes = slice(width * line + 128 * i, width * line + 128 * (i + 1))
                        vec_ref[:, lanes] = tail[base + n + line : base + n + line + 1]


def unpack_rest(scalar, mine, other, rows, width, hidden):
    return call(
        unpack_rest_kernel,
        "unpack_rest",
        scalar,
        [mine, other],
        [sds((width, 3 * width), f32), sds((rows, width), f32)]
        + [sds((1, width), f32)] * 9
        + [sds((1, hidden), f32)],
    )


def shift(array, axis, step):
    size = lax.axis_size(axis)
    return lax.ppermute(array, axis, [(i, (i + step) % size) for i in range(size)])


def peers(array, axis):
    return [shift(array, axis, step) for step in (1, 3, 2)]


def swap(array):
    return shift(array, "core", 1)


def total(parts):
    return functools.reduce(jnp.add, [p.astype(f32) for p in parts])


SPACE = ("x", "z", "y")
PLANE = ("z", "y", "core")


def step_plane(array, step, near):
    sizes = [lax.axis_size(name) for name in PLANE]
    pairs = []
    for z in range(sizes[0]):
        for y in range(sizes[1]):
            for core in range(sizes[2]):
                if (core == 0) == near:
                    target = (z, (y + step) % sizes[1], core)
                else:
                    target = ((z + step) % sizes[0], y, core)
                index = lambda p: (p[0] * sizes[1] + p[1]) * sizes[2] + p[2]
                pairs.append((index((z, y, core)), index(target)))
    return lax.ppermute(array, PLANE, pairs)


def step_cores(array):
    size = lax.axis_size("x")
    pairs = []
    for core in range(2):
        for x in range(size):
            pairs.append((core * size + x, core * size + (x + 1 - 2 * core) % size))
    return lax.ppermute(array, ("core", "x"), pairs)


def plane_peers(array, near):
    return [step_plane(array, step, near) for step in (2, 1, 3)]


def exchange(array, axes):
    return lax.all_to_all(array, axes, 0, 0, tiled=True)


def body(
    vis,
    keep_slots,
    counts,
    band_mask,
    mask_token,
    pos,
    ln1_gain,
    ln1_bias,
    w_qkv,
    b_query,
    b_value,
    w_out,
    b_out,
    ln2_gain,
    ln2_bias,
    w_up,
    b_up,
    w_down,
    b_down,
    d_out,
):
    barrier = lax.optimization_barrier
    x = lax.axis_index("x")
    core = lax.axis_index("core")
    piece = keep_slots.shape[1]
    rows, width = pos.shape
    half = rows // 2
    hidden = w_up.shape[1]

    vis = vis[0]

    y, z = lax.axis_index("y"), lax.axis_index("z")
    relative, far = jnp.array(RELATIVE, jnp.int32), jnp.array(OPPOSITE, jnp.int32)
    order = (x + relative) % GROUPS
    live = jnp.sum(jnp.where(order[:, None] == jnp.arange(GROUPS)[None, :], band_mask, 0), axis=1)
    here = (x * lax.axis_size("z") + z) * lax.axis_size("y") + y
    chunks = width // 128 * half // 16
    shared = (here >= chunks) & (here < chunks + width // 128)
    scalar = jnp.concatenate(
        [live, order * rows, jnp.stack([core, shared.astype(jnp.int32), y, z]), (z + far) % GROUPS, (x + far) % GROUPS]
    ).astype(jnp.int32)
    pack = lambda *vs: jnp.pad(jnp.stack(vs), ((0, 8 - len(vs)), (0, 0)))
    vectors = pack(mask_token, ln1_gain, ln1_bias, b_query, b_value)
    feed_vectors = pack(b_out, ln2_gain, ln2_bias, b_down)

    index = lax.broadcasted_iota(jnp.int32, (1, piece), 1)
    code = jnp.where(index < counts, keep_slots, -1) + 1
    marks = jnp.concatenate([code // 64, code % 64], axis=0).astype(bf)
    marks = jnp.pad(marks, ((0, MARKS - 2), (0, width - piece)))
    message = jnp.concatenate([marks, vis], axis=0)
    pieces = [message] + [shift(message, "x", step) for step in (2, 1, 3)]
    pos_half = lax.dynamic_slice(pos, (half * core, 0), (half, width))
    pos_mine = [step_cores(pos), shift(pos_half, "x", 2)]
    scalar, vectors, feed_vectors, pieces = barrier((scalar, vectors, feed_vectors, pieces))
    aux, *bases = front(scalar, pieces, vectors, rows)
    start, q, turned_own, k_own, v_own, *state, p_own = attention_own(scalar, bases[0], pos, vectors, w_qkv)
    state, pos_mine = barrier((state, pos_mine))
    pos_other = [swap(p) for p in pos_mine]
    out = middle(scalar, bases[1:], pos_mine + pos_other, vectors, w_qkv, q, state)
    rest, (mixed, lse), kept = out[: 3 * (GROUPS - 1)], out[3 * (GROUPS - 1) :][:2], out[3 * (GROUPS - 1) + 2 :]
    keys, values = [k_own, *rest[1::3]], [v_own, *rest[2::3]]
    weights, peaks = [p_own, *kept[0::2]], [state[0], *kept[1::2]]

    out, middle_rows, second, kept, sent, grad_b_up = feed_forward(
        scalar, mixed, start, d_out[0], w_out, feed_vectors, w_up, b_up[None], w_down
    )
    got = swap(sent)
    grad_middle, grad_mixed, out_kept, out_sent, feed_vec = feed_backward(
        scalar, mixed, middle_rows, second, d_out[0], w_out, feed_vectors
    )
    factors = softmax_factors(scalar, mixed, grad_mixed, lse, peaks)
    inputs = list(zip(factors[:GROUPS], weights, keys, values, factors[GROUPS:]))
    feed = fold_feed(scalar, kept, got, out_kept, swap(out_sent))
    inputs, feed = barrier((inputs, feed))
    feed = [feed[0]] + [step_plane(feed[r], r, True) for r in (1, 2, 3)]
    dq, d_3, part = attention_grad(scalar, (3,), q, w_qkv, [inputs[3]], None)
    dq, part = barrier((dq, part))
    from_3 = shift(part, "x", 2)
    dq, d_1, part = attention_grad(scalar, (1,), q, w_qkv, [inputs[1]], dq)
    feed = fold_line(scalar, feed)
    dq, part, feed = barrier((dq, part, feed))
    feed = [feed[0]] + [shift(feed[r], "x", r) for r in (2, 1, 3)]
    from_1 = shift(part, "x", 3)
    dq, d_2, part = attention_grad(scalar, (2,), q, w_qkv, [inputs[2]], dq)
    feed = add_up(scalar, "fold_point", feed)
    dq, part, from_3, feed = barrier((dq, part, from_3, feed))
    feed_peers = [step_plane(feed, step, False) for step in (1, 3, 2)]
    from_2 = shift(part, "x", 1)
    part, at_kept, at_sent, grad_b_query, grad_b_value = attention_grad(
        scalar, (0,), q, w_qkv, [inputs[0]], dq, [turned_own, *rest[0::3], d_3, d_1, d_2]
    )
    at_kept, at_sent, part, from_1, from_2, feed_peers = barrier(
        (at_kept, at_sent, part, from_1, from_2, feed_peers)
    )

    at_got = swap(at_sent)
    feed = add_up(scalar, "sum_line", [feed] + feed_peers)
    gathered = [shift(feed, "x", step) for step in (2, 1, 3)]
    tail_kept, tail_sent, low = finish(
        scalar,
        part,
        (from_3, from_1, from_2),
        start,
        grad_middle,
        vectors,
        aux,
        grad_b_query,
        grad_b_value,
        feed_vec,
        grad_b_up,
    )
    spread = lambda a: a.reshape(GROUPS * SPREAD, 16, -1)
    bundle = fold_rest(scalar, spread(at_kept), spread(at_got), tail_kept, swap(tail_sent))
    bundle, feed = barrier((bundle, jnp.stack([feed] + gathered)))
    bundle = exchange(bundle, SPACE)
    feed_other = [swap(feed)]
    feed = [feed] + plane_peers(feed, True)
    bundle, shares, feed_other = barrier((bundle, share(scalar, low, aux, piece), feed_other))
    bundle = sum_space(scalar, bundle)
    feed, _ = barrier((feed, bundle))
    rest_mine = exchange(bundle, SPACE)
    feed_other += [swap(a) for a in feed[1:]]
    feed_other[1], shares = barrier((feed_other[1], shares))
    returned = [shares[0], shift(shares[3], "x", 1), shift(shares[2], "x", 3), shift(shares[1], "x", 2)]
    grad_w_down, grad_w_up, grad_w_out = unpack_feed(scalar, feed, feed_other, width, hidden)
    grad_vis = collect(scalar, aux, returned, rows, piece)
    rest_mine, grad_w_down, grad_vis = barrier((rest_mine, grad_w_down, grad_vis))
    rest_other = swap(rest_mine)
    grad_w_qkv, grad_pos, *sums = unpack_rest(scalar, rest_mine, rest_other, rows, width, hidden)
    sums = [a[0] for a in sums]

    return (
        out[None],
        grad_vis[None],
        sums[0],
        grad_pos,
        sums[1],
        sums[2],
        grad_w_qkv,
        sums[3],
        sums[4],
        grad_w_out,
        sums[5],
        sums[6],
        sums[7],
        grad_w_up,
        sums[9],
        grad_w_down,
        sums[8],
    )


CUBE = ("z", "y", "core")


def solution(mesh):
    fine = Mesh(mesh.devices.reshape(4, 4, 2, 4), ("z", "y", "core", "x"))
    return jax.shard_map(
        body,
        mesh=fine,
        in_specs=(
            P(CUBE, "x", None),
            P(CUBE, "x"),
            P(CUBE, "x"),
            P(CUBE, None),
            P(),
            P("x", None),
        )
        + (P(),) * 13
        + (P(CUBE, "x", None),),
        out_specs=(P(CUBE, "x", None), P(CUBE, "x", None), P(), P("x", None)) + (P(),) * 13,
        check_vma=False,
    )
```

```python
import functools

import jax
import jax.numpy as jnp
from jax import lax
from jax.experimental import pallas as pl
from jax.experimental.pallas import tpu as pltpu
from jax.sharding import Mesh, PartitionSpec as P

bf = jnp.bfloat16
f32 = jnp.float32

HEADS = 16
DEPTH = 32
QUAD = 4
GROUPS = 4
LOG2E = 1.4426950408889634
SCALE = DEPTH**-0.5
EPS = 1e-05
BIG = 1e30
GELU_SCALE = 0.7978845608028654
GELU_CUBE = 0.044715
RELATIVE = (0, 3, 1, 2)
OPPOSITE = (0, 2, 3, 1)
CAP = 80
MARKS = 16
SPREAD = 16

NT = (((1,), (1,)), ((), ()))
NN = (((1,), (0,)), ((), ()))
TN = (((0,), (0,)), ((), ()))
VMEM_LIMIT = 56 * 1024 * 1024


def dg(a, b, dims):
    return lax.dot_general(a, b, dims, preferred_element_type=f32)


def sds(shape, dtype):
    return jax.ShapeDtypeStruct(shape, dtype)


def call(kernel, name, scalar, operands, out_shape, scratch=(), aliases=None, limit=5, micro=0.001):
    inside = pl.BlockSpec(memory_space=pltpu.VMEM)
    return pl.pallas_call(
        kernel,
        in_specs=[pl.BlockSpec(memory_space=pltpu.SMEM)] + [inside] * len(operands),
        out_specs=[inside] * len(out_shape),
        out_shape=out_shape,
        scratch_shapes=list(scratch),
        compiler_params=pltpu.CompilerParams(vmem_limit_bytes=limit * 1024 * 1024),
        cost_estimate=pl.CostEstimate(flops=int(micro * 1e9), bytes_accessed=1000, transcendentals=0),
        input_output_aliases=aliases or {},
        name=name,
    )(scalar, *operands)


def grid_call(kernel, name, scalar, steps, in_specs, out_specs, out_shape, operands):
    return pl.pallas_call(
        kernel,
        grid_spec=pltpu.PrefetchScalarGridSpec(
            num_scalar_prefetch=1, grid=(steps,), in_specs=in_specs, out_specs=out_specs
        ),
        out_shape=out_shape,
        compiler_params=pltpu.CompilerParams(vmem_limit_bytes=32 * 1024 * 1024),
        cost_estimate=pl.CostEstimate(flops=1000, bytes_accessed=1000, transcendentals=0),
        name=name,
    )(scalar, *operands)


def column_sum(tensor):
    return jnp.sum(tensor.astype(f32), axis=0, keepdims=True)


def norm_parts(values):
    centered = values - jnp.mean(values, axis=-1, keepdims=True)
    variance = jnp.mean(centered * centered, axis=-1, keepdims=True)
    inverse = lax.rsqrt(variance + EPS)
    return centered * inverse, inverse


def norm_pull(grad, n, inverse, gain):
    g = grad * gain
    return inverse * (
        g - jnp.mean(g, axis=-1, keepdims=True) - n * jnp.mean(g * n, axis=-1, keepdims=True)
    )


def place_rows(base, pieces, ids, rows, rows_ref):
    piece, width = ids[0].shape[1], rows_ref.shape[1]
    slot = lax.broadcasted_iota(jnp.int32, (rows, piece), 0) + base
    placed = jnp.zeros((rows, width), f32)
    seen = jnp.zeros((rows, 1), f32)
    for v, i in zip(pieces, ids):
        hot = (slot == i).astype(f32)
        seen += jnp.sum(hot, axis=1, keepdims=True)
        placed += dg(hot.astype(bf), v[MARKS : MARKS + piece, :], NN)
    unseen = 1.0 - seen
    return placed + unseen * rows_ref[0:1], unseen


def first_norm(start, rows_ref):
    n, _ = norm_parts(start)
    return (n * rows_ref[1:2] + rows_ref[2:3]).astype(bf)


def keys_values(normed, rows_ref, w_ref, turned_ref, k_ref, v_ref):
    width = normed.shape[1]
    k_ref[...] = dg(normed, w_ref[:, width : 2 * width], NN).astype(bf)
    v_ref[...] = (dg(normed, w_ref[:, 2 * width :], NN) + rows_ref[4:5]).astype(bf)
    turned_ref[...] = normed.T


def stack_heads(x):
    lane = lax.broadcasted_iota(jnp.int32, x.shape, 1) // DEPTH
    return jnp.concatenate([jnp.where(lane == h, x, jnp.zeros_like(x)) for h in range(QUAD)], axis=0)


def unstack_heads(xt):
    rows = xt.shape[1] // QUAD
    parts = [xt[DEPTH * h : DEPTH * (h + 1), rows * h : rows * (h + 1)] for h in range(QUAD)]
    return jnp.concatenate(parts, axis=0).T


def fwd_steps(steps, scalar_ref, query, key, value, state, keep_weights, finish):
    stacked = {}

    def scores(quad, group):
        if quad not in stacked:
            stacked[quad] = stack_heads(query(quad))
        return dg(key(quad, group), stacked[quad], NT)

    ahead = scores(*steps[0])
    for i, (quad, group) in enumerate(steps):
        s = ahead
        if i + 1 < len(steps):
            ahead = scores(*steps[i + 1])
        live = scalar_ref[group] > 0
        peak = jnp.where(live, jnp.max(s, axis=0, keepdims=True), -BIG)
        old = state(quad) if i == 0 or steps[i - 1][0] != quad else new
        if old is not None:
            peak = jnp.maximum(old[0], peak)
        p = jnp.exp2(s - jnp.where(live, peak, BIG)).astype(bf)
        keep_weights(quad, group, p, peak)
        v = value(quad, group)
        turned = jnp.concatenate([v.T, jnp.ones((16, v.shape[0]), bf)], axis=0)
        both = dg(turned, p, NN)
        o, l = both[: v.shape[1]], both[v.shape[1] : v.shape[1] + 1]
        if old is not None:
            keep = jnp.exp2(old[0] - peak)
            o += old[2] * keep
            l += old[1] * keep
        new = (peak, l, o)
        if i + 1 == len(steps) or steps[i + 1][0] != quad:
            finish(quad, new)


def quad_at(quad):
    return (slice(None), slice(128 * quad, 128 * (quad + 1)))


def front_kernel(scalar_ref, *refs):
    pieces, (rows_ref, aux_ref), bases = refs[:GROUPS], refs[GROUPS : GROUPS + 2], refs[GROUPS + 2 :]
    rows = bases[0].shape[0]
    piece = pieces[0].shape[0] - MARKS
    ids = []
    for i, v in enumerate(pieces):
        marks = v[:MARKS, :].astype(f32)[:8, :piece]
        line = marks[0:1] * 64.0 + marks[1:2] - 1.0
        aux_ref[rows + i : rows + i + 1, :piece] = line
        ids.append(line.astype(jnp.int32))
    for g, base in enumerate(bases):
        base[...], unseen = place_rows(scalar_ref[GROUPS + g], pieces, ids, rows, rows_ref)
        if g == 0:
            aux_ref[:rows, :128] = jnp.broadcast_to(unseen, (rows, 128))


def read_slots(aux_ref, count, piece):
    rows = aux_ref.shape[0] - 8
    return [aux_ref[rows + i : rows + i + 1, :piece].astype(jnp.int32) for i in range(count)]


def front(scalar, pieces, vectors, rows):
    width = vectors.shape[1]
    return call(
        front_kernel,
        "front",
        scalar,
        [*pieces, vectors],
        [sds((rows + 8, 256), f32)] + [sds((rows, width), f32)] * GROUPS,
        micro=4,
    )


def attention_own_kernel(
    scalar_ref,
    base_ref,
    pos_ref,
    rows_ref,
    w_ref,
    start_ref,
    q_ref,
    turned_ref,
    k_ref,
    v_ref,
    m_ref,
    l_ref,
    o_ref,
    p_ref,
):
    start = base_ref[...] + pos_ref[...].astype(f32)
    start_ref[...] = start
    normed = first_norm(start, rows_ref)
    width = normed.shape[1]
    q_ref[...] = ((dg(normed, w_ref[:, :width], NN) + rows_ref[3:4]) * (SCALE * LOG2E)).astype(bf)
    keys_values(normed, rows_ref, w_ref, turned_ref, k_ref, v_ref)

    def keep_weights(quad, group, p, peak):
        p_ref[quad] = p

    def finish(quad, state):
        m_ref[quad], l_ref[quad], o_ref[quad] = state

    fwd_steps(
        [(quad, 0) for quad in range(m_ref.shape[0])],
        scalar_ref,
        lambda quad: q_ref[quad_at(quad)],
        lambda quad, group: k_ref[quad_at(quad)],
        lambda quad, group: v_ref[quad_at(quad)],
        lambda quad: None,
        keep_weights,
        finish,
    )


def attention_own(scalar, base, pos, vectors, w_qkv):
    rows, width = pos.shape
    quads, n = width // 128, rows * QUAD
    return call(
        attention_own_kernel,
        "attention_own",
        scalar,
        [base, pos, vectors, w_qkv],
        [
            sds((rows, width), f32),
            sds((rows, width), bf),
            sds((width, rows), bf),
            sds((rows, width), bf),
            sds((rows, width), bf),
            sds((quads, 1, n), f32),
            sds((quads, 1, n), f32),
            sds((quads, 128, n), f32),
            sds((quads, rows, n), bf),
        ],
        limit=7,
        micro=5,
    )


def middle_kernel(scalar_ref, *refs):
    bases, refs = refs[: GROUPS - 1], refs[GROUPS - 1 :]
    pos_refs, refs = refs[:4], refs[4:]
    rows_ref, w_ref, q_ref, m_ref, l_ref, o_ref, *refs = refs
    groups, (mixed_ref, lse_ref), kept = refs[: 3 * (GROUPS - 1)], refs[3 * (GROUPS - 1) :][:2], refs[3 * (GROUPS - 1) + 2 :]
    first = scalar_ref[GROUPS + GROUPS] == 0
    near, far, other_near, other_far = [ref[...].astype(f32) for ref in pos_refs]
    for g, base in enumerate(bases):
        if g < 2:
            pos = jnp.where(first == (g == 0), near, other_near)
        else:
            pos = jnp.concatenate([jnp.where(first, far, other_far), jnp.where(first, other_far, far)], axis=0)
        keys_values(first_norm(base[...] + pos, rows_ref), rows_ref, w_ref, *groups[3 * g : 3 * g + 3])

    def keep_weights(quad, group, p, peak):
        kept[2 * group - 2][quad] = p
        kept[2 * group - 1][quad] = peak

    def finish(quad, state):
        m, l, o = state
        mixed_ref[quad_at(quad)] = unstack_heads(o / l).astype(bf)
        lse_ref[quad] = m + jnp.log2(l)

    fwd_steps(
        [(quad, group) for quad in range(m_ref.shape[0]) for group in range(1, GROUPS)],
        scalar_ref,
        lambda quad: q_ref[quad_at(quad)],
        lambda quad, group: groups[3 * group - 2][quad_at(quad)],
        lambda quad, group: groups[3 * group - 1][quad_at(quad)],
        lambda quad: (m_ref[quad], l_ref[quad], o_ref[quad]),
        keep_weights,
        finish,
    )


def middle(scalar, bases, pos, vectors, w_qkv, q, state):
    rows, width = q.shape
    quads, n = width // 128, rows * QUAD
    group = [sds((width, rows), bf), sds((rows, width), bf), sds((rows, width), bf)]
    return call(
        middle_kernel,
        "middle",
        scalar,
        [*bases, *pos, vectors, w_qkv, q, *state],
        [*(group * (GROUPS - 1)), sds((rows, width), bf), sds((quads, 1, n), f32)]
        + [sds((quads, rows, n), bf), sds((quads, 1, n), f32)] * (GROUPS - 1),
        limit=9,
    )


def bwd_kernel(scalar_ref, q_ref, w_ref, *refs, groups, carried):
    width = q_ref.shape[1]
    inputs, refs = [refs[5 * i : 5 * i + 5] for i in range(len(groups))], refs[5 * len(groups) :]
    if carried:
        dq_in, *refs = refs
    own = groups == (0,)
    if own:
        *turned_refs, d_3, d_1, d_2, part_ref, kept_ref, sent_ref, bq_ref, bv_ref, d_s = refs
        base, outs = width, [(d_s, part_ref)]
    else:
        dq_ref, *refs = refs
        base, outs = 0, [refs[2 * i : 2 * i + 2] for i in range(len(groups))]
    quads = width // 128
    for j in range(quads):
        at = quad_at(j)
        qs = stack_heads(q_ref[at])
        dq = dq_in[at] if carried else None
        for (do_ref, p_ref, k_ref, v_ref, delta_ref), (d_ref, _) in zip(inputs, outs):
            columns = lambda i: (
                slice(None),
                slice(base + (i - 1) * width + 128 * j, base + (i - 1) * width + 128 * (j + 1)),
            )
            dos = stack_heads(do_ref[at])
            k, p = k_ref[at], p_ref[j]
            ds = (p.astype(f32) * (dg(v_ref[at], dos, NT) - delta_ref[j])).astype(bf)
            d_ref[columns(2)] = dg(p, dos, NN).astype(bf)
            d_ref[columns(1)] = (dg(ds, qs, NN) * (1.0 / LOG2E)).astype(bf)
            term = unstack_heads(dg(k, ds, TN))
            dq = term if dq is None else dq + term
        if own:
            d_s[at] = (dq * SCALE).astype(bf)
        else:
            dq_ref[at] = dq
    for d_ref, part_ref in outs:
        grads = d_ref[...]
        part_ref[...] = dg(grads, w_ref[...] if own else w_ref[:, width:], NT).astype(part_ref.dtype)
    if not own:
        return
    own, *rest = turned_refs
    g = dg(own[...], grads[:, width:], NN)
    bv = column_sum(grads[:, 2 * width :])
    for turned, d_ref in zip(rest, (d_1, d_2, d_3)):
        d = d_ref[...]
        g += dg(turned[...], d, NN)
        bv += column_sum(d[:, width:])
    bv_ref[...] = bv
    bq_ref[...] = column_sum(grads[:, :width])
    gq = dg(own[...], grads[:, :width], NN)
    first = scalar_ref[GROUPS + 4] == 0
    half = width // 2
    for j in range(quads):
        at = slice(128 * j, 128 * (j + 1))
        block = jnp.concatenate([gq[:, at], g[:, at], g[:, width + 128 * j : width + 128 * (j + 1)]], axis=1)
        kept_ref[j] = jnp.where(first, block[:half], block[half:]).astype(bf)
        sent_ref[j] = jnp.where(first, block[half:], block[:half]).astype(bf)


def attention_grad(scalar, groups, q, w_qkv, inputs, dq, more=()):
    rows, width = q.shape
    quads = width // 128
    operands = [q, w_qkv] + [a for group in inputs for a in group]
    aliases = {}
    if dq is not None:
        aliases = {len(operands) + 1: 0}
        operands.append(dq)
    operands += list(more)
    scratch = []
    if groups == (0,):
        packed = (quads, width // 2, 3 * 128)
        out_shape = [sds((rows, width), f32)] + [sds(packed, bf)] * 2 + [sds((1, width), f32)] * 2
        scratch = [pltpu.VMEM((rows, 3 * width), bf)]
    else:
        out_shape = [sds((rows, width), f32)]
        out_shape += [sds((rows, 2 * width), bf), sds((rows, width), bf)] * len(groups)
    return call(
        functools.partial(bwd_kernel, groups=groups, carried=dq is not None),
        "attention_grad_" + "_".join(str(g) for g in groups),
        scalar,
        operands,
        out_shape,
        scratch,
        aliases,
    )


def feed_kernel(
    scalar_ref,
    mixed_ref,
    start_ref,
    dout_ref,
    wout_ref,
    rows_ref,
    wup_ref,
    bup_ref,
    wdown_ref,
    out_ref,
    middle_ref,
    second_ref,
    kept_ref,
    sent_ref,
    gbup_ref,
):
    first = scalar_ref[GROUPS + 4] == 0
    width = mixed_ref.shape[1]
    hidden = wup_ref.shape[1]
    dout = dout_ref[...]
    middle = start_ref[...] + (dg(mixed_ref[...], wout_ref[...], NN) + rows_ref[0:1])
    middle_ref[...] = middle
    n, _ = norm_parts(middle)
    normed = (n * rows_ref[1:2] + rows_ref[2:3]).astype(bf)
    turned = normed.T
    result = middle + rows_ref[3:4]
    second = jnp.zeros_like(middle)
    lines = hidden // SPREAD
    for h in range(hidden // width):
        at = slice(width * h, width * (h + 1))
        u = dg(normed, wup_ref[:, at], NN) + bup_ref[:, at]
        square = u * u
        t = jnp.tanh(u * (GELU_SCALE + (GELU_SCALE * GELU_CUBE) * square))
        near = 0.5 + 0.5 * t
        act = (u * near).astype(bf)
        result += dg(act, wdown_ref[at, :], NN)
        slope = near + u * (0.5 - 0.5 * (t * t)) * (GELU_SCALE + (3.0 * GELU_SCALE * GELU_CUBE) * square)
        gup = (dg(dout, wdown_ref[at, :], NT) * slope).astype(bf)
        second += dg(gup, wup_ref[:, at], NT)
        gbup_ref[:, at] = column_sum(gup)
        down = dg(act, dout, TN).astype(bf)
        up = dg(turned, gup, NN).astype(bf)
        chunks = (width // lines, lines, width)
        places = slice(h * chunks[0], (h + 1) * chunks[0])
        kept_ref[places] = jnp.where(first, down, up).reshape(chunks)
        sent_ref[places] = jnp.where(first, up, down).reshape(chunks)
    out_ref[...] = result.astype(bf)
    second_ref[...] = second


def feed_backward_kernel(
    scalar_ref,
    mixed_ref,
    middle_ref,
    second_ref,
    dout_ref,
    wout_ref,
    rows_ref,
    gmid_ref,
    gmix_ref,
    kept_ref,
    sent_ref,
    vec_ref,
):
    first = scalar_ref[GROUPS + 4] == 0
    mixed = mixed_ref[...]
    width = mixed.shape[1]
    second = second_ref[...]
    grad = dout_ref[...].astype(f32)
    n, inverse = norm_parts(middle_ref[...])
    gmid = grad + norm_pull(second, n, inverse, rows_ref[1:2])
    gmid_ref[...] = gmid
    branch = gmid.astype(bf)
    gmix_ref[...] = dg(branch, wout_ref[...], NT).astype(bf)
    wout = dg(mixed, branch, TN)
    half = width // 2
    extra = (SPREAD, half // SPREAD, width)
    kept_ref[...] = jnp.where(first, wout[:half], wout[half:]).astype(bf).reshape(extra)
    sent_ref[...] = jnp.where(first, wout[half:], wout[:half]).astype(bf).reshape(extra)
    vec_ref[...] = jnp.concatenate(
        [
            column_sum(branch),
            column_sum(second * n),
            column_sum(second),
            column_sum(grad),
            jnp.zeros((4, width), f32),
        ],
        axis=0,
    )


def factor_kernel(scalar_ref, mixed_ref, gmix_ref, lse_ref, *refs):
    peaks, outs = refs[:GROUPS], refs[GROUPS:]
    gmix = gmix_ref[...].astype(f32)
    width = gmix.shape[1]
    product = mixed_ref[...].astype(f32) * gmix
    head = lax.broadcasted_iota(jnp.int32, (HEADS, width), 0)
    lane = lax.broadcasted_iota(jnp.int32, (HEADS, width), 1) // DEPTH
    pick = (head == lane).astype(bf)
    halves = lambda a: (a.astype(bf), (a - a.astype(bf).astype(f32)).astype(bf))
    high, low = halves(product)
    delta = dg(pick, high, NT) + dg(pick, low, NT)
    rows = delta.shape[1]
    for peak_ref, do_ref, delta_ref in zip(peaks, outs[:GROUPS], outs[GROUPS:]):
        lines = []
        for j in range(HEADS // QUAD):
            factor = jnp.exp2(peak_ref[j] - lse_ref[j])
            delta_ref[j] = factor * jnp.concatenate([delta[QUAD * j + i : QUAD * j + i + 1] for i in range(QUAD)], axis=1)
            lines += [factor[:, rows * i : rows * (i + 1)] for i in range(QUAD)]
        high, low = halves(jnp.concatenate(lines, axis=0))
        do_ref[...] = (gmix * (dg(high, pick, TN) + dg(low, pick, TN))).astype(bf)


def feed_forward(scalar, mixed, start, d_out, w_out, vectors, w_up, b_up, w_down):
    rows, width = mixed.shape
    hidden = w_up.shape[1]
    packed = (SPREAD, hidden // SPREAD, width)
    return call(
        feed_kernel,
        "feed_forward",
        scalar,
        [mixed, start, d_out, w_out, vectors, w_up, b_up, w_down],
        [sds((rows, width), bf)] + [sds((rows, width), f32)] * 2 + [sds(packed, bf)] * 2 + [sds((1, hidden), f32)],
        limit=8,
    )


def feed_backward(scalar, mixed, middle, second, d_out, w_out, vectors):
    rows, width = mixed.shape
    packed = (SPREAD, width // 2 // SPREAD, width)
    return call(
        feed_backward_kernel,
        "feed_backward",
        scalar,
        [mixed, middle, second, d_out, w_out, vectors],
        [sds((rows, width), f32), sds((rows, width), bf), sds(packed, bf), sds(packed, bf), sds((8, width), f32)],
    )


def softmax_factors(scalar, mixed, gmix, lse, peaks):
    return call(
        factor_kernel,
        "softmax_factors",
        scalar,
        [mixed, gmix, lse, *peaks],
        [sds(gmix.shape, bf)] * GROUPS + [sds(lse.shape, f32)] * GROUPS,
        micro=2,
    )


def turn(place, steps):
    return lax.rem(place + steps, GROUPS)


def fold_feed_kernel(scalar_ref, a, b, c, d, *outs):
    first, y, z = scalar_ref[GROUPS + 4] == 0, scalar_ref[GROUPS + 6], scalar_ref[GROUPS + 7]
    near = jnp.where(first, y, z)
    lines = a.shape[1]
    for r, out_ref in enumerate(outs):
        place = turn(near, r)
        for i in range(GROUPS):
            at = jnp.where(first, GROUPS * i + place, GROUPS * place + i)
            out_ref[i, :lines] = a[at] + b[at]
            out_ref[i, lines:] = c[at] + d[at]


def fold_feed(scalar, a, b, c, d):
    shape = sds((GROUPS, a.shape[1] + c.shape[1], a.shape[2]), bf)
    return call(fold_feed_kernel, "fold_feed", scalar, [a, b, c, d], [shape] * GROUPS)


def fold_line_kernel(scalar_ref, *refs):
    sources, outs = refs[:GROUPS], refs[GROUPS:]
    for r, out_ref in enumerate(outs):
        at = turn(scalar_ref[GROUPS + 12], r)
        out_ref[...] = sum(ref[at].astype(f32) for ref in sources).astype(bf)


def fold_line(scalar, sources):
    return call(fold_line_kernel, "fold_line", scalar, sources, [sds(sources[0].shape[1:], bf)] * GROUPS)


def add_up_kernel(scalar_ref, *refs):
    *sources, out_ref = refs
    out_ref[...] = sum(ref[...].astype(f32) for ref in sources).astype(bf)


def add_up(scalar, name, arrays):
    return call(add_up_kernel, name, scalar, list(arrays), [sds(arrays[0].shape, bf)])[0]


def fold_rest_kernel(scalar_ref, a, b, c, d, out_ref):
    cut = a.shape[2]
    out_ref[:, :, :cut] = a[...] + b[...]
    out_ref[:, :, cut:] = c[...] + d[...]


def fold_rest(scalar, a, b, c, d):
    shape = a.shape[:2] + (a.shape[2] + c.shape[2],)
    return call(fold_rest_kernel, "fold_rest", scalar, [a, b, c, d], [sds(shape, bf)])[0]


def sum_space_kernel(scalar_ref, got_ref, out_ref):
    chunk = got_ref.shape[0] // GROUPS
    lanes = 3 * 128
    sums = []
    for x in range(GROUPS):
        acc = got_ref[chunk * x].astype(f32)
        for i in range(1, chunk):
            acc += got_ref[chunk * x + i].astype(f32)
        sums.append(acc)
    everything = functools.reduce(jnp.add, sums)
    shared = scalar_ref[GROUPS + 5] > 0
    for x in range(GROUPS):
        tail = jnp.where(shared, everything[:, lanes:], sums[x][:, lanes:])
        block = jnp.concatenate([everything[:, :lanes], tail], axis=1).astype(bf)
        for i in range(chunk):
            out_ref[chunk * x + i] = block


def sum_space(scalar, got):
    return call(sum_space_kernel, "sum_space", scalar, [got], [sds(got.shape, bf)])[0]


def finish_kernel(
    scalar_ref,
    part_ref,
    r3,
    r1,
    r2,
    start_ref,
    gmid_ref,
    rows_ref,
    unseen_ref,
    bq_ref,
    bv_ref,
    feed_ref,
    bup_ref,
    kept_ref,
    sent_ref,
    low_ref,
):
    rows, width = start_ref.shape
    first_grad = part_ref[...] + r3[...].astype(f32) + r1[...].astype(f32) + r2[...].astype(f32)
    n, inverse = norm_parts(start_ref[...])
    grad = gmid_ref[...] + norm_pull(first_grad, n, inverse, rows_ref[1:2])
    low_ref[...] = grad.astype(bf)
    half = rows // 2
    first = scalar_ref[GROUPS + 4] == 0
    top, low = grad[:half], grad[half:]
    lines = [
        column_sum(unseen_ref[:rows, :1] * grad),
        column_sum(first_grad * n),
        column_sum(first_grad),
        bq_ref[...],
        bv_ref[...],
        feed_ref[:4],
    ]
    blocks = bup_ref.shape[1] // width
    lines += [bup_ref[:, width * i : width * (i + 1)] for i in range(blocks)]
    spare = 16 - sum(a.shape[0] for a in lines)
    lines = jnp.concatenate(lines + [jnp.zeros((spare, width), f32)], axis=0)

    def narrow(values):
        cut = [a[:, 128 * i : 128 * (i + 1)] for a in (values, lines) for i in range(width // 128)]
        cut.append(jnp.zeros((kept_ref.shape[0] * kept_ref.shape[1] - sum(a.shape[0] for a in cut), 128), f32))
        return jnp.concatenate(cut, axis=0).reshape(kept_ref.shape).astype(bf)

    kept_ref[...] = narrow(jnp.where(first, top, low))
    sent_ref[...] = narrow(jnp.where(first, low, top))


def finish(scalar, part, received, start, gmid, vectors, unseen, bq, bv, feed_vec, grad_b_up):
    rows, width = start.shape
    tail = sds((GROUPS * SPREAD, 16, 128), bf)
    return call(
        finish_kernel,
        "finish",
        scalar,
        [part, *received, start, gmid, vectors, unseen, bq, bv, feed_vec, grad_b_up],
        [tail, tail, sds((rows, width), bf)],
        micro=8,
    )


def ranked(lines, bases, rows):
    piece = lines[0].shape[1]
    flags = [((ids >= base) & (ids < base + rows)).astype(f32) for ids, base in zip(lines, bases)]
    flags = jnp.concatenate(flags + [jnp.zeros((8 - len(flags), piece), f32)], axis=0).astype(bf)
    row = lax.broadcasted_iota(jnp.int32, (piece, piece), 0)
    column = lax.broadcasted_iota(jnp.int32, (piece, piece), 1)
    rank = dg((column < row).astype(bf), flags, NT)
    here = dg((column == row).astype(bf), flags, NT)
    place = lax.broadcasted_iota(jnp.int32, (piece, CAP), 1).astype(f32)
    return [jnp.where(rank[:, i : i + 1] == place, here[:, i : i + 1], 0.0).astype(bf) for i in range(len(lines))]


def share_kernel(scalar_ref, low_ref, aux_ref, *refs, piece):
    outs, (share_ref, sem) = refs[:GROUPS], refs[GROUPS:]
    rows = low_ref.shape[0]
    base = scalar_ref[GROUPS]
    slot = lax.broadcasted_iota(jnp.int32, (rows, piece), 0) + base
    lines = read_slots(aux_ref, GROUPS, piece)
    for i, (ids, rank) in enumerate(zip(lines, ranked(lines, [base] * GROUPS, rows))):
        pick = dg((slot == ids).astype(bf), rank, NN).astype(bf)
        share_ref[i] = dg(pick, low_ref[...], TN).astype(bf)
    copies = [pltpu.make_async_copy(share_ref.at[i], out, sem.at[i]) for i, out in enumerate(outs)]
    for copy in copies:
        copy.start()
    for copy in copies:
        copy.wait()


def share(scalar, low, aux, piece):
    shape = (CAP, low.shape[1])
    inside = pl.BlockSpec(memory_space=pltpu.VMEM)
    return pl.pallas_call(
        functools.partial(share_kernel, piece=piece),
        in_specs=[pl.BlockSpec(memory_space=pltpu.SMEM), inside, inside],
        out_specs=[pl.BlockSpec(memory_space=pltpu.HBM)] * GROUPS,
        out_shape=[sds(shape, bf)] * GROUPS,
        scratch_shapes=[pltpu.VMEM((GROUPS,) + shape, bf), pltpu.SemaphoreType.DMA((GROUPS,))],
        compiler_params=pltpu.CompilerParams(vmem_limit_bytes=11 * 1024 * 1024),
        cost_estimate=pl.CostEstimate(flops=1000, bytes_accessed=1000, transcendentals=0),
        name="share",
    )(scalar, low, aux)


def collect_kernel(scalar_ref, aux_ref, *refs, rows):
    *shares, out_ref = refs
    (ids,) = read_slots(aux_ref, 1, out_ref.shape[0])
    ranks = ranked([ids] * GROUPS, [scalar_ref[GROUPS + i] for i in range(GROUPS)], rows)
    out_ref[...] = sum(dg(rank, ref[...], NN) for rank, ref in zip(ranks, shares)).astype(bf)


def collect(scalar, aux, shares, rows, piece):
    shape = (piece, shares[0].shape[1])
    return call(
        functools.partial(collect_kernel, rows=rows), "collect", scalar, [aux, *shares], [sds(shape, bf)]
    )[0]


def unpack_feed_kernel(scalar_ref, *refs):
    *sources, down_ref, up_ref, out_ref = refs
    mine, other = sources[:GROUPS], sources[GROUPS:]
    first = scalar_ref[GROUPS + 4] == 0
    lines = down_ref.shape[0] // GROUPS
    half = out_ref.shape[0] // 2
    extra = half // SPREAD

    def unpack(g):
        z_low, z_high = scalar_ref[GROUPS + 12 + g], scalar_ref[GROUPS + 8 + g]
        for k, far in enumerate(OPPOSITE):
            low = jnp.where(first, mine[k][g], other[k][g]).astype(f32)
            high = jnp.where(first, other[g][k], mine[g][k]).astype(f32)
            y_low, y_high = turn(scalar_ref[GROUPS + 6], far), turn(scalar_ref[GROUPS + 12], far)
            down_ref[pl.ds(pl.multiple_of(lines * y_low, 16), lines), :] = low[:lines]
            up_ref[pl.ds(pl.multiple_of(lines * y_high, 16), lines), :] = high[:lines]
            at = extra * (GROUPS * z_low + y_low)
            out_ref[pl.ds(pl.multiple_of(at, 16), extra), :] = low[lines:]
            at = half + extra * (GROUPS * z_high + y_high)
            out_ref[pl.ds(pl.multiple_of(at, 16), extra), :] = high[lines:]

    for g in range(GROUPS):
        pl.when(pl.program_id(0) == g)(functools.partial(unpack, g))


def unpack_feed(scalar, mine, other, width, hidden):
    block = pl.BlockSpec(mine[0].shape, lambda g, s: (0, 0, 0))
    return grid_call(
        unpack_feed_kernel,
        "unpack_feed",
        scalar,
        GROUPS,
        [block] * (2 * GROUPS),
        [
            pl.BlockSpec((width, width), lambda g, s: (s[GROUPS + 12 + g], 0)),
            pl.BlockSpec((width, width), lambda g, s: (0, s[GROUPS + 8 + g])),
            pl.BlockSpec((width, width), lambda g, s: (0, 0)),
        ],
        [sds((hidden, width), f32), sds((width, hidden), f32), sds((width, width), f32)],
        [*mine, *other],
    )


def unpack_rest_kernel(scalar_ref, mine_ref, other_ref, out_ref, pos_ref, *vec_refs):
    core = scalar_ref[GROUPS + 4]
    half = out_ref.shape[0] // 2
    width = out_ref.shape[1] // 3
    rows = pos_ref.shape[0] // 2
    chunk = mine_ref.shape[0] // GROUPS
    for kept, ref in ((core, mine_ref), (1 - core, other_ref)):
        lines = pl.ds(pl.multiple_of(kept * half, half), half)
        for j in range(GROUPS):
            for w in range(3):
                lanes = slice(w * width + 128 * j, w * width + 128 * (j + 1))
                block = ref[chunk * j : chunk * (j + 1), :, 128 * w : 128 * (w + 1)]
                out_ref[lines, lanes] = block.reshape(half, 128).astype(f32)
        tail = ref[:, :, 3 * 128 :].astype(f32).reshape(-1, 128)
        lines = pl.ds(pl.multiple_of(kept * rows, 8), rows)
        blocks = width // 128
        for i in range(blocks):
            pos_ref[lines, 128 * i : 128 * (i + 1)] = tail[rows * i : rows * (i + 1)]
            if ref is mine_ref:
                base = rows * blocks + 16 * i
                for n, vec_ref in enumerate(vec_refs):
                    for line in range(vec_ref.shape[1] // width):
                        lanes = slice(width * line + 128 * i, width * line + 128 * (i + 1))
                        vec_ref[:, lanes] = tail[base + n + line : base + n + line + 1]


def unpack_rest(scalar, mine, other, rows, width, hidden):
    return call(
        unpack_rest_kernel,
        "unpack_rest",
        scalar,
        [mine, other],
        [sds((width, 3 * width), f32), sds((rows, width), f32)]
        + [sds((1, width), f32)] * 9
        + [sds((1, hidden), f32)],
    )


def shift(array, axis, step):
    size = lax.axis_size(axis)
    return lax.ppermute(array, axis, [(i, (i + step) % size) for i in range(size)])


def peers(array, axis):
    return [shift(array, axis, step) for step in (1, 3, 2)]


def swap(array):
    return shift(array, "core", 1)


def total(parts):
    return functools.reduce(jnp.add, [p.astype(f32) for p in parts])


SPACE = ("x", "z", "y")
PLANE = ("z", "y", "core")


def step_plane(array, step, near):
    sizes = [lax.axis_size(name) for name in PLANE]
    pairs = []
    for z in range(sizes[0]):
        for y in range(sizes[1]):
            for core in range(sizes[2]):
                if (core == 0) == near:
                    target = (z, (y + step) % sizes[1], core)
                else:
                    target = ((z + step) % sizes[0], y, core)
                index = lambda p: (p[0] * sizes[1] + p[1]) * sizes[2] + p[2]
                pairs.append((index((z, y, core)), index(target)))
    return lax.ppermute(array, PLANE, pairs)


def step_cores(array):
    size = lax.axis_size("x")
    pairs = []
    for core in range(2):
        for x in range(size):
            pairs.append((core * size + x, core * size + (x + 1 - 2 * core) % size))
    return lax.ppermute(array, ("core", "x"), pairs)


def plane_peers(array, near):
    return [step_plane(array, step, near) for step in (2, 1, 3)]


def exchange(array, axes):
    return lax.all_to_all(array, axes, 0, 0, tiled=True)


def body(
    vis,
    keep_slots,
    counts,
    band_mask,
    mask_token,
    pos,
    ln1_gain,
    ln1_bias,
    w_qkv,
    b_query,
    b_value,
    w_out,
    b_out,
    ln2_gain,
    ln2_bias,
    w_up,
    b_up,
    w_down,
    b_down,
    d_out,
):
    barrier = lax.optimization_barrier
    x = lax.axis_index("x")
    core = lax.axis_index("core")
    piece = keep_slots.shape[1]
    rows, width = pos.shape
    half = rows // 2
    hidden = w_up.shape[1]

    vis = vis[0]

    y, z = lax.axis_index("y"), lax.axis_index("z")
    relative, far = jnp.array(RELATIVE, jnp.int32), jnp.array(OPPOSITE, jnp.int32)
    order = (x + relative) % GROUPS
    live = jnp.sum(jnp.where(order[:, None] == jnp.arange(GROUPS)[None, :], band_mask, 0), axis=1)
    here = (x * lax.axis_size("z") + z) * lax.axis_size("y") + y
    chunks = width // 128 * half // 16
    shared = (here >= chunks) & (here < chunks + width // 128)
    scalar = jnp.concatenate(
        [live, order * rows, jnp.stack([core, shared.astype(jnp.int32), y, z]), (z + far) % GROUPS, (x + far) % GROUPS]
    ).astype(jnp.int32)
    pack = lambda *vs: jnp.pad(jnp.stack(vs), ((0, 8 - len(vs)), (0, 0)))
    vectors = pack(mask_token, ln1_gain, ln1_bias, b_query, b_value)
    feed_vectors = pack(b_out, ln2_gain, ln2_bias, b_down)

    index = lax.broadcasted_iota(jnp.int32, (1, piece), 1)
    code = jnp.where(index < counts, keep_slots, -1) + 1
    marks = jnp.concatenate([code // 64, code % 64], axis=0).astype(bf)
    marks = jnp.pad(marks, ((0, MARKS - 2), (0, width - piece)))
    message = jnp.concatenate([marks, vis], axis=0)
    pieces = [message] + [shift(message, "x", step) for step in (2, 1, 3)]
    pos_half = lax.dynamic_slice(pos, (half * core, 0), (half, width))
    pos_mine = [step_cores(pos), shift(pos_half, "x", 2)]
    scalar, vectors, feed_vectors, pieces = barrier((scalar, vectors, feed_vectors, pieces))
    aux, *bases = front(scalar, pieces, vectors, rows)
    start, q, turned_own, k_own, v_own, *state, p_own = attention_own(scalar, bases[0], pos, vectors, w_qkv)
    state, pos_mine = barrier((state, pos_mine))
    pos_other = [swap(p) for p in pos_mine]
    out = middle(scalar, bases[1:], pos_mine + pos_other, vectors, w_qkv, q, state)
    rest, (mixed, lse), kept = out[: 3 * (GROUPS - 1)], out[3 * (GROUPS - 1) :][:2], out[3 * (GROUPS - 1) + 2 :]
    keys, values = [k_own, *rest[1::3]], [v_own, *rest[2::3]]
    weights, peaks = [p_own, *kept[0::2]], [state[0], *kept[1::2]]

    out, middle_rows, second, kept, sent, grad_b_up = feed_forward(
        scalar, mixed, start, d_out[0], w_out, feed_vectors, w_up, b_up[None], w_down
    )
    got = swap(sent)
    grad_middle, grad_mixed, out_kept, out_sent, feed_vec = feed_backward(
        scalar, mixed, middle_rows, second, d_out[0], w_out, feed_vectors
    )
    factors = softmax_factors(scalar, mixed, grad_mixed, lse, peaks)
    inputs = list(zip(factors[:GROUPS], weights, keys, values, factors[GROUPS:]))
    feed = fold_feed(scalar, kept, got, out_kept, swap(out_sent))
    inputs, feed = barrier((inputs, feed))
    feed = [feed[0]] + [step_plane(feed[r], r, True) for r in (1, 2, 3)]
    dq, d_3, part = attention_grad(scalar, (3,), q, w_qkv, [inputs[3]], None)
    dq, part = barrier((dq, part))
    from_3 = shift(part, "x", 2)
    dq, d_1, part = attention_grad(scalar, (1,), q, w_qkv, [inputs[1]], dq)
    feed = fold_line(scalar, feed)
    dq, part, feed = barrier((dq, part, feed))
    feed = [feed[0]] + [shift(feed[r], "x", r) for r in (2, 1, 3)]
    from_1 = shift(part, "x", 3)
    dq, d_2, part = attention_grad(scalar, (2,), q, w_qkv, [inputs[2]], dq)
    feed = add_up(scalar, "fold_point", feed)
    dq, part, from_3, feed = barrier((dq, part, from_3, feed))
    feed_peers = [step_plane(feed, step, False) for step in (1, 3, 2)]
    from_2 = shift(part, "x", 1)
    part, at_kept, at_sent, grad_b_query, grad_b_value = attention_grad(
        scalar, (0,), q, w_qkv, [inputs[0]], dq, [turned_own, *rest[0::3], d_3, d_1, d_2]
    )
    at_kept, at_sent, part, from_1, from_2, feed_peers = barrier(
        (at_kept, at_sent, part, from_1, from_2, feed_peers)
    )

    at_got = swap(at_sent)
    feed = add_up(scalar, "sum_line", [feed] + feed_peers)
    gathered = [shift(feed, "x", step) for step in (2, 1, 3)]
    tail_kept, tail_sent, low = finish(
        scalar,
        part,
        (from_3, from_1, from_2),
        start,
        grad_middle,
        vectors,
        aux,
        grad_b_query,
        grad_b_value,
        feed_vec,
        grad_b_up,
    )
    spread = lambda a: a.reshape(GROUPS * SPREAD, 16, -1)
    bundle = fold_rest(scalar, spread(at_kept), spread(at_got), tail_kept, swap(tail_sent))
    bundle, feed = barrier((bundle, jnp.stack([feed] + gathered)))
    bundle = exchange(bundle, SPACE)
    feed_other = [swap(feed)]
    feed = [feed] + plane_peers(feed, True)
    bundle, shares, feed_other = barrier((bundle, share(scalar, low, aux, piece), feed_other))
    bundle = sum_space(scalar, bundle)
    feed, _ = barrier((feed, bundle))
    rest_mine = exchange(bundle, SPACE)
    feed_other += [swap(a) for a in feed[1:]]
    shares = list(shares)
    feed_other[1], shares[1] = barrier((feed_other[1], shares[1]))
    returned = [shares[0], shift(shares[3], "x", 1), shift(shares[2], "x", 3), shift(shares[1], "x", 2)]
    grad_w_down, grad_w_up, grad_w_out = unpack_feed(scalar, feed, feed_other, width, hidden)
    grad_vis = collect(scalar, aux, returned, rows, piece)
    rest_mine, grad_w_down, grad_vis = barrier((rest_mine, grad_w_down, grad_vis))
    rest_other = swap(rest_mine)
    grad_w_qkv, grad_pos, *sums = unpack_rest(scalar, rest_mine, rest_other, rows, width, hidden)
    sums = [a[0] for a in sums]

    return (
        out[None],
        grad_vis[None],
        sums[0],
        grad_pos,
        sums[1],
        sums[2],
        grad_w_qkv,
        sums[3],
        sums[4],
        grad_w_out,
        sums[5],
        sums[6],
        sums[7],
        grad_w_up,
        sums[9],
        grad_w_down,
        sums[8],
    )


CUBE = ("z", "y", "core")


def solution(mesh):
    fine = Mesh(mesh.devices.reshape(4, 4, 2, 4), ("z", "y", "core", "x"))
    return jax.shard_map(
        body,
        mesh=fine,
        in_specs=(
            P(CUBE, "x", None),
            P(CUBE, "x"),
            P(CUBE, "x"),
            P(CUBE, None),
            P(),
            P("x", None),
        )
        + (P(),) * 13
        + (P(CUBE, "x", None),),
        out_specs=(P(CUBE, "x", None), P(CUBE, "x", None), P(), P("x", None)) + (P(),) * 13,
        check_vma=False,
    )
```

```python
import functools

import jax
import jax.numpy as jnp
from jax import lax
from jax.experimental import pallas as pl
from jax.experimental.pallas import tpu as pltpu
from jax.sharding import Mesh, PartitionSpec as P

bf = jnp.bfloat16
f32 = jnp.float32

HEADS = 16
DEPTH = 32
QUAD = 4
GROUPS = 4
LOG2E = 1.4426950408889634
SCALE = DEPTH**-0.5
EPS = 1e-05
BIG = 1e30
GELU_SCALE = 0.7978845608028654
GELU_CUBE = 0.044715
RELATIVE = (0, 3, 1, 2)
OPPOSITE = (0, 2, 3, 1)
CAP = 80
MARKS = 16
SPREAD = 16

NT = (((1,), (1,)), ((), ()))
NN = (((1,), (0,)), ((), ()))
TN = (((0,), (0,)), ((), ()))
VMEM_LIMIT = 56 * 1024 * 1024


def dg(a, b, dims):
    return lax.dot_general(a, b, dims, preferred_element_type=f32)


def sds(shape, dtype):
    return jax.ShapeDtypeStruct(shape, dtype)


def call(kernel, name, scalar, operands, out_shape, scratch=(), aliases=None, limit=5, micro=0.001):
    inside = pl.BlockSpec(memory_space=pltpu.VMEM)
    return pl.pallas_call(
        kernel,
        in_specs=[pl.BlockSpec(memory_space=pltpu.SMEM)] + [inside] * len(operands),
        out_specs=[inside] * len(out_shape),
        out_shape=out_shape,
        scratch_shapes=list(scratch),
        compiler_params=pltpu.CompilerParams(vmem_limit_bytes=limit * 1024 * 1024),
        cost_estimate=pl.CostEstimate(flops=int(micro * 1e9), bytes_accessed=1000, transcendentals=0),
        input_output_aliases=aliases or {},
        name=name,
    )(scalar, *operands)


def grid_call(kernel, name, scalar, steps, in_specs, out_specs, out_shape, operands):
    return pl.pallas_call(
        kernel,
        grid_spec=pltpu.PrefetchScalarGridSpec(
            num_scalar_prefetch=1, grid=(steps,), in_specs=in_specs, out_specs=out_specs
        ),
        out_shape=out_shape,
        compiler_params=pltpu.CompilerParams(vmem_limit_bytes=32 * 1024 * 1024),
        cost_estimate=pl.CostEstimate(flops=1000, bytes_accessed=1000, transcendentals=0),
        name=name,
    )(scalar, *operands)


def column_sum(tensor):
    return jnp.sum(tensor.astype(f32), axis=0, keepdims=True)


def norm_parts(values):
    centered = values - jnp.mean(values, axis=-1, keepdims=True)
    variance = jnp.mean(centered * centered, axis=-1, keepdims=True)
    inverse = lax.rsqrt(variance + EPS)
    return centered * inverse, inverse


def norm_pull(grad, n, inverse, gain):
    g = grad * gain
    return inverse * (
        g - jnp.mean(g, axis=-1, keepdims=True) - n * jnp.mean(g * n, axis=-1, keepdims=True)
    )


def place_rows(base, pieces, ids, rows, rows_ref):
    piece, width = ids[0].shape[1], rows_ref.shape[1]
    slot = lax.broadcasted_iota(jnp.int32, (rows, piece), 0) + base
    placed = jnp.zeros((rows, width), f32)
    taken = jnp.zeros((rows, piece), f32)
    for v, i in zip(pieces, ids):
        hot = (slot == i).astype(f32)
        taken += hot
        placed += dg(hot.astype(bf), v[MARKS : MARKS + piece, :], NN)
    unseen = 1.0 - jnp.sum(taken, axis=1, keepdims=True)
    return placed + unseen * rows_ref[0:1], unseen


def first_norm(start, rows_ref):
    n, _ = norm_parts(start)
    return (n * rows_ref[1:2] + rows_ref[2:3]).astype(bf)


def keys_values(normed, rows_ref, w_ref, turned_ref, k_ref, v_ref):
    width = normed.shape[1]
    k_ref[...] = dg(normed, w_ref[:, width : 2 * width], NN).astype(bf)
    v_ref[...] = (dg(normed, w_ref[:, 2 * width :], NN) + rows_ref[4:5]).astype(bf)
    turned_ref[...] = normed.T


def stack_heads(x):
    lane = lax.broadcasted_iota(jnp.int32, x.shape, 1) // DEPTH
    return jnp.concatenate([jnp.where(lane == h, x, jnp.zeros_like(x)) for h in range(QUAD)], axis=0)


def unstack_heads(xt):
    rows = xt.shape[1] // QUAD
    parts = [xt[DEPTH * h : DEPTH * (h + 1), rows * h : rows * (h + 1)] for h in range(QUAD)]
    return jnp.concatenate(parts, axis=0).T


def fwd_steps(steps, scalar_ref, query, key, value, state, keep_weights, finish):
    stacked = {}

    def scores(quad, group):
        if quad not in stacked:
            stacked[quad] = stack_heads(query(quad))
        return dg(key(quad, group), stacked[quad], NT)

    ahead = scores(*steps[0])
    for i, (quad, group) in enumerate(steps):
        s = ahead
        if i + 1 < len(steps):
            ahead = scores(*steps[i + 1])
        live = scalar_ref[group] > 0
        peak = jnp.where(live, jnp.max(s, axis=0, keepdims=True), -BIG)
        old = state(quad) if i == 0 or steps[i - 1][0] != quad else new
        if old is not None:
            peak = jnp.maximum(old[0], peak)
        p = jnp.exp2(s - jnp.where(live, peak, BIG)).astype(bf)
        keep_weights(quad, group, p, peak)
        v = value(quad, group)
        turned = jnp.concatenate([v.T, jnp.ones((16, v.shape[0]), bf)], axis=0)
        both = dg(turned, p, NN)
        o, l = both[: v.shape[1]], both[v.shape[1] : v.shape[1] + 1]
        if old is not None:
            keep = jnp.exp2(old[0] - peak)
            o += old[2] * keep
            l += old[1] * keep
        new = (peak, l, o)
        if i + 1 == len(steps) or steps[i + 1][0] != quad:
            finish(quad, new)


def quad_at(quad):
    return (slice(None), slice(128 * quad, 128 * (quad + 1)))


def front_kernel(scalar_ref, *refs):
    pieces, (rows_ref, aux_ref), bases = refs[:GROUPS], refs[GROUPS : GROUPS + 2], refs[GROUPS + 2 :]
    rows = bases[0].shape[0]
    piece = pieces[0].shape[0] - MARKS
    ids = []
    for i, v in enumerate(pieces):
        marks = v[:MARKS, :].astype(f32)[:8, :piece]
        line = marks[0:1] * 64.0 + marks[1:2] - 1.0
        aux_ref[rows + i : rows + i + 1, :piece] = line
        ids.append(line.astype(jnp.int32))
    for g, base in enumerate(bases):
        base[...], unseen = place_rows(scalar_ref[GROUPS + g], pieces, ids, rows, rows_ref)
        if g == 0:
            aux_ref[:rows, :128] = jnp.broadcast_to(unseen, (rows, 128))


def read_slots(aux_ref, count, piece):
    rows = aux_ref.shape[0] - 8
    return [aux_ref[rows + i : rows + i + 1, :piece].astype(jnp.int32) for i in range(count)]


def front(scalar, pieces, vectors, rows):
    width = vectors.shape[1]
    return call(
        front_kernel,
        "front",
        scalar,
        [*pieces, vectors],
        [sds((rows + 8, 256), f32)] + [sds((rows, width), f32)] * GROUPS,
        micro=4,
    )


def attention_own_kernel(
    scalar_ref,
    base_ref,
    pos_ref,
    rows_ref,
    w_ref,
    start_ref,
    q_ref,
    turned_ref,
    k_ref,
    v_ref,
    m_ref,
    l_ref,
    o_ref,
    p_ref,
):
    start = base_ref[...] + pos_ref[...].astype(f32)
    start_ref[...] = start
    normed = first_norm(start, rows_ref)
    width = normed.shape[1]
    q_ref[...] = ((dg(normed, w_ref[:, :width], NN) + rows_ref[3:4]) * (SCALE * LOG2E)).astype(bf)
    keys_values(normed, rows_ref, w_ref, turned_ref, k_ref, v_ref)

    def keep_weights(quad, group, p, peak):
        p_ref[quad] = p

    def finish(quad, state):
        m_ref[quad], l_ref[quad], o_ref[quad] = state

    fwd_steps(
        [(quad, 0) for quad in range(m_ref.shape[0])],
        scalar_ref,
        lambda quad: q_ref[quad_at(quad)],
        lambda quad, group: k_ref[quad_at(quad)],
        lambda quad, group: v_ref[quad_at(quad)],
        lambda quad: None,
        keep_weights,
        finish,
    )


def attention_own(scalar, base, pos, vectors, w_qkv):
    rows, width = pos.shape
    quads, n = width // 128, rows * QUAD
    return call(
        attention_own_kernel,
        "attention_own",
        scalar,
        [base, pos, vectors, w_qkv],
        [
            sds((rows, width), f32),
            sds((rows, width), bf),
            sds((width, rows), bf),
            sds((rows, width), bf),
            sds((rows, width), bf),
            sds((quads, 1, n), f32),
            sds((quads, 1, n), f32),
            sds((quads, 128, n), f32),
            sds((quads, rows, n), bf),
        ],
        limit=7,
        micro=5,
    )


def middle_kernel(scalar_ref, *refs):
    bases, refs = refs[: GROUPS - 1], refs[GROUPS - 1 :]
    pos_refs, refs = refs[:4], refs[4:]
    rows_ref, w_ref, q_ref, m_ref, l_ref, o_ref, *refs = refs
    groups, (mixed_ref, lse_ref), kept = refs[: 3 * (GROUPS - 1)], refs[3 * (GROUPS - 1) :][:2], refs[3 * (GROUPS - 1) + 2 :]
    first = scalar_ref[GROUPS + GROUPS] == 0
    near, far, other_near, other_far = [ref[...].astype(f32) for ref in pos_refs]
    for g, base in enumerate(bases):
        if g < 2:
            pos = jnp.where(first == (g == 0), near, other_near)
        else:
            pos = jnp.concatenate([jnp.where(first, far, other_far), jnp.where(first, other_far, far)], axis=0)
        keys_values(first_norm(base[...] + pos, rows_ref), rows_ref, w_ref, *groups[3 * g : 3 * g + 3])

    def keep_weights(quad, group, p, peak):
        kept[2 * group - 2][quad] = p
        kept[2 * group - 1][quad] = peak

    def finish(quad, state):
        m, l, o = state
        mixed_ref[quad_at(quad)] = unstack_heads(o / l).astype(bf)
        lse_ref[quad] = m + jnp.log2(l)

    fwd_steps(
        [(quad, group) for quad in range(m_ref.shape[0]) for group in range(1, GROUPS)],
        scalar_ref,
        lambda quad: q_ref[quad_at(quad)],
        lambda quad, group: groups[3 * group - 2][quad_at(quad)],
        lambda quad, group: groups[3 * group - 1][quad_at(quad)],
        lambda quad: (m_ref[quad], l_ref[quad], o_ref[quad]),
        keep_weights,
        finish,
    )


def middle(scalar, bases, pos, vectors, w_qkv, q, state):
    rows, width = q.shape
    quads, n = width // 128, rows * QUAD
    group = [sds((width, rows), bf), sds((rows, width), bf), sds((rows, width), bf)]
    return call(
        middle_kernel,
        "middle",
        scalar,
        [*bases, *pos, vectors, w_qkv, q, *state],
        [*(group * (GROUPS - 1)), sds((rows, width), bf), sds((quads, 1, n), f32)]
        + [sds((quads, rows, n), bf), sds((quads, 1, n), f32)] * (GROUPS - 1),
        limit=9,
    )


def bwd_kernel(scalar_ref, q_ref, w_ref, *refs, groups, carried):
    width = q_ref.shape[1]
    inputs, refs = [refs[5 * i : 5 * i + 5] for i in range(len(groups))], refs[5 * len(groups) :]
    if carried:
        dq_in, *refs = refs
    own = groups == (0,)
    if own:
        *turned_refs, d_3, d_1, d_2, part_ref, kept_ref, sent_ref, bq_ref, bv_ref, d_s = refs
        base, outs = width, [(d_s, part_ref)]
    else:
        dq_ref, *refs = refs
        base, outs = 0, [refs[2 * i : 2 * i + 2] for i in range(len(groups))]
    quads = width // 128
    (do_ref, p_ref, k_ref, v_ref, delta_ref), (d_ref, _) = inputs[0], outs[0]

    def ahead(j):
        dos = stack_heads(do_ref[quad_at(j)])
        return dos, dg(v_ref[quad_at(j)], dos, NT)

    later = ahead(0)
    for j in range(quads):
        at = quad_at(j)
        dos, products = later
        if j + 1 < quads:
            later = ahead(j + 1)
        columns = lambda i: (
            slice(None),
            slice(base + (i - 1) * width + 128 * j, base + (i - 1) * width + 128 * (j + 1)),
        )
        qs = stack_heads(q_ref[at])
        k, p = k_ref[at], p_ref[j]
        ds = (p.astype(f32) * (products - delta_ref[j])).astype(bf)
        d_ref[columns(2)] = dg(p, dos, NN).astype(bf)
        d_ref[columns(1)] = (dg(ds, qs, NN) * (1.0 / LOG2E)).astype(bf)
        dq = unstack_heads(dg(k, ds, TN))
        if carried:
            dq += dq_in[at]
        if own:
            d_s[at] = (dq * SCALE).astype(bf)
        else:
            dq_ref[at] = dq
    for d_ref, part_ref in outs:
        grads = d_ref[...]
        part_ref[...] = dg(grads, w_ref[...] if own else w_ref[:, width:], NT).astype(part_ref.dtype)
    if not own:
        return
    own, *rest = turned_refs
    g = dg(own[...], grads[:, width:], NN)
    bv = column_sum(grads[:, 2 * width :])
    for turned, d_ref in zip(rest, (d_1, d_2, d_3)):
        d = d_ref[...]
        g += dg(turned[...], d, NN)
        bv += column_sum(d[:, width:])
    bv_ref[...] = bv
    bq_ref[...] = column_sum(grads[:, :width])
    gq = dg(own[...], grads[:, :width], NN)
    first = scalar_ref[GROUPS + 4] == 0
    half = width // 2
    for j in range(quads):
        at = slice(128 * j, 128 * (j + 1))
        block = jnp.concatenate([gq[:, at], g[:, at], g[:, width + 128 * j : width + 128 * (j + 1)]], axis=1)
        kept_ref[j] = jnp.where(first, block[:half], block[half:]).astype(bf)
        sent_ref[j] = jnp.where(first, block[half:], block[:half]).astype(bf)


def attention_grad(scalar, groups, q, w_qkv, inputs, dq, more=()):
    rows, width = q.shape
    quads = width // 128
    operands = [q, w_qkv] + [a for group in inputs for a in group]
    aliases = {}
    if dq is not None:
        aliases = {len(operands) + 1: 0}
        operands.append(dq)
    operands += list(more)
    scratch = []
    if groups == (0,):
        packed = (quads, width // 2, 3 * 128)
        out_shape = [sds((rows, width), f32)] + [sds(packed, bf)] * 2 + [sds((1, width), f32)] * 2
        scratch = [pltpu.VMEM((rows, 3 * width), bf)]
    else:
        out_shape = [sds((rows, width), f32)]
        out_shape += [sds((rows, 2 * width), bf), sds((rows, width), bf)] * len(groups)
    return call(
        functools.partial(bwd_kernel, groups=groups, carried=dq is not None),
        "attention_grad_" + "_".join(str(g) for g in groups),
        scalar,
        operands,
        out_shape,
        scratch,
        aliases,
        limit=9,
    )


def feed_kernel(
    scalar_ref,
    mixed_ref,
    start_ref,
    dout_ref,
    wout_ref,
    rows_ref,
    wup_ref,
    bup_ref,
    wdown_ref,
    out_ref,
    middle_ref,
    second_ref,
    kept_ref,
    sent_ref,
    gbup_ref,
):
    first = scalar_ref[GROUPS + 4] == 0
    width = mixed_ref.shape[1]
    hidden = wup_ref.shape[1]
    dout = dout_ref[...]
    middle = start_ref[...] + (dg(mixed_ref[...], wout_ref[...], NN) + rows_ref[0:1])
    middle_ref[...] = middle
    n, _ = norm_parts(middle)
    normed = (n * rows_ref[1:2] + rows_ref[2:3]).astype(bf)
    turned = normed.T
    result = middle + rows_ref[3:4]
    second = jnp.zeros_like(middle)
    lines = hidden // SPREAD
    for h in range(hidden // width):
        at = slice(width * h, width * (h + 1))
        u = dg(normed, wup_ref[:, at], NN) + bup_ref[:, at]
        square = u * u
        t = jnp.tanh(u * (GELU_SCALE + (GELU_SCALE * GELU_CUBE) * square))
        near = 0.5 + 0.5 * t
        act = (u * near).astype(bf)
        result += dg(act, wdown_ref[at, :], NN)
        slope = near + u * (0.5 - 0.5 * (t * t)) * (GELU_SCALE + (3.0 * GELU_SCALE * GELU_CUBE) * square)
        gup = (dg(dout, wdown_ref[at, :], NT) * slope).astype(bf)
        second += dg(gup, wup_ref[:, at], NT)
        gbup_ref[:, at] = column_sum(gup)
        down = dg(act, dout, TN).astype(bf)
        up = dg(turned, gup, NN).astype(bf)
        chunks = (width // lines, lines, width)
        places = slice(h * chunks[0], (h + 1) * chunks[0])
        kept_ref[places] = jnp.where(first, down, up).reshape(chunks)
        sent_ref[places] = jnp.where(first, up, down).reshape(chunks)
    out_ref[...] = result.astype(bf)
    second_ref[...] = second


def feed_backward_kernel(
    scalar_ref,
    mixed_ref,
    middle_ref,
    second_ref,
    dout_ref,
    wout_ref,
    rows_ref,
    gmid_ref,
    gmix_ref,
    kept_ref,
    sent_ref,
    vec_ref,
):
    first = scalar_ref[GROUPS + 4] == 0
    mixed = mixed_ref[...]
    width = mixed.shape[1]
    second = second_ref[...]
    grad = dout_ref[...].astype(f32)
    n, inverse = norm_parts(middle_ref[...])
    gmid = grad + norm_pull(second, n, inverse, rows_ref[1:2])
    gmid_ref[...] = gmid
    branch = gmid.astype(bf)
    gmix_ref[...] = dg(branch, wout_ref[...], NT).astype(bf)
    wout = dg(mixed, branch, TN)
    half = width // 2
    extra = (SPREAD, half // SPREAD, width)
    kept_ref[...] = jnp.where(first, wout[:half], wout[half:]).astype(bf).reshape(extra)
    sent_ref[...] = jnp.where(first, wout[half:], wout[:half]).astype(bf).reshape(extra)
    vec_ref[...] = jnp.concatenate(
        [
            column_sum(branch),
            column_sum(second * n),
            column_sum(second),
            column_sum(grad),
            jnp.zeros((4, width), f32),
        ],
        axis=0,
    )


def factor_kernel(scalar_ref, mixed_ref, gmix_ref, lse_ref, *refs):
    peaks, outs = refs[:GROUPS], refs[GROUPS:]
    gmix = gmix_ref[...].astype(f32)
    width = gmix.shape[1]
    product = mixed_ref[...].astype(f32) * gmix
    head = lax.broadcasted_iota(jnp.int32, (HEADS, width), 0)
    lane = lax.broadcasted_iota(jnp.int32, (HEADS, width), 1) // DEPTH
    pick = (head == lane).astype(bf)
    halves = lambda a: (a.astype(bf), (a - a.astype(bf).astype(f32)).astype(bf))
    high, low = halves(product)
    delta = dg(pick, high, NT) + dg(pick, low, NT)
    rows = delta.shape[1]
    for peak_ref, do_ref, delta_ref in zip(peaks, outs[:GROUPS], outs[GROUPS:]):
        lines = []
        for j in range(HEADS // QUAD):
            factor = jnp.exp2(peak_ref[j] - lse_ref[j])
            delta_ref[j] = factor * jnp.concatenate([delta[QUAD * j + i : QUAD * j + i + 1] for i in range(QUAD)], axis=1)
            lines += [factor[:, rows * i : rows * (i + 1)] for i in range(QUAD)]
        high, low = halves(jnp.concatenate(lines, axis=0))
        do_ref[...] = (gmix * (dg(high, pick, TN) + dg(low, pick, TN))).astype(bf)


def feed_forward(scalar, mixed, start, d_out, w_out, vectors, w_up, b_up, w_down):
    rows, width = mixed.shape
    hidden = w_up.shape[1]
    packed = (SPREAD, hidden // SPREAD, width)
    return call(
        feed_kernel,
        "feed_forward",
        scalar,
        [mixed, start, d_out, w_out, vectors, w_up, b_up, w_down],
        [sds((rows, width), bf)] + [sds((rows, width), f32)] * 2 + [sds(packed, bf)] * 2 + [sds((1, hidden), f32)],
        limit=11,
    )


def feed_backward(scalar, mixed, middle, second, d_out, w_out, vectors):
    rows, width = mixed.shape
    packed = (SPREAD, width // 2 // SPREAD, width)
    return call(
        feed_backward_kernel,
        "feed_backward",
        scalar,
        [mixed, middle, second, d_out, w_out, vectors],
        [sds((rows, width), f32), sds((rows, width), bf), sds(packed, bf), sds(packed, bf), sds((8, width), f32)],
    )


def softmax_factors(scalar, mixed, gmix, lse, peaks):
    return call(
        factor_kernel,
        "softmax_factors",
        scalar,
        [mixed, gmix, lse, *peaks],
        [sds(gmix.shape, bf)] * GROUPS + [sds(lse.shape, f32)] * GROUPS,
        micro=2,
    )


def turn(place, steps):
    return lax.rem(place + steps, GROUPS)


def fold_feed_kernel(scalar_ref, a, b, c, d, *outs):
    first, y, z = scalar_ref[GROUPS + 4] == 0, scalar_ref[GROUPS + 6], scalar_ref[GROUPS + 7]
    near = jnp.where(first, y, z)
    lines = a.shape[1]
    for r, out_ref in enumerate(outs):
        place = turn(near, r)
        for i in range(GROUPS):
            at = jnp.where(first, GROUPS * i + place, GROUPS * place + i)
            out_ref[i, :lines] = a[at] + b[at]
            out_ref[i, lines:] = c[at] + d[at]


def fold_feed(scalar, a, b, c, d):
    shape = sds((GROUPS, a.shape[1] + c.shape[1], a.shape[2]), bf)
    return call(fold_feed_kernel, "fold_feed", scalar, [a, b, c, d], [shape] * GROUPS)


def fold_line_kernel(scalar_ref, *refs):
    sources, outs = refs[:GROUPS], refs[GROUPS:]
    for r, out_ref in enumerate(outs):
        at = turn(scalar_ref[GROUPS + 12], r)
        out_ref[...] = sum(ref[at].astype(f32) for ref in sources).astype(bf)


def fold_line(scalar, sources):
    return call(fold_line_kernel, "fold_line", scalar, sources, [sds(sources[0].shape[1:], bf)] * GROUPS)


def add_up_kernel(scalar_ref, *refs):
    *sources, out_ref = refs
    out_ref[...] = sum(ref[...].astype(f32) for ref in sources).astype(bf)


def add_up(scalar, name, arrays):
    return call(add_up_kernel, name, scalar, list(arrays), [sds(arrays[0].shape, bf)])[0]


def fold_rest_kernel(scalar_ref, a, b, c, d, out_ref):
    cut = a.shape[2]
    out_ref[:, :, :cut] = a[...] + b[...]
    out_ref[:, :, cut:] = c[...] + d[...]


def fold_rest(scalar, a, b, c, d):
    shape = a.shape[:2] + (a.shape[2] + c.shape[2],)
    return call(fold_rest_kernel, "fold_rest", scalar, [a, b, c, d], [sds(shape, bf)])[0]


def sum_space_kernel(scalar_ref, got_ref, out_ref):
    chunk = got_ref.shape[0] // GROUPS
    lanes = 3 * 128
    sums = []
    for x in range(GROUPS):
        acc = got_ref[chunk * x].astype(f32)
        for i in range(1, chunk):
            acc += got_ref[chunk * x + i].astype(f32)
        sums.append(acc)
    everything = functools.reduce(jnp.add, sums)
    shared = scalar_ref[GROUPS + 5] > 0
    for x in range(GROUPS):
        tail = jnp.where(shared, everything[:, lanes:], sums[x][:, lanes:])
        block = jnp.concatenate([everything[:, :lanes], tail], axis=1).astype(bf)
        for i in range(chunk):
            out_ref[chunk * x + i] = block


def sum_space(scalar, got):
    return call(sum_space_kernel, "sum_space", scalar, [got], [sds(got.shape, bf)])[0]


def finish_kernel(
    scalar_ref,
    part_ref,
    r3,
    r1,
    r2,
    start_ref,
    gmid_ref,
    rows_ref,
    unseen_ref,
    bq_ref,
    bv_ref,
    feed_ref,
    bup_ref,
    kept_ref,
    sent_ref,
    low_ref,
):
    rows, width = start_ref.shape
    first_grad = part_ref[...] + r3[...].astype(f32) + r1[...].astype(f32) + r2[...].astype(f32)
    n, inverse = norm_parts(start_ref[...])
    grad = gmid_ref[...] + norm_pull(first_grad, n, inverse, rows_ref[1:2])
    low_ref[...] = grad.astype(bf)
    half = rows // 2
    first = scalar_ref[GROUPS + 4] == 0
    top, low = grad[:half], grad[half:]
    lines = [
        column_sum(unseen_ref[:rows, :1] * grad),
        column_sum(first_grad * n),
        column_sum(first_grad),
        bq_ref[...],
        bv_ref[...],
        feed_ref[:4],
    ]
    blocks = bup_ref.shape[1] // width
    lines += [bup_ref[:, width * i : width * (i + 1)] for i in range(blocks)]
    spare = 16 - sum(a.shape[0] for a in lines)
    lines = jnp.concatenate(lines + [jnp.zeros((spare, width), f32)], axis=0)

    def narrow(values):
        cut = [a[:, 128 * i : 128 * (i + 1)] for a in (values, lines) for i in range(width // 128)]
        cut.append(jnp.zeros((kept_ref.shape[0] * kept_ref.shape[1] - sum(a.shape[0] for a in cut), 128), f32))
        return jnp.concatenate(cut, axis=0).reshape(kept_ref.shape).astype(bf)

    kept_ref[...] = narrow(jnp.where(first, top, low))
    sent_ref[...] = narrow(jnp.where(first, low, top))


def finish(scalar, part, received, start, gmid, vectors, unseen, bq, bv, feed_vec, grad_b_up):
    rows, width = start.shape
    tail = sds((GROUPS * SPREAD, 16, 128), bf)
    return call(
        finish_kernel,
        "finish",
        scalar,
        [part, *received, start, gmid, vectors, unseen, bq, bv, feed_vec, grad_b_up],
        [tail, tail, sds((rows, width), bf)],
        micro=8,
    )


def ranked(lines, bases, rows):
    piece = lines[0].shape[1]
    flags = [((ids >= base) & (ids < base + rows)).astype(f32) for ids, base in zip(lines, bases)]
    flags = jnp.concatenate(flags + [jnp.zeros((8 - len(flags), piece), f32)], axis=0).astype(bf)
    row = lax.broadcasted_iota(jnp.int32, (piece, piece), 0)
    column = lax.broadcasted_iota(jnp.int32, (piece, piece), 1)
    rank = dg((column < row).astype(bf), flags, NT)
    here = dg((column == row).astype(bf), flags, NT)
    place = lax.broadcasted_iota(jnp.int32, (piece, CAP), 1).astype(f32)
    return [jnp.where(rank[:, i : i + 1] == place, here[:, i : i + 1], 0.0).astype(bf) for i in range(len(lines))]


def share_kernel(scalar_ref, low_ref, aux_ref, *refs, piece):
    outs, (share_ref, sem) = refs[:GROUPS], refs[GROUPS:]
    rows = low_ref.shape[0]
    base = scalar_ref[GROUPS]
    slot = lax.broadcasted_iota(jnp.int32, (rows, piece), 0) + base
    lines = read_slots(aux_ref, GROUPS, piece)
    for i, (ids, rank) in enumerate(zip(lines, ranked(lines, [base] * GROUPS, rows))):
        pick = dg((slot == ids).astype(bf), rank, NN).astype(bf)
        share_ref[i] = dg(pick, low_ref[...], TN).astype(bf)
    copies = [pltpu.make_async_copy(share_ref.at[i], out, sem.at[i]) for i, out in enumerate(outs)]
    for copy in copies:
        copy.start()
    for copy in copies:
        copy.wait()


def share(scalar, low, aux, piece):
    shape = (CAP, low.shape[1])
    inside = pl.BlockSpec(memory_space=pltpu.VMEM)
    return pl.pallas_call(
        functools.partial(share_kernel, piece=piece),
        in_specs=[pl.BlockSpec(memory_space=pltpu.SMEM), inside, inside],
        out_specs=[pl.BlockSpec(memory_space=pltpu.HBM)] * GROUPS,
        out_shape=[sds(shape, bf)] * GROUPS,
        scratch_shapes=[pltpu.VMEM((GROUPS,) + shape, bf), pltpu.SemaphoreType.DMA((GROUPS,))],
        compiler_params=pltpu.CompilerParams(vmem_limit_bytes=11 * 1024 * 1024),
        cost_estimate=pl.CostEstimate(flops=1000, bytes_accessed=1000, transcendentals=0),
        name="share",
    )(scalar, low, aux)


def collect_kernel(scalar_ref, aux_ref, *refs, rows):
    *shares, out_ref = refs
    (ids,) = read_slots(aux_ref, 1, out_ref.shape[0])
    ranks = ranked([ids] * GROUPS, [scalar_ref[GROUPS + i] for i in range(GROUPS)], rows)
    out_ref[...] = sum(dg(rank, ref[...], NN) for rank, ref in zip(ranks, shares)).astype(bf)


def collect(scalar, aux, shares, rows, piece):
    shape = (piece, shares[0].shape[1])
    return call(
        functools.partial(collect_kernel, rows=rows), "collect", scalar, [aux, *shares], [sds(shape, bf)]
    )[0]


def unpack_feed_kernel(scalar_ref, *refs):
    *sources, down_ref, up_ref, out_ref = refs
    mine, other = sources[:GROUPS], sources[GROUPS:]
    first = scalar_ref[GROUPS + 4] == 0
    lines = down_ref.shape[0] // GROUPS
    half = out_ref.shape[0] // 2
    extra = half // SPREAD

    def unpack(g):
        z_low, z_high = scalar_ref[GROUPS + 12 + g], scalar_ref[GROUPS + 8 + g]
        for k, far in enumerate(OPPOSITE):
            low = jnp.where(first, mine[k][g], other[k][g]).astype(f32)
            high = jnp.where(first, other[g][k], mine[g][k]).astype(f32)
            y_low, y_high = turn(scalar_ref[GROUPS + 6], far), turn(scalar_ref[GROUPS + 12], far)
            down_ref[pl.ds(pl.multiple_of(lines * y_low, 16), lines), :] = low[:lines]
            up_ref[pl.ds(pl.multiple_of(lines * y_high, 16), lines), :] = high[:lines]
            at = extra * (GROUPS * z_low + y_low)
            out_ref[pl.ds(pl.multiple_of(at, 16), extra), :] = low[lines:]
            at = half + extra * (GROUPS * z_high + y_high)
            out_ref[pl.ds(pl.multiple_of(at, 16), extra), :] = high[lines:]

    for g in range(GROUPS):
        pl.when(pl.program_id(0) == g)(functools.partial(unpack, g))


def unpack_feed(scalar, mine, other, width, hidden):
    block = pl.BlockSpec(mine[0].shape, lambda g, s: (0, 0, 0))
    return grid_call(
        unpack_feed_kernel,
        "unpack_feed",
        scalar,
        GROUPS,
        [block] * (2 * GROUPS),
        [
            pl.BlockSpec((width, width), lambda g, s: (s[GROUPS + 12 + g], 0)),
            pl.BlockSpec((width, width), lambda g, s: (0, s[GROUPS + 8 + g])),
            pl.BlockSpec((width, width), lambda g, s: (0, 0)),
        ],
        [sds((hidden, width), f32), sds((width, hidden), f32), sds((width, width), f32)],
        [*mine, *other],
    )


def unpack_rest_kernel(scalar_ref, mine_ref, other_ref, out_ref, pos_ref, *vec_refs):
    core = scalar_ref[GROUPS + 4]
    half = out_ref.shape[0] // 2
    width = out_ref.shape[1] // 3
    rows = pos_ref.shape[0] // 2
    chunk = mine_ref.shape[0] // GROUPS
    for kept, ref in ((core, mine_ref), (1 - core, other_ref)):
        lines = pl.ds(pl.multiple_of(kept * half, half), half)
        for j in range(GROUPS):
            for w in range(3):
                lanes = slice(w * width + 128 * j, w * width + 128 * (j + 1))
                block = ref[chunk * j : chunk * (j + 1), :, 128 * w : 128 * (w + 1)]
                out_ref[lines, lanes] = block.reshape(half, 128).astype(f32)
        tail = ref[:, :, 3 * 128 :].astype(f32).reshape(-1, 128)
        lines = pl.ds(pl.multiple_of(kept * rows, 8), rows)
        blocks = width // 128
        for i in range(blocks):
            pos_ref[lines, 128 * i : 128 * (i + 1)] = tail[rows * i : rows * (i + 1)]
            if ref is mine_ref:
                base = rows * blocks + 16 * i
                for n, vec_ref in enumerate(vec_refs):
                    for line in range(vec_ref.shape[1] // width):
                        lanes = slice(width * line + 128 * i, width * line + 128 * (i + 1))
                        vec_ref[:, lanes] = tail[base + n + line : base + n + line + 1]


def unpack_rest(scalar, mine, other, rows, width, hidden):
    return call(
        unpack_rest_kernel,
        "unpack_rest",
        scalar,
        [mine, other],
        [sds((width, 3 * width), f32), sds((rows, width), f32)]
        + [sds((1, width), f32)] * 9
        + [sds((1, hidden), f32)],
    )


def shift(array, axis, step):
    size = lax.axis_size(axis)
    return lax.ppermute(array, axis, [(i, (i + step) % size) for i in range(size)])


def peers(array, axis):
    return [shift(array, axis, step) for step in (1, 3, 2)]


def swap(array):
    return shift(array, "core", 1)


def total(parts):
    return functools.reduce(jnp.add, [p.astype(f32) for p in parts])


SPACE = ("x", "z", "y")
PLANE = ("z", "y", "core")


def step_plane(array, step, near):
    sizes = [lax.axis_size(name) for name in PLANE]
    pairs = []
    for z in range(sizes[0]):
        for y in range(sizes[1]):
            for core in range(sizes[2]):
                if (core == 0) == near:
                    target = (z, (y + step) % sizes[1], core)
                else:
                    target = ((z + step) % sizes[0], y, core)
                index = lambda p: (p[0] * sizes[1] + p[1]) * sizes[2] + p[2]
                pairs.append((index((z, y, core)), index(target)))
    return lax.ppermute(array, PLANE, pairs)


def step_cores(array):
    size = lax.axis_size("x")
    pairs = []
    for core in range(2):
        for x in range(size):
            pairs.append((core * size + x, core * size + (x + 1 - 2 * core) % size))
    return lax.ppermute(array, ("core", "x"), pairs)


def plane_peers(array, near):
    return [step_plane(array, step, near) for step in (2, 1, 3)]


def exchange(array, axes):
    return lax.all_to_all(array, axes, 0, 0, tiled=True)


def body(
    vis,
    keep_slots,
    counts,
    band_mask,
    mask_token,
    pos,
    ln1_gain,
    ln1_bias,
    w_qkv,
    b_query,
    b_value,
    w_out,
    b_out,
    ln2_gain,
    ln2_bias,
    w_up,
    b_up,
    w_down,
    b_down,
    d_out,
):
    barrier = lax.optimization_barrier
    x = lax.axis_index("x")
    core = lax.axis_index("core")
    piece = keep_slots.shape[1]
    rows, width = pos.shape
    half = rows // 2
    hidden = w_up.shape[1]

    vis = vis[0]

    y, z = lax.axis_index("y"), lax.axis_index("z")
    relative, far = jnp.array(RELATIVE, jnp.int32), jnp.array(OPPOSITE, jnp.int32)
    order = (x + relative) % GROUPS
    live = jnp.sum(jnp.where(order[:, None] == jnp.arange(GROUPS)[None, :], band_mask, 0), axis=1)
    here = (x * lax.axis_size("z") + z) * lax.axis_size("y") + y
    chunks = width // 128 * half // 16
    shared = (here >= chunks) & (here < chunks + width // 128)
    scalar = jnp.concatenate(
        [live, order * rows, jnp.stack([core, shared.astype(jnp.int32), y, z]), (z + far) % GROUPS, (x + far) % GROUPS]
    ).astype(jnp.int32)
    pack = lambda *vs: jnp.pad(jnp.stack(vs), ((0, 8 - len(vs)), (0, 0)))
    vectors = pack(mask_token, ln1_gain, ln1_bias, b_query, b_value)
    feed_vectors = pack(b_out, ln2_gain, ln2_bias, b_down)

    index = lax.broadcasted_iota(jnp.int32, (1, piece), 1)
    code = jnp.where(index < counts, keep_slots, -1) + 1
    marks = jnp.concatenate([code // 64, code % 64], axis=0).astype(bf)
    marks = jnp.pad(marks, ((0, MARKS - 2), (0, width - piece)))
    message = jnp.concatenate([marks, vis], axis=0)
    pieces = [message] + [shift(message, "x", step) for step in (2, 1, 3)]
    pos_half = lax.dynamic_slice(pos, (half * core, 0), (half, width))
    pos_mine = [step_cores(pos), shift(pos_half, "x", 2)]
    scalar, vectors, feed_vectors, pieces = barrier((scalar, vectors, feed_vectors, pieces))
    aux, *bases = front(scalar, pieces, vectors, rows)
    start, q, turned_own, k_own, v_own, *state, p_own = attention_own(scalar, bases[0], pos, vectors, w_qkv)
    state, pos_mine = barrier((state, pos_mine))
    pos_other = [swap(p) for p in pos_mine]
    out = middle(scalar, bases[1:], pos_mine + pos_other, vectors, w_qkv, q, state)
    rest, (mixed, lse), kept = out[: 3 * (GROUPS - 1)], out[3 * (GROUPS - 1) :][:2], out[3 * (GROUPS - 1) + 2 :]
    keys, values = [k_own, *rest[1::3]], [v_own, *rest[2::3]]
    weights, peaks = [p_own, *kept[0::2]], [state[0], *kept[1::2]]

    out, middle_rows, second, kept, sent, grad_b_up = feed_forward(
        scalar, mixed, start, d_out[0], w_out, feed_vectors, w_up, b_up[None], w_down
    )
    got = swap(sent)
    grad_middle, grad_mixed, out_kept, out_sent, feed_vec = feed_backward(
        scalar, mixed, middle_rows, second, d_out[0], w_out, feed_vectors
    )
    factors = softmax_factors(scalar, mixed, grad_mixed, lse, peaks)
    inputs = list(zip(factors[:GROUPS], weights, keys, values, factors[GROUPS:]))
    feed = fold_feed(scalar, kept, got, out_kept, swap(out_sent))
    inputs, feed = barrier((inputs, feed))
    feed = [feed[0]] + [step_plane(feed[r], r, True) for r in (1, 2, 3)]
    dq, d_3, part = attention_grad(scalar, (3,), q, w_qkv, [inputs[3]], None)
    dq, part = barrier((dq, part))
    from_3 = shift(part, "x", 2)
    dq, d_1, part = attention_grad(scalar, (1,), q, w_qkv, [inputs[1]], dq)
    feed = fold_line(scalar, feed)
    dq, part, feed = barrier((dq, part, feed))
    feed = [feed[0]] + [shift(feed[r], "x", r) for r in (2, 1, 3)]
    from_1 = shift(part, "x", 3)
    dq, d_2, part = attention_grad(scalar, (2,), q, w_qkv, [inputs[2]], dq)
    feed = add_up(scalar, "fold_point", feed)
    dq, part, from_3, feed = barrier((dq, part, from_3, feed))
    feed_peers = [step_plane(feed, step, False) for step in (1, 3, 2)]
    from_2 = shift(part, "x", 1)
    part, at_kept, at_sent, grad_b_query, grad_b_value = attention_grad(
        scalar, (0,), q, w_qkv, [inputs[0]], dq, [turned_own, *rest[0::3], d_3, d_1, d_2]
    )
    at_kept, at_sent, part, from_1, from_2, feed_peers = barrier(
        (at_kept, at_sent, part, from_1, from_2, feed_peers)
    )

    at_got = swap(at_sent)
    feed = add_up(scalar, "sum_line", [feed] + feed_peers)
    gathered = [shift(feed, "x", step) for step in (2, 1, 3)]
    tail_kept, tail_sent, low = finish(
        scalar,
        part,
        (from_3, from_1, from_2),
        start,
        grad_middle,
        vectors,
        aux,
        grad_b_query,
        grad_b_value,
        feed_vec,
        grad_b_up,
    )
    spread = lambda a: a.reshape(GROUPS * SPREAD, 16, -1)
    bundle = fold_rest(scalar, spread(at_kept), spread(at_got), tail_kept, swap(tail_sent))
    bundle, feed = barrier((bundle, jnp.stack([feed] + gathered)))
    bundle = exchange(bundle, SPACE)
    feed_other = [swap(feed)]
    feed = [feed] + plane_peers(feed, True)
    bundle, shares, feed_other = barrier((bundle, share(scalar, low, aux, piece), feed_other))
    bundle = sum_space(scalar, bundle)
    feed, _ = barrier((feed, bundle))
    rest_mine = exchange(bundle, SPACE)
    feed_other += [swap(a) for a in feed[1:]]
    shares = list(shares)
    feed_other[1], shares[1] = barrier((feed_other[1], shares[1]))
    returned = [shares[0], shift(shares[3], "x", 1), shift(shares[2], "x", 3), shift(shares[1], "x", 2)]
    grad_w_down, grad_w_up, grad_w_out = unpack_feed(scalar, feed, feed_other, width, hidden)
    grad_vis = collect(scalar, aux, returned, rows, piece)
    rest_mine, grad_w_down, grad_vis = barrier((rest_mine, grad_w_down, grad_vis))
    rest_other = swap(rest_mine)
    grad_w_qkv, grad_pos, *sums = unpack_rest(scalar, rest_mine, rest_other, rows, width, hidden)
    sums = [a[0] for a in sums]

    return (
        out[None],
        grad_vis[None],
        sums[0],
        grad_pos,
        sums[1],
        sums[2],
        grad_w_qkv,
        sums[3],
        sums[4],
        grad_w_out,
        sums[5],
        sums[6],
        sums[7],
        grad_w_up,
        sums[9],
        grad_w_down,
        sums[8],
    )


CUBE = ("z", "y", "core")


def solution(mesh):
    fine = Mesh(mesh.devices.reshape(4, 4, 2, 4), ("z", "y", "core", "x"))
    return jax.shard_map(
        body,
        mesh=fine,
        in_specs=(
            P(CUBE, "x", None),
            P(CUBE, "x"),
            P(CUBE, "x"),
            P(CUBE, None),
            P(),
            P("x", None),
        )
        + (P(),) * 13
        + (P(CUBE, "x", None),),
        out_specs=(P(CUBE, "x", None), P(CUBE, "x", None), P(), P("x", None)) + (P(),) * 13,
        check_vma=False,
    )
```
